32 devices in a mesh: view: 16 (over z, x, core), joint: 2 (over y).
Axes of the slice: x: 2, y: 2, z: 4, core: 2. Of those that a mesh axis runs over, the one named last changes fastest.
Arguments:
- pose_tokens: bfloat16 [128, 2, 133, 1024], P('view', None, None, 'joint')
- gain_attn: float32 [1024], replicated, may hold values from 0.1 to 1.9
- gain_graph: float32 [1024], replicated, may hold values from 0.1 to 1.9
- w_query: bfloat16 [1024, 1024], P(None, 'joint')
- w_key: bfloat16 [1024, 1024], P(None, 'joint')
- w_value: bfloat16 [1024, 1024], P(None, 'joint'), may hold values from -0.1875 to 0.1875
- w_out: bfloat16 [1024, 1024], P('joint'), may hold values from -0.375 to 0.375
- w_graph: bfloat16 [1024, 1024], replicated, may hold values from -0.1875 to 0.1875
- partners: int32 [128, 4], P('view'), may hold values from 0 to 127, as said below
- parents: int32 [133], replicated, may hold values from 0 to 131, as said below
- view_links: int32 [128, 8], replicated, may hold values from 0 to 127
Outputs:
- graph_out: bfloat16 [2, 1024, 133, 128], P('joint', 'view')
The draws below stay inside these ranges and needn't reach their ends.
Inputs may be any that keep to these rules, and one draw needn't show every extreme that they name: partners[v] holds four distinct views: two among v - 8, ..., v - 1 and two among v + 1, ..., v + 8, taken modulo 128; some view has a partner 8 views before it, and some view has a partner 8 views after it. parents[0] = 0 and parents[j] < j for every other joint j: a tree rooted at joint 0.
All inputs are finite; a program needn't handle non-finite values.
Results may differ from the reference program's by a relative error of at most 0.011.
The reference program's roundings to bfloat16 on the way count: a program that leaves them out, or rounds other values in their place, can miss the bound.
Values may be sent and summed in bfloat16 or wider, within the bound.
No kernel may reach another device: no remote copies, remote signals or barrier semaphores. Data moves between devices by JAX's collectives and lax.ppermute only.
A program may use at most 192 MiB of HBM per device.

```python
import math
import jax
import jax.numpy as jnp
from jax import lax

D = 1024
H = 16
HD = 64
J = 133
FR = 2
VIEW_DEV = 8
KV = 8
VIEWS = 128


def draw_pose_tokens(key, part):
    sample = jax.random.normal(jax.random.fold_in(key, 11), (VIEWS, FR, J, D), jnp.float32)
    return jnp.clip(sample, -6.0, 6.0).astype(jnp.bfloat16)


def shared_projection(key, own_tag):
    private = jax.random.normal(jax.random.fold_in(key, own_tag), (D, D), jnp.float32)
    mixed_draw = private
    return mixed_draw * (2.0 / math.sqrt(D))


def draw_w_query(key, part):
    return shared_projection(key, 1).astype(jnp.bfloat16)


def draw_w_key(key, part):
    return shared_projection(key, 2).astype(jnp.bfloat16)


def offset_pair(key):
    step_one = jax.random.randint(jax.random.fold_in(key, 1), (VIEWS,), 1, VIEW_DEV + 1)
    step_two = jax.random.randint(jax.random.fold_in(key, 2), (VIEWS,), 1, VIEW_DEV)
    return (step_one, step_two)


def draw_partners(key, part):
    view_ids = jnp.arange(VIEWS, dtype=jnp.int32)
    back_one, back_two = offset_pair(jax.random.fold_in(key, 31))
    ahead_one, ahead_two = offset_pair(jax.random.fold_in(key, 32))
    back_one = jnp.where(view_ids == 0, 1, jnp.where(view_ids == 1, VIEW_DEV, back_one))
    ahead_one = jnp.where(view_ids == VIEWS - 1, 1, jnp.where(view_ids == VIEWS - 2, VIEW_DEV, ahead_one))
    back_two = back_two + (back_two >= back_one).astype(jnp.int32)
    ahead_two = ahead_two + (ahead_two >= ahead_one).astype(jnp.int32)
    stacked = jnp.stack((view_ids - back_one, view_ids - back_two, view_ids + ahead_one, view_ids + ahead_two), axis=1)
    return jnp.mod(stacked, VIEWS).astype(jnp.int32)


def draw_parents(key, part):
    joint_ids = jnp.arange(J, dtype=jnp.int32)
    drawn = jax.random.randint(jax.random.fold_in(key, 41), (J,), 0, jnp.maximum(joint_ids, 1))
    return jnp.where(joint_ids == 0, 0, drawn).astype(jnp.int32)


def place_ends(values, own_key, smallest, high):
    index_at = [jax.random.randint(jax.random.fold_in(own_key, axis), (), 0, length) for axis, length in enumerate(values.shape)]
    longest = values.shape.index(max(values.shape))
    neighbour = index_at[:longest] + [(index_at[longest] + 1) % values.shape[longest]] + index_at[longest + 1:]
    return values.at[tuple(index_at)].set(smallest).at[tuple(neighbour)].set(high)


def level_of(stream_key, dims, shards, smallest, top_value):
    def one(position, blocks):
        steps = jax.random.uniform(jax.random.fold_in(jax.random.fold_in(stream_key, 6), position), (blocks,), jnp.float32, smallest / len(shards), top_value / len(shards))
        return jnp.repeat(jnp.exp(steps), dims[position] // blocks).reshape((-1,) + (1,) * (len(dims) - position - 1))

    level = one(*shards[0])
    for cut in shards[1:]:
        level = level * one(*cut)
    return level


def normal_values(key, shape, width, limit, shards=(), held_as=jnp.bfloat16):
    level = level_of(key, shape, shards, -0.22, 0.18) if shards else 1.0
    entries = jax.random.normal(key, shape, jnp.float32) * width * level
    return jnp.minimum(jnp.maximum(entries, -limit), limit).astype(held_as)


def setup_inputs(seed: int = 0) -> dict:
    key_of = jax.random.split(jax.random.key(seed), 12)
    pose_tokens = draw_pose_tokens(jax.random.fold_in(key_of[11], 71), 0)
    gain_attn = jnp.clip(1.0 + 0.18 * jax.random.normal(key_of[1], (D,), jnp.float32), 0.1, 1.9)
    gain_graph = jnp.clip(1.0 + 0.18 * jax.random.normal(key_of[2], (D,), jnp.float32), 0.1, 1.9)
    w_query = draw_w_query(jax.random.fold_in(key_of[11], 71), 0)
    w_key = draw_w_key(jax.random.fold_in(key_of[11], 71), 0)
    w_value = normal_values(key_of[5], (D, D), D ** -0.5, 0.1875, ((1, 2),))
    w_out = normal_values(key_of[6], (D, D), (D // 4) ** -0.5, 0.375, ((0, 2),))
    w_graph = normal_values(key_of[7], (D, D), D ** -0.5, 0.1875)
    partners = draw_partners(jax.random.fold_in(key_of[11], 71), 0)
    parents = draw_parents(jax.random.fold_in(key_of[11], 71), 0)
    view_links = place_ends(jax.random.randint(key_of[10], (VIEWS, KV), 0, VIEWS), jax.random.fold_in(key_of[10], 1), 0, VIEWS - 1).astype(jnp.int32)
    return dict(pose_tokens=pose_tokens, gain_attn=gain_attn, gain_graph=gain_graph, w_query=w_query, w_key=w_key, w_value=w_value, w_out=w_out, w_graph=w_graph, partners=partners, parents=parents, view_links=view_links)


norm_eps = 1e-05

def layer_norm(values, gain):
    floats = values.astype(jnp.float32)
    average = lax.optimization_barrier(jnp.mean(floats, axis=-1, keepdims=True))
    centred = floats - average
    spread = lax.optimization_barrier(jnp.mean(centred * centred, axis=-1, keepdims=True))
    return centred * lax.rsqrt(spread + norm_eps) * gain

def reference(pose_tokens, gain_attn, gain_graph, w_query, w_key, w_value, w_out, w_graph, partners, parents, view_links):
    tokens_view = FR * J
    score_scale = HD ** (-0.5)
    normed = layer_norm(pose_tokens, gain_attn).astype(jnp.bfloat16).reshape(VIEWS * tokens_view, D)
    query = jnp.dot(normed, w_query, preferred_element_type=jnp.float32).astype(jnp.bfloat16)
    keys = jnp.dot(normed, w_key, preferred_element_type=jnp.float32).astype(jnp.bfloat16)
    values = jnp.dot(normed, w_value, preferred_element_type=jnp.float32).astype(jnp.bfloat16)
    query = lax.optimization_barrier(query).reshape(VIEWS, tokens_view, H, HD)
    keys = lax.optimization_barrier(keys).reshape(VIEWS, tokens_view, H, HD)
    values = lax.optimization_barrier(values).reshape(VIEWS, tokens_view, H, HD)

    def attend(view_index):
        chosen = jnp.concatenate((view_index[None], partners[view_index])).astype(jnp.int32)
        key_set = jnp.take(keys, chosen, axis=0).reshape(-1, H, HD).astype(jnp.float32)
        value_set = jnp.take(values, chosen, axis=0).reshape(-1, H, HD).astype(jnp.float32)
        queries = query[view_index].astype(jnp.float32)
        scores = jnp.einsum('qhd,khd->hqk', queries, key_set) * score_scale
        weights = jax.nn.softmax(scores, axis=-1).astype(jnp.bfloat16)
        weights = lax.optimization_barrier(weights).astype(jnp.float32)
        return jnp.einsum('hqk,khd->qhd', weights, value_set).astype(jnp.bfloat16)
    attended = lax.map(attend, jnp.arange(VIEWS, dtype=jnp.int32))
    projected = jnp.dot(attended.reshape(-1, D), w_out, preferred_element_type=jnp.float32)
    hidden = (pose_tokens.reshape(-1, D).astype(jnp.float32) + projected).astype(jnp.bfloat16)
    hidden = hidden.reshape(VIEWS, FR, J, D)
    normed_mid = layer_norm(hidden, gain_graph).astype(jnp.bfloat16)
    normed_mid = lax.optimization_barrier(normed_mid)
    joint_ids = jnp.arange(J, dtype=jnp.int32)
    skeleton = (joint_ids[:, None] == joint_ids[None, :]).astype(jnp.float32) + (joint_ids[None, :] == parents[:, None]).astype(jnp.float32) + (joint_ids[:, None] == parents[None, :]).astype(jnp.float32)
    degree = lax.optimization_barrier(jnp.sum(skeleton, axis=1))
    summed = jnp.einsum('jk,vfkc->vfjc', skeleton, normed_mid.astype(jnp.float32))
    skeletal = (summed / degree[None, None, :, None]).astype(jnp.bfloat16)
    graph_term = jnp.dot(skeletal.reshape(-1, D), w_graph, preferred_element_type=jnp.float32).astype(jnp.bfloat16)
    graph_term = lax.optimization_barrier(graph_term).reshape(VIEWS, FR, J, D)
    view_ids = jnp.arange(VIEWS, dtype=jnp.int32)
    counts = (view_ids[:, None] == view_ids[None, :]).astype(jnp.float32)
    counts = counts + lax.optimization_barrier(jnp.sum((view_links[:, :, None] == view_ids[None, None, :]).astype(jnp.float32), axis=1))
    mixed_term = jnp.einsum('wv,vfjc->fcjw', counts, graph_term.astype(jnp.float32)) * (1.0 / (KV + 1))
    residual = jnp.transpose(hidden, (1, 3, 2, 0)).astype(jnp.float32)
    return (residual + mixed_term).astype(jnp.bfloat16)
```

```python
import functools

import jax
import jax.numpy as jnp
from jax import lax
from jax.experimental import pallas as pl
from jax.experimental.pallas import tpu as pltpu
from jax.sharding import PartitionSpec as P

HD = 64
LANES = 128
norm_eps = 1e-05
MIB = 1024 * 1024
F32 = jnp.float32
BF16 = jnp.bfloat16
LOG2E = 1.4426950408889634


def round_up(value, unit):
    return (value + unit - 1) // unit * unit


def layer_norm(values, gain):
    average = jnp.mean(values, axis=-1, keepdims=True)
    centred = values - average
    spread = jnp.mean(centred * centred, axis=-1, keepdims=True)
    return centred * lax.rsqrt(spread + norm_eps) * gain


def pad_rows(values, rows, fill):
    missing = rows - values.shape[0]
    if not missing:
        return values
    return jnp.concatenate([values, jnp.broadcast_to(fill, (missing, values.shape[1]))], axis=0)


def both_halves(joint, own, other):
    low = jnp.where(joint == 0, own, other)
    high = jnp.where(joint == 0, other, own)
    return jnp.concatenate([low, high], axis=1)


def params(limit_mib):
    return pltpu.CompilerParams(vmem_limit_bytes=limit_mib * MIB)


def cost(flops, bytes_accessed, transcendentals=0):
    return pl.CostEstimate(
        flops=int(flops), bytes_accessed=int(bytes_accessed), transcendentals=int(transcendentals)
    )


def project_kernel(joint_ref, own_ref, other_ref, gain_ref, wq_ref, wk_ref, wv_ref, q_ref, kv_ref):
    views, frames, joints, _ = own_ref.shape
    width = wq_ref.shape[1]
    padded = q_ref.shape[1] // frames
    joint = joint_ref[0]
    gain = gain_ref[...]
    pieces = []
    for view in range(views):
        for frame in range(frames):
            whole = both_halves(
                joint, own_ref[view, frame].astype(F32), other_ref[view, frame].astype(F32)
            )
            normed = layer_norm(whole, gain)
            pieces.append(pad_rows(normed, padded, normed[0:1]))
    tokens = jnp.concatenate(pieces, axis=0).astype(BF16)
    rows = frames * padded
    row = lax.broadcasted_iota(jnp.int32, (tokens.shape[0], 1), 0)
    real = lax.rem(row, padded) < joints
    query = jnp.dot(tokens, wq_ref[...], preferred_element_type=F32).astype(BF16)
    keys = jnp.dot(tokens, wk_ref[...], preferred_element_type=F32).astype(BF16)
    values = jnp.dot(tokens, wv_ref[...], preferred_element_type=F32)
    values = jnp.where(real, values, 0.0).astype(BF16)
    for view in range(views):
        part = slice(view * rows, (view + 1) * rows)
        q_ref[view] = query[part]
        kv_ref[view, :, :width] = keys[part]
        kv_ref[view, :, width:] = values[part]


def project(joint, own, other, gain, w_query, w_key, w_value, padded):
    views, frames, joints, half = own.shape
    model, width = w_query.shape
    rows = frames * padded
    step = 2 if views % 2 == 0 else 1
    tokens = pl.BlockSpec((step, frames, joints, half), lambda i, s: (i, 0, 0, 0))
    weight = pl.BlockSpec((model, width), lambda i, s: (0, 0))
    return pl.pallas_call(
        project_kernel,
        grid_spec=pltpu.PrefetchScalarGridSpec(
            num_scalar_prefetch=1,
            grid=(views // step,),
            in_specs=[
                tokens,
                tokens,
                pl.BlockSpec((1, model), lambda i, s: (0, 0)),
                weight,
                weight,
                weight,
            ],
            out_specs=[
                pl.BlockSpec((step, rows, width), lambda i, s: (i, 0, 0)),
                pl.BlockSpec((step, rows, 2 * width), lambda i, s: (i, 0, 0)),
            ],
        ),
        out_shape=[
            jax.ShapeDtypeStruct((views, rows, width), BF16),
            jax.ShapeDtypeStruct((views, rows, 2 * width), BF16),
        ],
        compiler_params=params(48),
        cost_estimate=cost(
            2 * views * rows * model * 3 * width, 2 * (views * rows * (model + 3 * width))
        ),
        name="project",
    )(joint, own, other, gain, w_query, w_key, w_value)


def attend_kernel(chunk, joint_ref, slot_ref, q_ref, ones_ref, *rest):
    sources = rest[:-4]
    mine_ref, theirs_ref, keyval, sems = rest[-4:]
    _, rows, width = q_ref.shape
    blocks = slot_ref.shape[1]
    step = pl.program_id(0)
    steps = pl.num_programs(0)
    joint = joint_ref[0]

    def fetch(view, buffer):
        for block in range(blocks):
            slot = slot_ref[view, block]
            owner = slot // chunk
            for index, source in enumerate(sources):

                @pl.when(owner == index)
                def _():
                    pltpu.make_async_copy(
                        source.at[slot - index * chunk],
                        keyval.at[buffer, pl.ds(block * rows, rows)],
                        sems.at[buffer, block],
                    ).start()

    buffer = lax.rem(step, 2)

    @pl.when(step == 0)
    def _():
        fetch(0, 0)

    @pl.when(step + 1 < steps)
    def _():
        fetch(step + 1, 1 - buffer)

    for block in range(blocks):
        pltpu.make_async_copy(
            sources[0].at[0], keyval.at[buffer, pl.ds(block * rows, rows)], sems.at[buffer, block]
        ).wait()

    lane = lax.broadcasted_iota(jnp.int32, (1, LANES), 1)
    ones = ones_ref[...]
    scale = HD**-0.5 * LOG2E
    half = rows // 2
    for pair in range(width // LANES):
        columns = slice(pair * LANES, (pair + 1) * LANES)
        query = q_ref[0, :, columns]
        keys = keyval[buffer, :, columns]
        values = jnp.concatenate(
            [keyval[buffer, :, width + pair * LANES : width + (pair + 1) * LANES], ones], axis=1
        )
        found = []
        for head in range(LANES // HD):
            mask = (lane // HD) == head
            scores = lax.dot_general(
                jnp.where(mask, query, jnp.zeros_like(query)),
                keys,
                (((1,), (1,)), ((), ())),
                preferred_element_type=F32,
            )
            top = jnp.max(scores, axis=1, keepdims=True)
            powers = jnp.exp2((scores - top) * scale).astype(BF16)
            found.append(jnp.dot(powers, values, preferred_element_type=F32))
        first = lane < HD
        total = jnp.where(first, found[0][:, :LANES], found[1][:, :LANES])
        weight = jnp.where(first, found[0][:, LANES:], found[1][:, LANES:])
        attended = total / weight
        early, late = attended[:half], attended[half:]
        mine_ref[0, :, columns] = jnp.where(joint == 0, early, late).astype(BF16)
        theirs_ref[0, :, columns] = jnp.where(joint == 0, late, early).astype(BF16)


def attend(joint, slots, query, ones, sources):
    views, rows, width = query.shape
    blocks = slots.shape[1]
    chunk = sources[0].shape[0]
    half = rows // 2
    out = jax.ShapeDtypeStruct((views, half, width), BF16)
    out_spec = pl.BlockSpec((1, half, width), lambda i, j, s: (i, 0, 0))
    heads = width // HD
    return pl.pallas_call(
        functools.partial(attend_kernel, chunk),
        grid_spec=pltpu.PrefetchScalarGridSpec(
            num_scalar_prefetch=2,
            grid=(views,),
            in_specs=[
                pl.BlockSpec((1, rows, width), lambda i, j, s: (i, 0, 0)),
                pl.BlockSpec(ones.shape, lambda i, j, s: (0, 0)),
            ]
            + [pl.BlockSpec(memory_space=pl.ANY)] * len(sources),
            out_specs=[out_spec, out_spec],
            scratch_shapes=[
                pltpu.VMEM((2, blocks * rows, 2 * width), BF16),
                pltpu.SemaphoreType.DMA((2, blocks)),
            ],
        ),
        out_shape=[out, out],
        compiler_params=params(56),
        cost_estimate=cost(
            2 * 2 * views * heads * rows * blocks * rows * 256,
            2 * views * rows * width * (2 + 2 * blocks),
            views * heads * rows * blocks * rows,
        ),
        name="attend",
    )(joint, slots, query, ones, *sources)


def graph_kernel(
    packed,
    joint_ref,
    mine_ref,
    theirs_ref,
    own_ref,
    other_ref,
    w_mine_ref,
    w_theirs_ref,
    gain_ref,
    skeleton_ref,
    degree_ref,
    w_graph_ref,
    *outs,
):
    views, padded, width = mine_ref.shape
    joints = own_ref.shape[2]
    joint = joint_ref[0]
    model = w_graph_ref.shape[0]
    gain = gain_ref[...]
    mine = mine_ref[...].astype(F32).reshape(views * padded, width).astype(BF16)
    theirs = theirs_ref[...].astype(F32).reshape(views * padded, width).astype(BF16)
    projected = jnp.dot(mine, w_mine_ref[...], preferred_element_type=F32) + jnp.dot(
        theirs, w_theirs_ref[...], preferred_element_type=F32
    )
    hiddens, mixed = [], []
    for view in range(views):
        whole = both_halves(
            joint, own_ref[view, 0].astype(F32), other_ref[view, 0].astype(F32)
        )
        whole = pad_rows(whole, padded, jnp.zeros((1, model), F32))
        part = projected[view * padded : (view + 1) * padded]
        hidden = (whole + part).astype(BF16).astype(F32)
        normed = layer_norm(hidden, gain).astype(BF16)
        summed = jnp.dot(skeleton_ref[...], normed, preferred_element_type=F32)
        hiddens.append(hidden)
        mixed.append(summed / degree_ref[...])
    skeletal = jnp.concatenate(mixed, axis=0).astype(BF16)
    graph = jnp.dot(skeletal, w_graph_ref[...], preferred_element_type=F32)
    if not packed:
        for view in range(views):
            outs[0][view] = hiddens[view].astype(BF16)
            outs[1][view] = graph[view * padded : (view + 1) * padded].astype(BF16)
        return
    first = lax.broadcasted_iota(jnp.int32, (1, LANES), 1) < LANES // 2
    for view in range(views):
        for tile in range(model // LANES):
            columns = slice(tile * LANES, (tile + 1) * LANES)
            kept = hiddens[view][:, columns]
            term = graph[view * padded : (view + 1) * padded, columns]
            outs[0][2 * tile, view] = jnp.where(first, kept, term).astype(BF16)
            outs[0][2 * tile + 1, view] = jnp.where(first, term, kept).astype(BF16)


def graph_part(
    packed, joint, mine, theirs, own, other, w_mine, w_theirs, gain, skeleton, degree, w_graph
):
    views, padded, width = mine.shape
    _, _, joints, half = own.shape
    model = w_graph.shape[0]
    step = 2 if views % 2 == 0 else 1
    heads = pl.BlockSpec((step, padded, width), lambda i, j: (i, 0, 0))
    tokens = pl.BlockSpec((step, 1, joints, half), lambda i, j: (i, j[0], 0, 0))

    def held(array):
        return pl.BlockSpec(array.shape, lambda i, j: (0, 0))

    if packed:
        devices = 2 * model // LANES
        out_shape = [jax.ShapeDtypeStruct((devices, views, padded, LANES), BF16)]
        out_specs = [pl.BlockSpec((devices, step, padded, LANES), lambda i, j: (0, i, 0, 0))]
    else:
        out_shape = [jax.ShapeDtypeStruct((views, padded, model), BF16)] * 2
        out_specs = [pl.BlockSpec((step, padded, model), lambda i, j: (i, 0, 0))] * 2
    return pl.pallas_call(
        functools.partial(graph_kernel, packed),
        grid_spec=pltpu.PrefetchScalarGridSpec(
            num_scalar_prefetch=1,
            grid=(views // step,),
            in_specs=[heads, heads, tokens, tokens]
            + [held(a) for a in (w_mine, w_theirs, gain, skeleton, degree, w_graph)],
            out_specs=out_specs,
        ),
        out_shape=out_shape,
        compiler_params=params(48),
        cost_estimate=cost(
            4 * views * padded * model * model, 2 * (views * padded * model * 4 + 2 * model * model)
        ),
        name="graph_part",
    )(joint, mine, theirs, own, other, w_mine, w_theirs, gain, skeleton, degree, w_graph)


def mix_kernel(share, order_ref, *rest):
    inputs, (mixer_ref, out_ref, wide, turned) = rest[:-4], rest[-4:]
    views = sum(ref.shape[0] for ref in inputs)
    rows = inputs[0].shape[1]
    channels = out_ref.shape[0]
    at = 0
    for ref in inputs:
        count = ref.shape[0]
        wide[at * rows : (at + count) * rows] = (
            ref[...].astype(F32).reshape(count * rows, LANES)
        )
        at += count
    mixer = mixer_ref[...]
    flipped = order_ref[0] == 1
    for row in range(rows):
        block = wide[pl.ds(row, views, stride=rows), :]
        lanes_first = block.T.astype(BF16)
        both = jnp.dot(lanes_first, mixer, preferred_element_type=F32)
        low, high = both[:channels], both[channels:]
        count_low, kept_low = low[:, :views], low[:, views:]
        count_high, kept_high = high[:, :views], high[:, views:]
        total = jnp.where(flipped, count_low + kept_high, count_high + kept_low) * share
        turned[pl.ds(row, channels, stride=rows), :] = total
    out_ref[...] = turned[...].reshape(channels, rows, views).astype(BF16)


def mix(order, parts, mixer, joints, share):
    views = mixer.shape[0]
    padded = parts[0].shape[1]
    channels = LANES // 2
    rows = 16
    return pl.pallas_call(
        functools.partial(mix_kernel, share),
        grid_spec=pltpu.PrefetchScalarGridSpec(
            num_scalar_prefetch=1,
            grid=(pl.cdiv(padded, rows),),
            in_specs=[
                pl.BlockSpec((part.shape[0], rows, LANES), lambda i, s: (0, i, 0))
                for part in parts
            ]
            + [pl.BlockSpec(mixer.shape, lambda i, s: (0, 0))],
            out_specs=pl.BlockSpec((channels, rows, views), lambda i, s: (0, i, 0)),
            scratch_shapes=[
                pltpu.VMEM((views * rows, LANES), F32),
                pltpu.VMEM((channels * rows, views), F32),
            ],
        ),
        out_shape=jax.ShapeDtypeStruct((channels, joints, views), BF16),
        compiler_params=params(32),
        cost_estimate=cost(
            2 * padded * LANES * views * 2 * views, 2 * padded * views * (LANES + channels)
        ),
        name="mix",
    )(order, *parts, mixer)


def body(
    pose_tokens,
    gain_attn,
    gain_graph,
    w_query,
    w_key,
    w_value,
    w_out,
    w_graph,
    partners,
    parents,
    view_links,
):
    views_dev, frames, joints, half_width = pose_tokens.shape
    model = w_graph.shape[0]
    devices = lax.axis_size("view")
    place = lax.axis_index("view").astype(jnp.int32)
    joint_place = lax.axis_index("joint").astype(jnp.int32)
    joint = joint_place.reshape(1)
    num_views = devices * views_dev
    channels = model // devices
    padded = round_up(joints, 8)
    rows = frames * padded
    chunks = 2
    chunk = views_dev // chunks
    packed = 2 * channels == LANES and num_views == LANES
    swap = [(0, 1), (1, 0)]
    up = [(i, (i + 1) % devices) for i in range(devices)]
    down = [(j, i) for i, j in up]
    gain_attn = gain_attn.reshape(1, model)
    gain_graph = gain_graph.reshape(1, model)

    own = [lax.slice_in_dim(pose_tokens, c * chunk, (c + 1) * chunk) for c in range(chunks)]
    other = [lax.ppermute(part, "joint", swap) for part in own]
    w_theirs = lax.ppermute(w_out, "joint", swap)

    query, here = [], []
    for c in range(chunks):
        q, kv = project(joint, own[c], other[c], gain_attn, w_query, w_key, w_value, padded)
        query.append(q)
        here.append(kv)
    before = [lax.ppermute(part, "view", up) for part in here]
    after = [lax.ppermute(part, "view", down) for part in here]
    window = before + here + after

    first_view = place * views_dev
    own_slot = jnp.arange(views_dev, dtype=jnp.int32)[:, None] + views_dev
    slots = jnp.concatenate(
        (own_slot, jnp.mod(partners - first_view + views_dev, num_views)), axis=1
    )
    key_rows = slots.shape[1] * rows
    ones = (jnp.arange(key_rows, dtype=jnp.int32) % padded < joints).astype(BF16)
    ones = jnp.broadcast_to(ones[:, None], (key_rows, LANES))

    joint_ids = jnp.arange(padded, dtype=jnp.int32)
    line = jnp.concatenate((parents, jnp.full((padded - joints,), -1, jnp.int32)))
    skeleton = (
        (joint_ids[:, None] == joint_ids[None, :]).astype(F32)
        + (joint_ids[None, :] == line[:, None]).astype(F32)
        + (joint_ids[:, None] == line[None, :]).astype(F32)
    )
    degree = jnp.sum(skeleton, axis=1, keepdims=True)
    skeleton = skeleton.astype(BF16)
    if packed:
        w_turned = jnp.roll(w_graph.reshape(model, model // LANES, LANES), LANES // 2, axis=2)
        w_turned = w_turned.reshape(model, model)
    else:
        w_turned = w_graph

    sent = []
    for c in range(chunks):
        reach = window[c : c + 2 * chunks + 1]
        local = jnp.clip(
            slots[c * chunk : (c + 1) * chunk] - c * chunk, 0, len(reach) * chunk - 1
        )
        mine, theirs = attend(joint, local, query[c], ones, reach)
        theirs = lax.ppermute(theirs, "joint", swap)
        sent.append(
            graph_part(
                packed,
                joint,
                mine,
                theirs,
                own[c],
                other[c],
                w_out,
                w_theirs,
                gain_graph,
                skeleton,
                degree,
                w_turned,
            )
        )

    view_ids = jnp.arange(num_views, dtype=jnp.int32)
    counts = (view_ids[:, None] == view_ids[None, :]).astype(F32)
    counts = counts + jnp.sum(
        (view_links[:, :, None] == view_ids[None, None, :]).astype(F32), axis=1
    )
    links = view_links.shape[1] + 1
    share = 1.0 / links
    if packed:
        mixer = jnp.concatenate(
            (counts.T, links * jnp.eye(num_views, dtype=F32)), axis=1
        )
        mixer = mixer.reshape(devices, chunks, chunk, 2 * num_views).transpose(1, 0, 2, 3)
        mixer = mixer.reshape(num_views, 2 * num_views).astype(BF16)
        parts = []
        for (part,) in sent:
            part = lax.all_to_all(part, "view", split_axis=0, concat_axis=0, tiled=True)
            parts.append(part.reshape(devices * chunk, padded, LANES))
        order = lax.rem(place, 2).reshape(1)
        return mix(order, parts, mixer, joints, share)[None]

    hidden = jnp.concatenate([part[0] for part in sent], axis=0)[:, :joints]
    graph_term = jnp.concatenate([part[1] for part in sent], axis=0)[:, :joints]
    residual = jnp.transpose(hidden, (2, 1, 0))
    graph_term = jnp.transpose(graph_term, (2, 1, 0))
    residual = lax.all_to_all(residual, "view", split_axis=0, concat_axis=2, tiled=True)
    graph_term = lax.all_to_all(graph_term, "view", split_axis=0, concat_axis=2, tiled=True)
    mixed = jnp.einsum(
        "cjv,wv->cjw", graph_term, counts.astype(BF16), preferred_element_type=F32
    )
    return (residual.astype(F32) + mixed * share).astype(BF16)[None]


def solution(mesh):
    placed = (
        P("view", None, None, "joint"),
        P(),
        P(),
        P(None, "joint"),
        P(None, "joint"),
        P(None, "joint"),
        P("joint", None),
        P(),
        P("view", None),
        P(),
        P(),
    )
    return jax.shard_map(
        body, mesh=mesh, in_specs=placed, out_specs=P("joint", "view", None, None), check_vma=False
    )
```

```python
import functools

import jax
import jax.numpy as jnp
from jax import lax
from jax.experimental import pallas as pl
from jax.experimental.layout import Layout, with_layout_constraint
from jax.experimental.pallas import tpu as pltpu
from jax.sharding import PartitionSpec as P

HD = 64
LANES = 128
norm_eps = 1e-05
MIB = 1024 * 1024
F32 = jnp.float32
BF16 = jnp.bfloat16
LOG2E = 1.4426950408889634


def round_up(value, unit):
    return (value + unit - 1) // unit * unit


def layer_norm(values, gain):
    average = jnp.mean(values, axis=-1, keepdims=True)
    centred = values - average
    spread = jnp.mean(centred * centred, axis=-1, keepdims=True)
    return centred * lax.rsqrt(spread + norm_eps) * gain


def both_halves(joint, own, other):
    low = jnp.where(joint == 0, own, other)
    high = jnp.where(joint == 0, other, own)
    return jnp.concatenate([low, high], axis=1)


def params(limit_mib):
    return pltpu.CompilerParams(vmem_limit_bytes=limit_mib * MIB)


def cost(flops, bytes_accessed, transcendentals=0):
    return pl.CostEstimate(
        flops=int(flops), bytes_accessed=int(bytes_accessed), transcendentals=int(transcendentals)
    )


def project_kernel(with_query, joints, place_ref, *refs):
    count = 3 if with_query else 2
    halves = 2 if with_query else 3
    tokens, rest = refs[:halves], refs[halves:]
    gain_ref, weights, outs = rest[0], rest[1 : 1 + count], rest[1 + count :]
    views, frames, padded, _ = tokens[0].shape
    joint = place_ref[0]
    gain = gain_ref[...]
    row = lax.broadcasted_iota(jnp.int32, (padded, 1), 0)
    real = row < joints
    pieces = []
    for view in range(views):
        for frame in range(frames):
            own = tokens[0][view, frame].astype(F32)
            other = tokens[1][view, frame].astype(F32)
            if not with_query:
                other = jnp.where(place_ref[1] == 0, other, tokens[2][view, frame].astype(F32))
            normed = layer_norm(both_halves(joint, own, other), gain)
            pieces.append(jnp.where(real, normed, normed[0:1]))
    flat = jnp.concatenate(pieces, axis=0).astype(BF16)
    real = jnp.concatenate([real] * (views * frames), axis=0)
    rows = frames * padded
    width = weights[-1].shape[1]
    keys = jnp.dot(flat, weights[-2][...], preferred_element_type=F32).astype(BF16)
    values = jnp.dot(flat, weights[-1][...], preferred_element_type=F32)
    values = jnp.where(real, values, 0.0).astype(BF16)
    for view in range(views):
        part = slice(view * rows, (view + 1) * rows)
        outs[-1][view, :, :width] = keys[part]
        outs[-1][view, :, width:] = values[part]
    if with_query:
        query = jnp.dot(flat, weights[0][...], preferred_element_type=F32).astype(BF16)
        for view in range(views):
            outs[0][view] = query[view * rows : (view + 1) * rows]


def project(place, tokens, gain, weights, joints):
    views, frames, padded, half = tokens[0].shape
    model, width = weights[0].shape
    rows = frames * padded
    with_query = len(weights) == 3
    out_shape = [jax.ShapeDtypeStruct((views, rows, 2 * width), BF16)]
    if with_query:
        out_shape = [jax.ShapeDtypeStruct((views, rows, width), BF16)] + out_shape

    def held(array):
        zeros = (0,) * len(array.shape)
        return pl.BlockSpec(array.shape, lambda i, s: zeros)

    operands = (*tokens, gain, *weights)
    return pl.pallas_call(
        functools.partial(project_kernel, with_query, joints),
        grid_spec=pltpu.PrefetchScalarGridSpec(
            num_scalar_prefetch=1,
            grid=(1,),
            in_specs=[held(a) for a in operands],
            out_specs=[held(a) for a in out_shape],
        ),
        out_shape=out_shape,
        compiler_params=params(40),
        cost_estimate=cost(
            2 * views * rows * model * len(weights) * width,
            2 * (views * rows * (model + len(weights) * width) + len(weights) * model * width),
        ),
        name="project",
    )(place, *operands)


def attend_kernel(chunk, first, joints, joint_ref, slot_ref, q_ref, *rest):
    sources = rest[:-5]
    mine_ref, theirs_ref, keyval, ones_ref, sems = rest[-5:]
    _, rows, width = q_ref.shape
    blocks = slot_ref.shape[1]
    step = pl.program_id(0)
    steps = pl.num_programs(0)
    joint = joint_ref[0]

    def fetch(view, buffer):
        for block in range(blocks):
            slot = slot_ref[first + view, block]
            owner = slot // chunk
            for index, source in enumerate(sources):

                @pl.when(owner == index)
                def _():
                    pltpu.make_async_copy(
                        source.at[slot - index * chunk],
                        keyval.at[buffer, pl.ds(block * rows, rows)],
                        sems.at[buffer, block],
                    ).start()

    buffer = lax.rem(step, 2)

    @pl.when(step == 0)
    def _():
        fetch(0, 0)
        row = lax.broadcasted_iota(jnp.int32, ones_ref.shape, 0)
        real = lax.rem(row, rows // 2) < joints
        ones_ref[...] = jnp.where(real, 1.0, 0.0).astype(BF16)

    @pl.when(step + 1 < steps)
    def _():
        fetch(step + 1, 1 - buffer)

    for block in range(blocks):
        pltpu.make_async_copy(
            sources[0].at[0], keyval.at[buffer, pl.ds(block * rows, rows)], sems.at[buffer, block]
        ).wait()

    lane = lax.broadcasted_iota(jnp.int32, (1, LANES), 1)
    ones = ones_ref[...]
    scale = HD**-0.5 * LOG2E
    half = rows // 2
    for pair in range(width // LANES):
        columns = slice(pair * LANES, (pair + 1) * LANES)
        query = q_ref[0, :, columns]
        keys = keyval[buffer, :, columns]
        values = jnp.concatenate(
            [keyval[buffer, :, width + pair * LANES : width + (pair + 1) * LANES], ones], axis=1
        )
        found = []
        for head in range(LANES // HD):
            mask = (lane // HD) == head
            scores = lax.dot_general(
                jnp.where(mask, query, jnp.zeros_like(query)),
                keys,
                (((1,), (1,)), ((), ())),
                preferred_element_type=F32,
            )
            top = jnp.max(scores, axis=1, keepdims=True)
            powers = jnp.exp2((scores - top) * scale).astype(BF16)
            found.append(jnp.dot(powers, values, preferred_element_type=F32))
        left = lane < HD
        total = jnp.where(left, found[0][:, :LANES], found[1][:, :LANES])
        weight = jnp.where(left, found[0][:, LANES:], found[1][:, LANES:])
        attended = total / weight
        early, late = attended[:half], attended[half:]
        mine_ref[0, :, columns] = jnp.where(joint == 0, early, late).astype(BF16)
        theirs_ref[0, :, columns] = jnp.where(joint == 0, late, early).astype(BF16)


def attend(joint, slots, first, query, sources, joints):
    views, rows, width = query.shape
    blocks = slots.shape[1]
    chunk = sources[0].shape[0]
    half = rows // 2
    out = jax.ShapeDtypeStruct((views, half, width), BF16)
    out_spec = pl.BlockSpec((1, half, width), lambda i, j, s: (i, 0, 0))
    heads = width // HD
    return pl.pallas_call(
        functools.partial(attend_kernel, chunk, first, joints),
        grid_spec=pltpu.PrefetchScalarGridSpec(
            num_scalar_prefetch=2,
            grid=(views,),
            in_specs=[pl.BlockSpec((1, rows, width), lambda i, j, s: (i, 0, 0))]
            + [pl.BlockSpec(memory_space=pl.ANY)] * len(sources),
            out_specs=[out_spec, out_spec],
            scratch_shapes=[
                pltpu.VMEM((2, blocks * rows, 2 * width), BF16),
                pltpu.VMEM((blocks * rows, LANES), BF16),
                pltpu.SemaphoreType.DMA((2, blocks)),
            ],
        ),
        out_shape=[out, out],
        compiler_params=params(56),
        cost_estimate=cost(
            2 * 2 * views * heads * rows * blocks * rows * 256,
            2 * views * rows * width * (2 + 2 * blocks),
            views * heads * rows * blocks * rows,
        ),
        name="attend",
    )(joint, slots, query, *sources)


def graph_kernel(packed, count, joint_ref, *refs):
    heads, refs = refs[: 2 * count], refs[2 * count :]
    tokens, refs = refs[: 2 * count], refs[2 * count :]
    w_mine_ref, w_theirs_ref, gain_ref, skeleton_ref, degree_ref, w_graph_ref, *outs = refs
    chunk, padded, width = heads[0].shape
    views = count * chunk
    joint = joint_ref[0]
    model = w_graph_ref.shape[0]
    gain = gain_ref[...]

    def rows_of(parts):
        pieces = [part[view].astype(F32) for part in parts for view in range(chunk)]
        return jnp.concatenate(pieces, axis=0).astype(BF16)

    mine, theirs = rows_of(heads[:count]), rows_of(heads[count:])
    projected = jnp.dot(mine, w_mine_ref[...], preferred_element_type=F32) + jnp.dot(
        theirs, w_theirs_ref[...], preferred_element_type=F32
    )
    hiddens, mixed = [], []
    for view in range(views):
        own, other = (
            tokens[side + view // chunk][view % chunk, 0].astype(F32) for side in (0, count)
        )
        part = projected[view * padded : (view + 1) * padded]
        hidden = (both_halves(joint, own, other) + part).astype(BF16).astype(F32)
        normed = layer_norm(hidden, gain).astype(BF16)
        summed = jnp.dot(skeleton_ref[...], normed, preferred_element_type=F32)
        hiddens.append(hidden)
        mixed.append(summed / degree_ref[...])
    skeletal = jnp.concatenate(mixed, axis=0).astype(BF16)
    graph = jnp.dot(skeletal, w_graph_ref[...], preferred_element_type=F32)
    first = lax.broadcasted_iota(jnp.int32, (1, LANES), 1) < LANES // 2
    for view in range(views):
        term = graph[view * padded : (view + 1) * padded]
        if not packed:
            outs[0][view] = hiddens[view].astype(BF16)
            outs[1][view] = term.astype(BF16)
            continue
        for tile in range(model // LANES):
            columns = slice(tile * LANES, (tile + 1) * LANES)
            kept = hiddens[view][:, columns]
            turned = pltpu.roll(term[:, columns], LANES // 2, axis=1)
            outs[0][2 * tile, view] = jnp.where(first, kept, turned).astype(BF16)
            outs[0][2 * tile + 1, view] = jnp.where(first, turned, kept).astype(BF16)


def graph_part(packed, joint, mine, theirs, own, other, held):
    count = len(mine)
    chunk, padded, width = mine[0].shape
    views = count * chunk
    half = own[0].shape[3]
    model = held[-1].shape[0]
    heads = pl.BlockSpec((chunk, padded, width), lambda i, j: (0, 0, 0))
    tokens = pl.BlockSpec((chunk, 1, padded, half), lambda i, j: (0, j[0], 0, 0))
    if packed:
        devices = 2 * model // LANES
        out_shape = [jax.ShapeDtypeStruct((devices, views, padded, LANES), BF16)]
        out_specs = [pl.BlockSpec((devices, views, padded, LANES), lambda i, j: (0, 0, 0, 0))]
    else:
        out_shape = [jax.ShapeDtypeStruct((views, padded, model), BF16)] * 2
        out_specs = [pl.BlockSpec((views, padded, model), lambda i, j: (0, 0, 0))] * 2
    return pl.pallas_call(
        functools.partial(graph_kernel, packed, count),
        grid_spec=pltpu.PrefetchScalarGridSpec(
            num_scalar_prefetch=1,
            grid=(1,),
            in_specs=[heads] * (2 * count)
            + [tokens] * (2 * count)
            + [pl.BlockSpec(a.shape, lambda i, j: (0, 0)) for a in held],
            out_specs=out_specs,
        ),
        out_shape=out_shape,
        compiler_params=params(48),
        cost_estimate=cost(
            4 * views * padded * model * model, 2 * (views * padded * model * 4 + 2 * model * model)
        ),
        name="graph_part",
    )(joint, *mine, *theirs, *own, *other, *held)


def mix_kernel(share, devices, order_ref, *rest):
    parts, (counts_ref, out_ref, wide) = rest[:-3], rest[-3:]
    views = wide.shape[0] // out_ref.shape[0]
    rows, channels, _ = out_ref.shape
    views_dev = views // devices
    chunk = views_dev // len(parts)
    for index, part in enumerate(parts):
        for device in range(devices):
            at = (device * views_dev + index * chunk) * rows
            block = part[device * chunk : (device + 1) * chunk].astype(F32)
            wide[at : at + chunk * rows] = block.reshape(chunk * rows, LANES)
    counts = counts_ref[...]
    flipped = order_ref[0] == 1
    for row in range(rows):
        lanes_first = wide[pl.ds(row, views, stride=rows), :].T
        low, high = lanes_first[:channels], lanes_first[channels:]
        term = jnp.where(flipped, low, high).astype(BF16)
        kept = jnp.where(flipped, high, low)
        mixed = jnp.dot(term, counts, preferred_element_type=F32)
        out_ref[row] = (kept + mixed * share).astype(BF16)


def mix(order, parts, counts, joints, share):
    views = counts.shape[0]
    devices = parts[0].shape[0]
    parts = [part.reshape(-1, *part.shape[2:]) for part in parts]
    padded = parts[0].shape[1]
    channels = LANES // 2
    rows = 16
    return pl.pallas_call(
        functools.partial(mix_kernel, share, devices),
        grid_spec=pltpu.PrefetchScalarGridSpec(
            num_scalar_prefetch=1,
            grid=(pl.cdiv(joints, rows),),
            in_specs=[
                pl.BlockSpec((part.shape[0], rows, LANES), lambda i, s: (0, i, 0))
                for part in parts
            ]
            + [pl.BlockSpec(counts.shape, lambda i, s: (0, 0))],
            out_specs=pl.BlockSpec((rows, channels, views), lambda i, s: (i, 0, 0)),
            scratch_shapes=[pltpu.VMEM((views * rows, LANES), F32)],
        ),
        out_shape=jax.ShapeDtypeStruct((joints, channels, views), BF16),
        compiler_params=params(32),
        cost_estimate=cost(
            2 * padded * LANES * views * views, 2 * padded * views * (LANES + channels)
        ),
        name="mix",
    )(order, *parts, counts)


def body(
    pose_tokens,
    gain_attn,
    gain_graph,
    w_query,
    w_key,
    w_value,
    w_out,
    w_graph,
    partners,
    parents,
    view_links,
):
    views_dev, frames, joints, half_width = pose_tokens.shape
    model = w_graph.shape[0]
    devices = lax.axis_size("view")
    place = lax.axis_index("view").astype(jnp.int32)
    joint_place = lax.axis_index("joint").astype(jnp.int32)
    joint = joint_place.reshape(1)
    num_views = devices * views_dev
    channels = model // devices
    padded = round_up(joints, 8)
    rows = frames * padded
    chunks = 4
    chunk = views_dev // chunks
    packed = 2 * channels == LANES and num_views == LANES
    swap = [(0, 1), (1, 0)]
    up = [(i, (i + 1) % devices) for i in range(devices)]
    down = [(j, i) for i, j in up]
    swap_even = [(2 * v + j, 2 * v + 1 - j) for v in range(0, devices, 2) for j in (0, 1)]
    to_odd = [(2 * v + j, 2 * v + 2 + j) for v in range(0, devices, 2) for j in (0, 1)]
    gain_attn = gain_attn.reshape(1, model)
    gain_graph = gain_graph.reshape(1, model)
    where = jnp.stack((joint_place, lax.rem(place, 2)))

    own, other = [], []
    for c in range(chunks):
        part = lax.slice_in_dim(pose_tokens, c * chunk, (c + 1) * chunk)
        part = jnp.pad(part, ((0, 0), (0, 0), (0, padded - joints), (0, 0)))
        part = with_layout_constraint(part, Layout(major_to_minor=(0, 1, 2, 3)))
        own.append(part)
        other.append(lax.ppermute(part, "joint", swap))
    query, here = [], []
    for c in range(chunks):
        q, kv = project(
            where, (own[c], other[c]), gain_attn, (w_query, w_key, w_value), joints
        )
        query.append(q)
        here.append(kv)
    after = [lax.ppermute(part, "view", down) for part in here]
    before = []
    for c in range(chunks):
        near = lax.ppermute(own[c], "view", up)
        far_even = lax.ppermute(near, ("view", "joint"), swap_even)
        far_odd = lax.ppermute(other[c], ("view", "joint"), to_odd)
        (kv,) = project(where, (near, far_even, far_odd), gain_attn, (w_key, w_value), joints)
        before.append(kv)
    window = before + here + after
    w_tied, _ = lax.optimization_barrier((w_out, before[-1]))
    w_theirs = lax.ppermute(w_tied, "joint", swap)

    first_view = place * views_dev
    own_slot = jnp.arange(views_dev, dtype=jnp.int32)[:, None] + views_dev
    slots = jnp.concatenate(
        (own_slot, jnp.mod(partners - first_view + views_dev, num_views)), axis=1
    )
    slots = jnp.clip(slots, 0, 3 * views_dev - 1)

    joint_ids = jnp.arange(padded, dtype=jnp.int32)
    line = jnp.concatenate((parents, jnp.full((padded - joints,), -1, jnp.int32)))
    skeleton = (
        (joint_ids[:, None] == joint_ids[None, :]).astype(F32)
        + (joint_ids[None, :] == line[:, None]).astype(F32)
        + (joint_ids[:, None] == line[None, :]).astype(F32)
    )
    degree = jnp.sum(skeleton, axis=1, keepdims=True)
    skeleton = skeleton.astype(BF16)
    held = (w_out, w_theirs, gain_graph, skeleton, degree, w_graph)
    joined = 2
    sent = []
    for start in range(0, chunks, joined):
        group = range(start, start + joined)
        mine, theirs = [], []
        for c in group:
            kept, moved = attend(joint, slots, c * chunk, query[c], window, joints)
            mine.append(kept)
            theirs.append(lax.ppermute(moved, "joint", swap))
        sent.append(
            graph_part(
                packed,
                joint,
                mine,
                theirs,
                [own[c] for c in group],
                [other[c] for c in group],
                held,
            )
        )

    view_ids = jnp.arange(num_views, dtype=jnp.int32)
    counts = (view_ids[:, None] == view_ids[None, :]).astype(F32)
    counts = counts + jnp.sum(
        (view_links[:, :, None] == view_ids[None, None, :]).astype(F32), axis=1
    )
    share = 1.0 / (view_links.shape[1] + 1)
    if packed:
        parts = [
            lax.all_to_all(part, "view", split_axis=0, concat_axis=0, tiled=True)
            for (part,) in sent
        ]
        order = lax.rem(place, 2).reshape(1)
        result = mix(order, parts, counts.T.astype(BF16), joints, share)
        return jnp.transpose(result, (1, 0, 2))[None]

    hidden = jnp.concatenate([part[0] for part in sent], axis=0)[:, :joints]
    graph_term = jnp.concatenate([part[1] for part in sent], axis=0)[:, :joints]
    residual = jnp.transpose(hidden, (2, 1, 0))
    graph_term = jnp.transpose(graph_term, (2, 1, 0))
    residual = lax.all_to_all(residual, "view", split_axis=0, concat_axis=2, tiled=True)
    graph_term = lax.all_to_all(graph_term, "view", split_axis=0, concat_axis=2, tiled=True)
    mixed = jnp.einsum(
        "cjv,wv->cjw", graph_term, counts.astype(BF16), preferred_element_type=F32
    )
    return (residual.astype(F32) + mixed * share).astype(BF16)[None]


def solution(mesh):
    placed = (
        P("view", None, None, "joint"),
        P(),
        P(),
        P(None, "joint"),
        P(None, "joint"),
        P(None, "joint"),
        P("joint", None),
        P(),
        P("view", None),
        P(),
        P(),
    )
    return jax.shard_map(
        body, mesh=mesh, in_specs=placed, out_specs=P("joint", "view", None, None), check_vma=False
    )
```

```python
import functools

import jax
import jax.numpy as jnp
from jax import lax
from jax.experimental import pallas as pl
from jax.experimental.layout import Layout, with_layout_constraint
from jax.experimental.pallas import tpu as pltpu
from jax.sharding import PartitionSpec as P

HD = 64
LANES = 128
norm_eps = 1e-05
MIB = 1024 * 1024
F32 = jnp.float32
BF16 = jnp.bfloat16
LOG2E = 1.4426950408889634


def round_up(value, unit):
    return (value + unit - 1) // unit * unit


def layer_norm(values, gain):
    average = jnp.mean(values, axis=-1, keepdims=True)
    centred = values - average
    spread = jnp.mean(centred * centred, axis=-1, keepdims=True)
    return centred * lax.rsqrt(spread + norm_eps) * gain


def both_halves(joint, own, other):
    low = jnp.where(joint == 0, own, other)
    high = jnp.where(joint == 0, other, own)
    return jnp.concatenate([low, high], axis=1)


def params(limit_mib):
    return pltpu.CompilerParams(vmem_limit_bytes=limit_mib * MIB)


def cost(flops, bytes_accessed, transcendentals=0):
    return pl.CostEstimate(
        flops=int(flops), bytes_accessed=int(bytes_accessed), transcendentals=int(transcendentals)
    )


def project_kernel(with_query, joints, place_ref, *refs):
    count = 3 if with_query else 2
    halves = 2 if with_query else 3
    tokens, rest = refs[:halves], refs[halves:]
    gain_ref, weights, outs = rest[0], rest[1 : 1 + count], rest[1 + count :]
    views, frames, padded, _ = tokens[0].shape
    joint = place_ref[0]
    gain = gain_ref[...]
    row = lax.broadcasted_iota(jnp.int32, (padded, 1), 0)
    real = row < joints
    pieces = []
    for view in range(views):
        for frame in range(frames):
            own = tokens[0][view, frame].astype(F32)
            other = tokens[1][view, frame].astype(F32)
            if not with_query:
                other = jnp.where(place_ref[1] == 0, other, tokens[2][view, frame].astype(F32))
            normed = layer_norm(both_halves(joint, own, other), gain)
            pieces.append(jnp.where(real, normed, normed[0:1]))
    flat = jnp.concatenate(pieces, axis=0).astype(BF16)
    real = jnp.concatenate([real] * (views * frames), axis=0)
    rows = frames * padded
    width = weights[-1].shape[1]
    keys = jnp.dot(flat, weights[-2][...], preferred_element_type=F32).astype(BF16)
    values = jnp.dot(flat, weights[-1][...], preferred_element_type=F32)
    values = jnp.where(real, values, 0.0).astype(BF16)
    for view in range(views):
        part = slice(view * rows, (view + 1) * rows)
        outs[-1][view, :, :width] = keys[part]
        outs[-1][view, :, width:] = values[part]
    if with_query:
        query = jnp.dot(flat, weights[0][...], preferred_element_type=F32).astype(BF16)
        for view in range(views):
            outs[0][view] = query[view * rows : (view + 1) * rows]


def project(place, tokens, gain, weights, joints):
    views, frames, padded, half = tokens[0].shape
    model, width = weights[0].shape
    rows = frames * padded
    with_query = len(weights) == 3
    out_shape = [pltpu.HBM((views, rows, 2 * width), BF16)]
    if with_query:
        out_shape = [pltpu.HBM((views, rows, width), BF16)] + out_shape

    def held(array):
        zeros = (0,) * len(array.shape)
        return pl.BlockSpec(array.shape, lambda i, s: zeros)

    operands = (*tokens, gain, *weights)
    return pl.pallas_call(
        functools.partial(project_kernel, with_query, joints),
        grid_spec=pltpu.PrefetchScalarGridSpec(
            num_scalar_prefetch=1,
            grid=(1,),
            in_specs=[held(a) for a in operands],
            out_specs=[held(a) for a in out_shape],
        ),
        out_shape=out_shape,
        compiler_params=params(40),
        cost_estimate=cost(
            2 * views * rows * model * len(weights) * width,
            2 * (views * rows * (model + len(weights) * width) + len(weights) * model * width),
        ),
        name="project",
    )(place, *operands)


def attend_kernel(first, joints, joint_ref, slot_ref, q_ref, *rest):
    sources = rest[:-5]
    mine_ref, theirs_ref, keyval, ones_ref, sems = rest[-5:]
    _, rows, width = q_ref.shape
    blocks = slot_ref.shape[1]
    step = pl.program_id(0)
    steps = pl.num_programs(0)
    joint = joint_ref[0]

    def fetch(view, buffer):
        for block in range(blocks):
            slot = slot_ref[first + view, block]
            begin = 0
            for source in sources:
                low, begin = begin, begin + source.shape[0]

                @pl.when((slot >= low) & (slot < begin))
                def _():
                    pltpu.make_async_copy(
                        source.at[slot - low],
                        keyval.at[buffer, pl.ds(block * rows, rows)],
                        sems.at[buffer, block],
                    ).start()

    buffer = lax.rem(step, 2)

    @pl.when(step == 0)
    def _():
        fetch(0, 0)
        row = lax.broadcasted_iota(jnp.int32, ones_ref.shape, 0)
        real = lax.rem(row, rows // 2) < joints
        ones_ref[...] = jnp.where(real, 1.0, 0.0).astype(BF16)

    @pl.when(step + 1 < steps)
    def _():
        fetch(step + 1, 1 - buffer)

    for block in range(blocks):
        pltpu.make_async_copy(
            sources[0].at[0], keyval.at[buffer, pl.ds(block * rows, rows)], sems.at[buffer, block]
        ).wait()

    lane = lax.broadcasted_iota(jnp.int32, (1, LANES), 1)
    ones = ones_ref[...]
    scale = HD**-0.5 * LOG2E
    half = rows // 2
    for pair in range(width // LANES):
        columns = slice(pair * LANES, (pair + 1) * LANES)
        query = q_ref[0, :, columns]
        keys = keyval[buffer, :, columns]
        values = jnp.concatenate(
            [keyval[buffer, :, width + pair * LANES : width + (pair + 1) * LANES], ones], axis=1
        )
        found = []
        for head in range(LANES // HD):
            mask = (lane // HD) == head
            scores = lax.dot_general(
                jnp.where(mask, query, jnp.zeros_like(query)),
                keys,
                (((1,), (1,)), ((), ())),
                preferred_element_type=F32,
            )
            top = jnp.max(scores, axis=1, keepdims=True)
            powers = jnp.exp2((scores - top) * scale).astype(BF16)
            found.append(jnp.dot(powers, values, preferred_element_type=F32))
        left = lane < HD
        total = jnp.where(left, found[0][:, :LANES], found[1][:, :LANES])
        weight = jnp.where(left, found[0][:, LANES:], found[1][:, LANES:])
        attended = total / weight
        early, late = attended[:half], attended[half:]
        mine_ref[0, :, columns] = jnp.where(joint == 0, early, late).astype(BF16)
        theirs_ref[0, :, columns] = jnp.where(joint == 0, late, early).astype(BF16)


def attend(joint, slots, first, query, sources, joints):
    views, rows, width = query.shape
    blocks = slots.shape[1]
    half = rows // 2
    out = jax.ShapeDtypeStruct((views, half, width), BF16)
    out_spec = pl.BlockSpec((1, half, width), lambda i, j, s: (i, 0, 0))
    heads = width // HD
    return pl.pallas_call(
        functools.partial(attend_kernel, first, joints),
        grid_spec=pltpu.PrefetchScalarGridSpec(
            num_scalar_prefetch=2,
            grid=(views,),
            in_specs=[pl.BlockSpec((1, rows, width), lambda i, j, s: (i, 0, 0))]
            + [pl.BlockSpec(memory_space=pl.ANY)] * len(sources),
            out_specs=[out_spec, out_spec],
            scratch_shapes=[
                pltpu.VMEM((2, blocks * rows, 2 * width), BF16),
                pltpu.VMEM((blocks * rows, LANES), BF16),
                pltpu.SemaphoreType.DMA((2, blocks)),
            ],
        ),
        out_shape=[out, out],
        compiler_params=params(56),
        cost_estimate=cost(
            2 * 2 * views * heads * rows * blocks * rows * 256,
            2 * views * rows * width * (2 + 2 * blocks),
            views * heads * rows * blocks * rows,
        ),
        name="attend",
    )(joint, slots, query, *sources)


def graph_kernel(packed, place_ref, *refs):
    mine_ref, theirs_ref, own_ref, other_ref, w_mine_ref, w_got_ref, w_shared_ref = refs[:7]
    gain_ref, skeleton_ref, degree_ref, w_graph_ref, *outs = refs[7:]
    views, padded, width = mine_ref.shape
    joint, core = place_ref[0], place_ref[1]
    model = w_graph_ref.shape[0]
    gain = gain_ref[...]

    def rows_of(ref):
        pieces = [ref[view].astype(F32) for view in range(views)]
        return jnp.concatenate(pieces, axis=0).astype(BF16)

    mine, theirs = rows_of(mine_ref), rows_of(theirs_ref)
    w_low = jnp.where(core == 0, w_got_ref[...], w_shared_ref[...])
    w_high = jnp.where(core == 0, w_shared_ref[...], w_got_ref[...])
    projected = (
        jnp.dot(mine, w_mine_ref[...], preferred_element_type=F32)
        + jnp.dot(theirs[:, : width // 2], w_low, preferred_element_type=F32)
        + jnp.dot(theirs[:, width // 2 :], w_high, preferred_element_type=F32)
    )
    hiddens, mixed = [], []
    for view in range(views):
        own, other = own_ref[view, 0].astype(F32), other_ref[view, 0].astype(F32)
        part = projected[view * padded : (view + 1) * padded]
        hidden = (both_halves(joint, own, other) + part).astype(BF16).astype(F32)
        normed = layer_norm(hidden, gain).astype(BF16)
        summed = jnp.dot(skeleton_ref[...], normed, preferred_element_type=F32)
        hiddens.append(hidden)
        mixed.append(summed / degree_ref[...])
    skeletal = jnp.concatenate(mixed, axis=0).astype(BF16)
    graph = jnp.dot(skeletal, w_graph_ref[...], preferred_element_type=F32)
    first = lax.broadcasted_iota(jnp.int32, (1, LANES), 1) < LANES // 2
    for view in range(views):
        term = graph[view * padded : (view + 1) * padded]
        if not packed:
            outs[0][view] = hiddens[view].astype(BF16)
            outs[1][view] = term.astype(BF16)
            continue
        for tile in range(model // LANES):
            columns = slice(tile * LANES, (tile + 1) * LANES)
            kept = hiddens[view][:, columns]
            turned = pltpu.roll(term[:, columns], LANES // 2, axis=1)
            outs[0][2 * tile, view] = jnp.where(first, kept, turned).astype(BF16)
            outs[0][2 * tile + 1, view] = jnp.where(first, turned, kept).astype(BF16)


def graph_part(packed, place, mine, theirs, own, other, held):
    views, padded, width = mine.shape
    half = own.shape[3]
    model = held[-1].shape[0]
    heads = pl.BlockSpec((views, padded, width), lambda i, j: (0, 0, 0))
    tokens = pl.BlockSpec((views, 1, padded, half), lambda i, j: (0, j[0], 0, 0))
    if packed:
        devices = 2 * model // LANES
        out_shape = [jax.ShapeDtypeStruct((devices, views, padded, LANES), BF16)]
        out_specs = [pl.BlockSpec((devices, views, padded, LANES), lambda i, j: (0, 0, 0, 0))]
    else:
        out_shape = [jax.ShapeDtypeStruct((views, padded, model), BF16)] * 2
        out_specs = [pl.BlockSpec((views, padded, model), lambda i, j: (0, 0, 0))] * 2
    return pl.pallas_call(
        functools.partial(graph_kernel, packed),
        grid_spec=pltpu.PrefetchScalarGridSpec(
            num_scalar_prefetch=1,
            grid=(1,),
            in_specs=[heads, heads, tokens, tokens]
            + [pl.BlockSpec(a.shape, lambda i, j: (0, 0)) for a in held],
            out_specs=out_specs,
        ),
        out_shape=out_shape,
        compiler_params=params(48),
        cost_estimate=cost(
            4 * views * padded * model * model, 2 * (views * padded * model * 4 + 2 * model * model)
        ),
        name="graph_part",
    )(place, mine, theirs, own, other, *held)


def mix_kernel(share, devices, order_ref, *rest):
    parts, (counts_ref, out_ref, wide) = rest[:-3], rest[-3:]
    views = wide.shape[0] // out_ref.shape[0]
    rows, channels, _ = out_ref.shape
    views_dev = views // devices
    first = 0
    for part in parts:
        chunk = part.shape[0] // devices
        for device in range(devices):
            at = (device * views_dev + first) * rows
            block = part[device * chunk : (device + 1) * chunk].astype(F32)
            wide[at : at + chunk * rows] = block.reshape(chunk * rows, LANES)
        first += chunk
    counts = counts_ref[...]
    flipped = order_ref[0] == 1
    for row in range(rows):
        lanes_first = wide[pl.ds(row, views, stride=rows), :].T
        low, high = lanes_first[:channels], lanes_first[channels:]
        term = jnp.where(flipped, low, high).astype(BF16)
        kept = jnp.where(flipped, high, low)
        mixed = jnp.dot(term, counts, preferred_element_type=F32)
        out_ref[row] = (kept + mixed * share).astype(BF16)


def mix(order, parts, counts, joints, share):
    views = counts.shape[0]
    devices = parts[0].shape[0]
    parts = [part.reshape(-1, *part.shape[2:]) for part in parts]
    padded = parts[0].shape[1]
    channels = LANES // 2
    rows = 16
    return pl.pallas_call(
        functools.partial(mix_kernel, share, devices),
        grid_spec=pltpu.PrefetchScalarGridSpec(
            num_scalar_prefetch=1,
            grid=(pl.cdiv(joints, rows),),
            in_specs=[
                pl.BlockSpec((part.shape[0], rows, LANES), lambda i, s: (0, i, 0))
                for part in parts
            ]
            + [pl.BlockSpec(counts.shape, lambda i, s: (0, 0))],
            out_specs=pl.BlockSpec((rows, channels, views), lambda i, s: (i, 0, 0)),
            scratch_shapes=[pltpu.VMEM((views * rows, LANES), F32)],
        ),
        out_shape=jax.ShapeDtypeStruct((joints, channels, views), BF16),
        compiler_params=params(32),
        cost_estimate=cost(
            2 * padded * LANES * views * views, 2 * padded * views * (LANES + channels)
        ),
        name="mix",
    )(order, *parts, counts)


def body(
    pose_tokens,
    gain_attn,
    gain_graph,
    w_query,
    w_key,
    w_value,
    w_out,
    w_graph,
    partners,
    parents,
    view_links,
):
    views_dev, frames, joints, half_width = pose_tokens.shape
    model = w_graph.shape[0]
    devices = lax.axis_size("view")
    place = lax.axis_index("view").astype(jnp.int32)
    joint_place = lax.axis_index("joint").astype(jnp.int32)
    joint = joint_place.reshape(1)
    num_views = devices * views_dev
    channels = model // devices
    padded = round_up(joints, 8)
    rows = frames * padded
    sizes = (2, 3, 3) if views_dev == 8 else (views_dev,)
    starts = [sum(sizes[:c]) for c in range(len(sizes))]
    chunks = range(len(sizes))
    packed = 2 * channels == LANES and num_views == LANES
    swap = [(0, 1), (1, 0)]
    up = [(i, (i + 1) % devices) for i in range(devices)]
    down = [(j, i) for i, j in up]
    swap_even = [(2 * v + j, 2 * v + 1 - j) for v in range(0, devices, 2) for j in (0, 1)]
    to_odd = [(2 * v + j, 2 * v + 2 + j) for v in range(0, devices, 2) for j in (0, 1)]
    gain_attn = gain_attn.reshape(1, model)
    gain_graph = gain_graph.reshape(1, model)
    where = jnp.stack((joint_place, lax.rem(place, 2)))

    to_other_core = [(v, v ^ 1) for v in range(devices)]

    own, other = [], []
    for c in chunks:
        part = lax.slice_in_dim(pose_tokens, starts[c], starts[c] + sizes[c])
        part = jnp.pad(part, ((0, 0), (0, 0), (0, padded - joints), (0, 0)))
        part = with_layout_constraint(part, Layout(major_to_minor=(0, 1, 2, 3)))
        own.append(part)
        other.append(lax.ppermute(part, "joint", swap))
    near = [lax.ppermute(part, "view", up) for part in own]
    query, here = [], []
    for c in chunks:
        q, kv = project(
            where, (own[c], other[c]), gain_attn, (w_query, w_key, w_value), joints
        )
        query.append(q)
        here.append(kv)
    after = [lax.ppermute(part, "view", down) for part in here]
    before = []
    for c in chunks:
        near_tied, other_tied, _ = lax.optimization_barrier(
            (near[c], other[c], here[max(c, min(1, len(sizes) - 1))])
        )
        far_even = lax.ppermute(near_tied, ("view", "joint"), swap_even)
        far_odd = lax.ppermute(other_tied, ("view", "joint"), to_odd)
        (kv,) = project(where, (near[c], far_even, far_odd), gain_attn, (w_key, w_value), joints)
        before.append(kv)
    window = before + here + after

    w_rows = w_out.shape[0] // 2
    w_part = lax.dynamic_slice_in_dim(w_out, lax.rem(place, 2) * w_rows, w_rows, 0)
    w_part, _ = lax.optimization_barrier((w_part, far_even))
    w_got = lax.ppermute(w_part, "joint", swap)
    w_shared = lax.ppermute(w_got, "view", to_other_core)

    first_view = place * views_dev
    own_slot = jnp.arange(views_dev, dtype=jnp.int32)[:, None] + views_dev
    slots = jnp.concatenate(
        (own_slot, jnp.mod(partners - first_view + views_dev, num_views)), axis=1
    )
    slots = jnp.clip(slots, 0, 3 * views_dev - 1)

    joint_ids = jnp.arange(padded, dtype=jnp.int32)
    line = jnp.concatenate((parents, jnp.full((padded - joints,), -1, jnp.int32)))
    skeleton = (
        (joint_ids[:, None] == joint_ids[None, :]).astype(F32)
        + (joint_ids[None, :] == line[:, None]).astype(F32)
        + (joint_ids[:, None] == line[None, :]).astype(F32)
    )
    degree = jnp.sum(skeleton, axis=1, keepdims=True)
    skeleton = skeleton.astype(BF16)
    held = (w_out, w_got, w_shared, gain_graph, skeleton, degree, w_graph)
    sent = []
    for c in chunks:
        q = query[c]
        if sent:
            q, _ = lax.optimization_barrier((q, sent[-1][0]))
        mine, theirs = attend(joint, slots, starts[c], q, window, joints)
        theirs = lax.ppermute(theirs, "joint", swap)
        sent.append(graph_part(packed, where, mine, theirs, own[c], other[c], held))

    view_ids = jnp.arange(num_views, dtype=jnp.int32)
    counts = (view_ids[:, None] == view_ids[None, :]).astype(F32)
    counts = counts + jnp.sum(
        (view_links[:, :, None] == view_ids[None, None, :]).astype(F32), axis=1
    )
    share = 1.0 / (view_links.shape[1] + 1)
    if packed:
        parts = [
            lax.all_to_all(part, "view", split_axis=0, concat_axis=0, tiled=True)
            for (part,) in sent
        ]
        order = lax.rem(place, 2).reshape(1)
        result = mix(order, parts, counts.T.astype(BF16), joints, share)
        return jnp.transpose(result, (1, 0, 2))[None]

    hidden = jnp.concatenate([part[0] for part in sent], axis=0)[:, :joints]
    graph_term = jnp.concatenate([part[1] for part in sent], axis=0)[:, :joints]
    residual = jnp.transpose(hidden, (2, 1, 0))
    graph_term = jnp.transpose(graph_term, (2, 1, 0))
    residual = lax.all_to_all(residual, "view", split_axis=0, concat_axis=2, tiled=True)
    graph_term = lax.all_to_all(graph_term, "view", split_axis=0, concat_axis=2, tiled=True)
    mixed = jnp.einsum(
        "cjv,wv->cjw", graph_term, counts.astype(BF16), preferred_element_type=F32
    )
    return (residual.astype(F32) + mixed * share).astype(BF16)[None]


def solution(mesh):
    placed = (
        P("view", None, None, "joint"),
        P(),
        P(),
        P(None, "joint"),
        P(None, "joint"),
        P(None, "joint"),
        P("joint", None),
        P(),
        P("view", None),
        P(),
        P(),
    )
    return jax.shard_map(
        body, mesh=mesh, in_specs=placed, out_specs=P("joint", "view", None, None), check_vma=False
    )
```

```python
import functools

import jax
import jax.numpy as jnp
from jax import lax
from jax.experimental import pallas as pl
from jax.experimental.layout import Layout, with_layout_constraint
from jax.experimental.pallas import tpu as pltpu
from jax.sharding import PartitionSpec as P

HD = 64
LANES = 128
norm_eps = 1e-05
MIB = 1024 * 1024
VMEM_MIB = 60
F32 = jnp.float32
BF16 = jnp.bfloat16
LOG2E = 1.4426950408889634


def round_up(value, unit):
    return (value + unit - 1) // unit * unit


def layer_norm(values, gain):
    average = jnp.mean(values, axis=-1, keepdims=True)
    centred = values - average
    spread = jnp.mean(centred * centred, axis=-1, keepdims=True)
    return centred * lax.rsqrt(spread + norm_eps) * gain


def both_halves(joint, own, other):
    low = jnp.where(joint == 0, own, other)
    high = jnp.where(joint == 0, other, own)
    return jnp.concatenate([low, high], axis=1)


def params(limit_mib):
    return pltpu.CompilerParams(vmem_limit_bytes=limit_mib * MIB)


def cost(flops, bytes_accessed, transcendentals=0):
    return pl.CostEstimate(
        flops=int(flops), bytes_accessed=int(bytes_accessed), transcendentals=int(transcendentals)
    )


def project_kernel(with_query, joints, place_ref, *refs):
    count = 3 if with_query else 2
    halves = 2 if with_query else 3
    tokens, rest = refs[:halves], refs[halves:]
    gain_ref, weights, outs = rest[0], rest[1 : 1 + count], rest[1 + count :]
    views, frames, padded, _ = tokens[0].shape
    joint = place_ref[0]
    gain = gain_ref[...]
    row = lax.broadcasted_iota(jnp.int32, (padded, 1), 0)
    real = row < joints
    pieces = []
    for view in range(views):
        for frame in range(frames):
            own = tokens[0][view, frame].astype(F32)
            other = tokens[1][view, frame].astype(F32)
            if not with_query:
                other = jnp.where(place_ref[1] == 0, other, tokens[2][view, frame].astype(F32))
            normed = layer_norm(both_halves(joint, own, other), gain)
            pieces.append(jnp.where(real, normed, normed[0:1]))
    flat = jnp.concatenate(pieces, axis=0).astype(BF16)
    real = jnp.concatenate([real] * (views * frames), axis=0)
    rows = frames * padded
    width = weights[-1].shape[1]
    keys = jnp.dot(flat, weights[-2][...], preferred_element_type=F32).astype(BF16)
    values = jnp.dot(flat, weights[-1][...], preferred_element_type=F32)
    values = jnp.where(real, values, 0.0).astype(BF16)
    for view in range(views):
        part = slice(view * rows, (view + 1) * rows)
        outs[-1][view, :, :width] = keys[part]
        outs[-1][view, :, width:] = values[part]
    if with_query:
        query = jnp.dot(flat, weights[0][...], preferred_element_type=F32)
        for view in range(views):
            for frame in range(frames):
                at = (view * frames + frame) * padded
                outs[0][view, frame] = query[at : at + padded].astype(BF16)


def project(place, tokens, gain, weights, joints):
    views, frames, padded, half = tokens[0].shape
    model, width = weights[0].shape
    rows = frames * padded
    with_query = len(weights) == 3
    step = 2 if views % 2 == 0 else 1
    out_shape = [pltpu.HBM((views, rows, 2 * width), BF16)]
    out_specs = [pl.BlockSpec((step, rows, 2 * width), lambda i, s: (i, 0, 0))]
    if with_query:
        out_shape = [pltpu.HBM((views, frames, padded, width), BF16)] + out_shape
        out_specs = [
            pl.BlockSpec((step, frames, padded, width), lambda i, s: (i, 0, 0, 0))
        ] + out_specs
    token = pl.BlockSpec((step, frames, padded, half), lambda i, s: (i, 0, 0, 0))
    weight = pl.BlockSpec((model, width), lambda i, s: (0, 0))
    return pl.pallas_call(
        functools.partial(project_kernel, with_query, joints),
        grid_spec=pltpu.PrefetchScalarGridSpec(
            num_scalar_prefetch=1,
            grid=(views // step,),
            in_specs=[token] * len(tokens)
            + [pl.BlockSpec((1, model), lambda i, s: (0, 0))]
            + [weight] * len(weights),
            out_specs=out_specs,
        ),
        out_shape=out_shape,
        compiler_params=params(VMEM_MIB),
        cost_estimate=cost(
            2 * views * rows * model * len(weights) * width,
            2 * (views * rows * (model + len(weights) * width) + len(weights) * model * width),
        ),
        name="project",
    )(place, *tokens, gain, *weights)


def attend_kernel(first, joints, place_ref, slot_ref, q_ref, *rest):
    sources = rest[:-4]
    out_ref, keyval, ones_ref, sems = rest[-4:]
    _, _, padded, width = q_ref.shape
    blocks = slot_ref.shape[1]
    rows = keyval.shape[1] // blocks
    step = pl.program_id(0)
    steps = pl.num_programs(0)

    def fetch(view, buffer):
        for block in range(blocks):
            slot = slot_ref[first + view, block]
            begin = 0
            for source in sources:
                low, begin = begin, begin + source.shape[0]

                @pl.when((slot >= low) & (slot < begin))
                def _():
                    pltpu.make_async_copy(
                        source.at[slot - low],
                        keyval.at[buffer, pl.ds(block * rows, rows)],
                        sems.at[buffer, block],
                    ).start()

    buffer = lax.rem(step, 2)

    @pl.when(step == 0)
    def _():
        fetch(0, 0)
        row = lax.broadcasted_iota(jnp.int32, (padded, LANES), 0)
        real = jnp.where(row < joints, 1.0, 0.0)
        ones_ref[...] = jnp.concatenate([real] * (blocks * rows // padded), axis=0).astype(BF16)

    @pl.when(step + 1 < steps)
    def _():
        fetch(step + 1, 1 - buffer)

    for block in range(blocks):
        pltpu.make_async_copy(
            sources[0].at[0], keyval.at[buffer, pl.ds(block * rows, rows)], sems.at[buffer, block]
        ).wait()

    left = lax.broadcasted_iota(jnp.int32, (1, LANES), 1) < HD
    ones = ones_ref[...]
    scale = HD**-0.5 * LOG2E
    for pair in range(width // LANES):
        columns = slice(pair * LANES, (pair + 1) * LANES)
        query = q_ref[0, 0, :, columns].astype(F32)
        stacked = jnp.concatenate(
            [jnp.where(left, query, 0.0), jnp.where(left, 0.0, query)], axis=0
        ).astype(BF16)
        values = jnp.concatenate(
            [keyval[buffer, :, width + pair * LANES : width + (pair + 1) * LANES], ones], axis=1
        )
        scores = lax.dot_general(
            stacked,
            keyval[buffer, :, columns],
            (((1,), (1,)), ((), ())),
            preferred_element_type=F32,
        )
        top = jnp.max(scores, axis=1, keepdims=True)
        powers = jnp.exp2((scores - top) * scale).astype(BF16)
        found = jnp.dot(powers, values, preferred_element_type=F32)
        total = jnp.where(left, found[:padded, :LANES], found[padded:, :LANES])
        weight = jnp.where(left, found[:padded, LANES:], found[padded:, LANES:])
        out_ref[0, :, columns] = (total / weight).astype(BF16)


def attend(place, frame, slots, first, query, begin, views, sources, joints):
    _, _, padded, width = query.shape
    _, rows, _ = sources[0].shape
    blocks = slots.shape[1]
    heads = width // HD
    return pl.pallas_call(
        functools.partial(attend_kernel, first, joints),
        grid_spec=pltpu.PrefetchScalarGridSpec(
            num_scalar_prefetch=2,
            grid=(views,),
            in_specs=[
                pl.BlockSpec((1, 1, padded, width), lambda i, p, s: (begin + i, p[frame], 0, 0))
            ]
            + [pl.BlockSpec(memory_space=pl.ANY)] * len(sources),
            out_specs=pl.BlockSpec((1, padded, width), lambda i, p, s: (i, 0, 0)),
            scratch_shapes=[
                pltpu.VMEM((2, blocks * rows, 2 * width), BF16),
                pltpu.VMEM((blocks * rows, LANES), BF16),
                pltpu.SemaphoreType.DMA((2, blocks)),
            ],
        ),
        out_shape=jax.ShapeDtypeStruct((views, padded, width), BF16),
        compiler_params=params(VMEM_MIB),
        cost_estimate=cost(
            2 * 2 * views * heads * padded * blocks * rows * 256,
            2 * views * padded * width * 2 + 2 * views * blocks * rows * 2 * width,
            views * heads * padded * blocks * rows,
        ),
        name="attend",
    )(place, slots, query, *sources)


def graph_kernel(packed, place_ref, *refs):
    mine_ref, theirs_ref, own_ref, other_ref, w_mine_ref, w_got_ref, w_shared_ref = refs[:7]
    gain_ref, skeleton_ref, degree_ref, w_graph_ref, *outs = refs[7:]
    views, padded, width = mine_ref.shape
    joint, core = place_ref[0], place_ref[1]
    model = w_graph_ref.shape[0]
    gain = gain_ref[...]

    def rows_of(ref):
        pieces = [ref[view].astype(F32) for view in range(views)]
        return jnp.concatenate(pieces, axis=0).astype(BF16)

    mine, theirs = rows_of(mine_ref), rows_of(theirs_ref)
    w_low = jnp.where(core == 0, w_got_ref[...], w_shared_ref[...])
    w_high = jnp.where(core == 0, w_shared_ref[...], w_got_ref[...])
    projected = (
        jnp.dot(mine, w_mine_ref[...], preferred_element_type=F32)
        + jnp.dot(theirs[:, : width // 2], w_low, preferred_element_type=F32)
        + jnp.dot(theirs[:, width // 2 :], w_high, preferred_element_type=F32)
    )
    hiddens, mixed = [], []
    for view in range(views):
        own, other = own_ref[view, 0].astype(F32), other_ref[view, 0].astype(F32)
        part = projected[view * padded : (view + 1) * padded]
        hidden = (both_halves(joint, own, other) + part).astype(BF16).astype(F32)
        normed = layer_norm(hidden, gain).astype(BF16)
        summed = jnp.dot(skeleton_ref[...], normed, preferred_element_type=F32)
        hiddens.append(hidden)
        mixed.append(summed / degree_ref[...])
    skeletal = jnp.concatenate(mixed, axis=0).astype(BF16)
    graph = jnp.dot(skeletal, w_graph_ref[...], preferred_element_type=F32)
    first = lax.broadcasted_iota(jnp.int32, (1, LANES), 1) < LANES // 2
    for view in range(views):
        term = graph[view * padded : (view + 1) * padded]
        if not packed:
            outs[0][view] = hiddens[view].astype(BF16)
            outs[1][view] = term.astype(BF16)
            continue
        for tile in range(model // LANES):
            columns = slice(tile * LANES, (tile + 1) * LANES)
            kept = hiddens[view][:, columns]
            turned = pltpu.roll(term[:, columns], LANES // 2, axis=1)
            outs[0][2 * tile, view] = jnp.where(first, kept, turned).astype(BF16)
            outs[0][2 * tile + 1, view] = jnp.where(first, turned, kept).astype(BF16)


def graph_part(packed, place, mine, theirs, own, other, begin, held):
    views, padded, width = mine.shape
    half = own.shape[3]
    model = held[-1].shape[0]
    heads = pl.BlockSpec((views, padded, width), lambda i, j: (0, 0, 0))
    tokens = pl.BlockSpec((views, 1, padded, half), lambda i, j: (begin // views, j[0], 0, 0))
    if packed:
        devices = 2 * model // LANES
        out_shape = [jax.ShapeDtypeStruct((devices, views, padded, LANES), BF16)]
        out_specs = [pl.BlockSpec((devices, views, padded, LANES), lambda i, j: (0, 0, 0, 0))]
    else:
        out_shape = [jax.ShapeDtypeStruct((views, padded, model), BF16)] * 2
        out_specs = [pl.BlockSpec((views, padded, model), lambda i, j: (0, 0, 0))] * 2
    return pl.pallas_call(
        functools.partial(graph_kernel, packed),
        grid_spec=pltpu.PrefetchScalarGridSpec(
            num_scalar_prefetch=1,
            grid=(1,),
            in_specs=[heads, heads, tokens, tokens]
            + [pl.BlockSpec(a.shape, lambda i, j: (0, 0)) for a in held],
            out_specs=out_specs,
        ),
        out_shape=out_shape,
        compiler_params=params(VMEM_MIB),
        cost_estimate=cost(
            4 * views * padded * model * model, 2 * (views * padded * model * 4 + 2 * model * model)
        ),
        name="graph_part",
    )(place, mine, theirs, own, other, *held)


def mix_kernel(share, devices, order_ref, *rest):
    parts, (counts_ref, out_ref, wide) = rest[:-3], rest[-3:]
    views = wide.shape[0] // out_ref.shape[0]
    rows, channels, _ = out_ref.shape
    views_dev = views // devices
    first = 0
    for part in parts:
        chunk = part.shape[0] // devices
        for device in range(devices):
            at = (device * views_dev + first) * rows
            block = part[device * chunk : (device + 1) * chunk].astype(F32)
            wide[at : at + chunk * rows] = block.reshape(chunk * rows, LANES)
        first += chunk
    counts = counts_ref[...]
    flipped = order_ref[0] == 1
    for row in range(rows):
        lanes_first = wide[pl.ds(row, views, stride=rows), :].T
        low, high = lanes_first[:channels], lanes_first[channels:]
        term = jnp.where(flipped, low, high).astype(BF16)
        kept = jnp.where(flipped, high, low)
        mixed = jnp.dot(term, counts, preferred_element_type=F32)
        out_ref[row] = (kept + mixed * share).astype(BF16)


def mix(order, parts, counts, joints, share):
    views = counts.shape[0]
    devices = parts[0].shape[0]
    parts = [part.reshape(-1, *part.shape[2:]) for part in parts]
    padded = parts[0].shape[1]
    channels = LANES // 2
    rows = 16
    return pl.pallas_call(
        functools.partial(mix_kernel, share, devices),
        grid_spec=pltpu.PrefetchScalarGridSpec(
            num_scalar_prefetch=1,
            grid=(pl.cdiv(joints, rows),),
            in_specs=[
                pl.BlockSpec((part.shape[0], rows, LANES), lambda i, s: (0, i, 0))
                for part in parts
            ]
            + [pl.BlockSpec(counts.shape, lambda i, s: (0, 0))],
            out_specs=pl.BlockSpec((rows, channels, views), lambda i, s: (i, 0, 0)),
            scratch_shapes=[pltpu.VMEM((views * rows, LANES), F32)],
        ),
        out_shape=jax.ShapeDtypeStruct((joints, channels, views), BF16),
        compiler_params=params(VMEM_MIB),
        cost_estimate=cost(
            2 * padded * LANES * views * views, 2 * padded * views * (LANES + channels)
        ),
        name="mix",
    )(order, *parts, counts)


def body(
    pose_tokens,
    gain_attn,
    gain_graph,
    w_query,
    w_key,
    w_value,
    w_out,
    w_graph,
    partners,
    parents,
    view_links,
):
    views_dev, frames, joints, half_width = pose_tokens.shape
    model = w_graph.shape[0]
    devices = lax.axis_size("view")
    place = lax.axis_index("view").astype(jnp.int32)
    joint_place = lax.axis_index("joint").astype(jnp.int32)
    num_views = devices * views_dev
    channels = model // devices
    padded = round_up(joints, 8)
    rows = frames * padded
    sizes = (2, 2, 4) if views_dev == 8 else (views_dev,)
    tail = 2 if views_dev == 8 else views_dev
    starts = [sum(sizes[:c]) for c in range(len(sizes))]
    chunks = range(len(sizes))
    packed = 2 * channels == LANES and num_views == LANES
    swap = [(0, 1), (1, 0)]
    up = [(i, (i + 1) % devices) for i in range(devices)]
    down = [(j, i) for i, j in up]
    swap_even = [(2 * v + j, 2 * v + 1 - j) for v in range(0, devices, 2) for j in (0, 1)]
    to_odd = [(2 * v + j, 2 * v + 2 + j) for v in range(0, devices, 2) for j in (0, 1)]
    gain_attn = gain_attn.reshape(1, model)
    gain_graph = gain_graph.reshape(1, model)
    where = jnp.stack((joint_place, lax.rem(place, 2), 1 - joint_place))

    to_other_core = [(v, v ^ 1) for v in range(devices)]

    def tied(array, *others):
        return lax.optimization_barrier((array, *others))[0]

    own = []
    for c in chunks:
        part = lax.slice_in_dim(pose_tokens, starts[c], starts[c] + sizes[c])
        part = jnp.pad(part, ((0, 0), (0, 0), (0, padded - joints), (0, 0)))
        own.append(with_layout_constraint(part, Layout(major_to_minor=(0, 1, 2, 3))))
    near = [lax.ppermute(part, "view", up) for part in own]
    other, query, here = [], [], []
    for c in chunks:
        part = tied(own[c], *other[-1:], *here[:-1])
        other.append(lax.ppermute(part, "joint", swap))
        q, kv = project(
            where, (own[c], other[c]), gain_attn, (w_query, w_key, w_value), joints
        )
        query.append(q)
        here.append(kv)
    after = [lax.ppermute(part, "view", down) for part in here]
    before, far = [], []
    for c in chunks:
        if c < 2:
            part = tied(near[c], other[-1], *here[:2])
        else:
            part = tied(near[c], far[c - 2], here[c])
        far.append(lax.ppermute(part, ("view", "joint"), swap_even))
        far_odd = lax.ppermute(tied(other[c], here[c]), ("view", "joint"), to_odd)
        (kv,) = project(where, (near[c], far[c], far_odd), gain_attn, (w_key, w_value), joints)
        before.append(kv)
    window = before + here + after

    w_rows = w_out.shape[0] // 2
    w_part = lax.dynamic_slice_in_dim(w_out, lax.rem(place, 2) * w_rows, w_rows, 0)
    w_part, _ = lax.optimization_barrier((w_part, far[-1]))
    w_got = lax.ppermute(w_part, "joint", swap)
    w_shared = lax.ppermute(w_got, "view", to_other_core)

    first_view = place * views_dev
    own_slot = jnp.arange(views_dev, dtype=jnp.int32)[:, None] + views_dev
    slots = jnp.concatenate(
        (own_slot, jnp.mod(partners - first_view + views_dev, num_views)), axis=1
    )
    slots = jnp.clip(slots, 0, 3 * views_dev - 1)

    joint_ids = jnp.arange(padded, dtype=jnp.int32)
    line = jnp.concatenate((parents, jnp.full((padded - joints,), -1, jnp.int32)))
    skeleton = (
        (joint_ids[:, None] == joint_ids[None, :]).astype(F32)
        + (joint_ids[None, :] == line[:, None]).astype(F32)
        + (joint_ids[:, None] == line[None, :]).astype(F32)
    )
    degree = jnp.sum(skeleton, axis=1, keepdims=True)
    skeleton = skeleton.astype(BF16)
    held = (w_out, w_got, w_shared, gain_graph, skeleton, degree, w_graph)
    sent = []
    for c in chunks:
        for begin in range(0, sizes[c], tail):
            first = starts[c] + begin
            q = query[c]
            if sent:
                q = tied(q, sent[-1][0])
            theirs = attend(where, 2, slots, first, q, begin, tail, window, joints)
            q = tied(q, theirs)
            moved = lax.ppermute(theirs, "joint", swap)
            mine = attend(where, 0, slots, first, q, begin, tail, window, joints)
            sent.append(
                graph_part(packed, where, mine, moved, own[c], other[c], begin, held)
            )

    view_ids = jnp.arange(num_views, dtype=jnp.int32)
    counts = (view_ids[:, None] == view_ids[None, :]).astype(F32)
    counts = counts + jnp.sum(
        (view_links[:, :, None] == view_ids[None, None, :]).astype(F32), axis=1
    )
    share = 1.0 / (view_links.shape[1] + 1)
    if packed:
        parts = [
            lax.all_to_all(part, "view", split_axis=0, concat_axis=0, tiled=True)
            for (part,) in sent
        ]
        order = lax.rem(place, 2).reshape(1)
        result = mix(order, parts, counts.T.astype(BF16), joints, share)
        return jnp.transpose(result, (1, 0, 2))[None]

    hidden = jnp.concatenate([part[0] for part in sent], axis=0)[:, :joints]
    graph_term = jnp.concatenate([part[1] for part in sent], axis=0)[:, :joints]
    residual = jnp.transpose(hidden, (2, 1, 0))
    graph_term = jnp.transpose(graph_term, (2, 1, 0))
    residual = lax.all_to_all(residual, "view", split_axis=0, concat_axis=2, tiled=True)
    graph_term = lax.all_to_all(graph_term, "view", split_axis=0, concat_axis=2, tiled=True)
    mixed = jnp.einsum(
        "cjv,wv->cjw", graph_term, counts.astype(BF16), preferred_element_type=F32
    )
    return (residual.astype(F32) + mixed * share).astype(BF16)[None]


def solution(mesh):
    placed = (
        P("view", None, None, "joint"),
        P(),
        P(),
        P(None, "joint"),
        P(None, "joint"),
        P(None, "joint"),
        P("joint", None),
        P(),
        P("view", None),
        P(),
        P(),
    )
    return jax.shard_map(
        body, mesh=mesh, in_specs=placed, out_specs=P("joint", "view", None, None), check_vma=False
    )
```

```python
import functools

import jax
import jax.numpy as jnp
from jax import lax
from jax.experimental import pallas as pl
from jax.experimental.layout import Layout, with_layout_constraint
from jax.experimental.pallas import tpu as pltpu
from jax.sharding import PartitionSpec as P

HD = 64
LANES = 128
norm_eps = 1e-05
MIB = 1024 * 1024
VMEM_MIB = 32
F32 = jnp.float32
BF16 = jnp.bfloat16
LOG2E = 1.4426950408889634


def round_up(value, unit):
    return (value + unit - 1) // unit * unit


def layer_norm(values, gain):
    average = jnp.mean(values, axis=-1, keepdims=True)
    centred = values - average
    spread = jnp.mean(centred * centred, axis=-1, keepdims=True)
    return centred * lax.rsqrt(spread + norm_eps) * gain


def both_halves(joint, own, other):
    low = jnp.where(joint == 0, own, other)
    high = jnp.where(joint == 0, other, own)
    return jnp.concatenate([low, high], axis=1)


def params(limit_mib):
    return pltpu.CompilerParams(vmem_limit_bytes=limit_mib * MIB)


def cost(flops, bytes_accessed, transcendentals=0):
    return pl.CostEstimate(
        flops=int(flops), bytes_accessed=int(bytes_accessed), transcendentals=int(transcendentals)
    )


def project_kernel(with_query, joints, place_ref, *refs):
    count = 3 if with_query else 2
    halves = 2 if with_query else 3
    tokens, rest = refs[:halves], refs[halves:]
    gain_ref, weights, outs = rest[0], rest[1 : 1 + count], rest[1 + count :]
    views, frames, padded, _ = tokens[0].shape
    joint = place_ref[0]
    gain = gain_ref[...]
    row = lax.broadcasted_iota(jnp.int32, (padded, 1), 0)
    real = row < joints
    pieces = []
    for view in range(views):
        for frame in range(frames):
            own = tokens[0][view, frame].astype(F32)
            other = tokens[1][view, frame].astype(F32)
            if not with_query:
                other = jnp.where(place_ref[1] == 0, other, tokens[2][view, frame].astype(F32))
            normed = layer_norm(both_halves(joint, own, other), gain)
            pieces.append(jnp.where(real, normed, normed[0:1]))
    flat = jnp.concatenate(pieces, axis=0).astype(BF16)
    real = jnp.concatenate([real] * (views * frames), axis=0)
    rows = frames * padded
    width = weights[-1].shape[1]
    keys = jnp.dot(flat, weights[-2][...], preferred_element_type=F32).astype(BF16)
    values = jnp.dot(flat, weights[-1][...], preferred_element_type=F32)
    values = jnp.where(real, values, 0.0).astype(BF16)
    for view in range(views):
        part = slice(view * rows, (view + 1) * rows)
        for pair in range(width // LANES):
            columns = slice(pair * LANES, (pair + 1) * LANES)
            outs[-1][view, pair, :, :LANES] = keys[part, columns]
            outs[-1][view, pair, :, LANES:] = values[part, columns]
    if with_query:
        query = jnp.dot(flat, weights[0][...], preferred_element_type=F32)
        for view in range(views):
            for frame in range(frames):
                at = (view * frames + frame) * padded
                outs[0][view, frame] = query[at : at + padded].astype(BF16)


def project(place, tokens, gain, weights, joints):
    views, frames, padded, half = tokens[0].shape
    model, width = weights[0].shape
    rows = frames * padded
    with_query = len(weights) == 3
    step = 2 if views % 2 == 0 else 1
    pairs = width // LANES
    out_shape = [pltpu.HBM((views, pairs, rows, 2 * LANES), BF16)]
    out_specs = [pl.BlockSpec((step, pairs, rows, 2 * LANES), lambda i, s: (i, 0, 0, 0))]
    if with_query:
        out_shape = [pltpu.HBM((views, frames, padded, width), BF16)] + out_shape
        out_specs = [
            pl.BlockSpec((step, frames, padded, width), lambda i, s: (i, 0, 0, 0))
        ] + out_specs
    token = pl.BlockSpec((step, frames, padded, half), lambda i, s: (i, 0, 0, 0))
    weight = pl.BlockSpec((model, width), lambda i, s: (0, 0))
    return pl.pallas_call(
        functools.partial(project_kernel, with_query, joints),
        grid_spec=pltpu.PrefetchScalarGridSpec(
            num_scalar_prefetch=1,
            grid=(views // step,),
            in_specs=[token] * len(tokens)
            + [pl.BlockSpec((1, model), lambda i, s: (0, 0))]
            + [weight] * len(weights),
            out_specs=out_specs,
        ),
        out_shape=out_shape,
        compiler_params=params(VMEM_MIB),
        cost_estimate=cost(
            2 * views * rows * model * len(weights) * width,
            2 * (views * rows * (model + len(weights) * width) + len(weights) * model * width),
        ),
        name="project",
    )(place, *tokens, gain, *weights)


def attend_kernel(first, joints, place_ref, slot_ref, q_ref, *rest):
    sources = rest[:-4]
    out_ref, keyval, ones_ref, sems = rest[-4:]
    _, _, padded, width = q_ref.shape
    blocks = slot_ref.shape[1]
    rows = keyval.shape[2] // blocks
    pairs = width // LANES
    group = pairs // 2
    step = pl.program_id(0)
    steps = pl.num_programs(0)

    def copy(source, slot, part, block, buffer):
        taken = pl.ds(part * group, group)
        return pltpu.make_async_copy(
            source.at[slot, taken],
            keyval.at[buffer, taken, pl.ds(block * rows, rows)],
            sems.at[buffer, block, part],
        )

    def fetch(view, buffer, parts):
        for block in range(blocks):
            slot = slot_ref[first + view, block]
            begin = 0
            for source in sources:
                low, begin = begin, begin + source.shape[0]

                @pl.when((slot >= low) & (slot < begin))
                def _():
                    for part in parts:
                        copy(source, slot - low, part, block, buffer).start()

    buffer = lax.rem(step, 2)

    @pl.when(step == 0)
    def _():
        fetch(0, 0, (0,))
        fetch(0, 0, (1,))
        row = lax.broadcasted_iota(jnp.int32, (padded, LANES), 0)
        real = jnp.where(row < joints, 1.0, 0.0)
        ones_ref[...] = jnp.concatenate([real] * (blocks * rows // padded), axis=0).astype(BF16)

    @pl.when(step + 1 < steps)
    def _():
        fetch(step + 1, 1 - buffer, (0, 1))

    left = lax.broadcasted_iota(jnp.int32, (1, LANES), 1) < HD
    ones = ones_ref[...]
    scale = HD**-0.5 * LOG2E
    for pair in range(pairs):
        if pair % group == 0:
            for block in range(blocks):
                copy(sources[0], 0, pair // group, block, buffer).wait()
        columns = slice(pair * LANES, (pair + 1) * LANES)
        query = q_ref[0, 0, :, columns].astype(F32)
        stacked = jnp.concatenate(
            [jnp.where(left, query, 0.0), jnp.where(left, 0.0, query)], axis=0
        ).astype(BF16)
        values = jnp.concatenate(
            [keyval[buffer, pair, :, LANES:], ones], axis=1
        )
        scores = lax.dot_general(
            stacked,
            keyval[buffer, pair, :, :LANES],
            (((1,), (1,)), ((), ())),
            preferred_element_type=F32,
        )
        top = jnp.max(scores, axis=1, keepdims=True)
        powers = jnp.exp2((scores - top) * scale).astype(BF16)
        found = jnp.dot(powers, values, preferred_element_type=F32)
        total = jnp.where(left, found[:padded, :LANES], found[padded:, :LANES])
        weight = jnp.where(left, found[:padded, LANES:], found[padded:, LANES:])
        out_ref[0, :, columns] = (total / weight).astype(BF16)


def attend(place, frame, slots, first, query, begin, views, sources, joints):
    _, _, padded, width = query.shape
    _, pairs, rows, _ = sources[0].shape
    blocks = slots.shape[1]
    heads = width // HD
    return pl.pallas_call(
        functools.partial(attend_kernel, first, joints),
        grid_spec=pltpu.PrefetchScalarGridSpec(
            num_scalar_prefetch=2,
            grid=(views,),
            in_specs=[
                pl.BlockSpec((1, 1, padded, width), lambda i, p, s: (begin + i, p[frame], 0, 0))
            ]
            + [pl.BlockSpec(memory_space=pl.ANY)] * len(sources),
            out_specs=pl.BlockSpec((1, padded, width), lambda i, p, s: (i, 0, 0)),
            scratch_shapes=[
                pltpu.VMEM((2, pairs, blocks * rows, 2 * LANES), BF16),
                pltpu.VMEM((blocks * rows, LANES), BF16),
                pltpu.SemaphoreType.DMA((2, blocks, 2)),
            ],
        ),
        out_shape=jax.ShapeDtypeStruct((views, padded, width), BF16),
        compiler_params=params(VMEM_MIB),
        cost_estimate=cost(
            2 * 2 * views * heads * padded * blocks * rows * 256,
            2 * views * padded * width * 2 + 2 * views * blocks * rows * 2 * width,
            views * heads * padded * blocks * rows,
        ),
        name="attend",
    )(place, slots, query, *sources)


def graph_kernel(packed, place_ref, *refs):
    mine_ref, theirs_ref, own_ref, other_ref, w_mine_ref, w_got_ref, w_shared_ref = refs[:7]
    gain_ref, skeleton_ref, degree_ref, w_graph_ref, *outs = refs[7:]
    views, padded, width = mine_ref.shape
    joint, core = place_ref[0], place_ref[1]
    model = w_graph_ref.shape[0]
    gain = gain_ref[...]

    def rows_of(ref):
        pieces = [ref[view].astype(F32) for view in range(views)]
        return jnp.concatenate(pieces, axis=0).astype(BF16)

    mine, theirs = rows_of(mine_ref), rows_of(theirs_ref)
    w_low = jnp.where(core == 0, w_got_ref[...], w_shared_ref[...])
    w_high = jnp.where(core == 0, w_shared_ref[...], w_got_ref[...])
    projected = (
        jnp.dot(mine, w_mine_ref[...], preferred_element_type=F32)
        + jnp.dot(theirs[:, : width // 2], w_low, preferred_element_type=F32)
        + jnp.dot(theirs[:, width // 2 :], w_high, preferred_element_type=F32)
    )
    hiddens, mixed = [], []
    for view in range(views):
        own, other = own_ref[view, 0].astype(F32), other_ref[view, 0].astype(F32)
        part = projected[view * padded : (view + 1) * padded]
        hidden = (both_halves(joint, own, other) + part).astype(BF16).astype(F32)
        normed = layer_norm(hidden, gain).astype(BF16)
        summed = jnp.dot(skeleton_ref[...], normed, preferred_element_type=F32)
        hiddens.append(hidden)
        mixed.append(summed / degree_ref[...])
    skeletal = jnp.concatenate(mixed, axis=0).astype(BF16)
    graph = jnp.dot(skeletal, w_graph_ref[...], preferred_element_type=F32)
    first = lax.broadcasted_iota(jnp.int32, (1, LANES), 1) < LANES // 2
    for view in range(views):
        term = graph[view * padded : (view + 1) * padded]
        if not packed:
            outs[0][view] = hiddens[view].astype(BF16)
            outs[1][view] = term.astype(BF16)
            continue
        for tile in range(model // LANES):
            columns = slice(tile * LANES, (tile + 1) * LANES)
            kept = hiddens[view][:, columns]
            turned = pltpu.roll(term[:, columns], LANES // 2, axis=1)
            outs[0][2 * tile, view] = jnp.where(first, kept, turned).astype(BF16)
            outs[0][2 * tile + 1, view] = jnp.where(first, turned, kept).astype(BF16)


def graph_part(packed, place, mine, theirs, own, other, begin, held):
    views, padded, width = mine.shape
    half = own.shape[3]
    model = held[-1].shape[0]
    heads = pl.BlockSpec((views, padded, width), lambda i, j: (0, 0, 0))
    tokens = pl.BlockSpec((views, 1, padded, half), lambda i, j: (begin // views, j[0], 0, 0))
    if packed:
        devices = 2 * model // LANES
        out_shape = [jax.ShapeDtypeStruct((devices, views, padded, LANES), BF16)]
        out_specs = [pl.BlockSpec((devices, views, padded, LANES), lambda i, j: (0, 0, 0, 0))]
    else:
        out_shape = [jax.ShapeDtypeStruct((views, padded, model), BF16)] * 2
        out_specs = [pl.BlockSpec((views, padded, model), lambda i, j: (0, 0, 0))] * 2
    return pl.pallas_call(
        functools.partial(graph_kernel, packed),
        grid_spec=pltpu.PrefetchScalarGridSpec(
            num_scalar_prefetch=1,
            grid=(1,),
            in_specs=[heads, heads, tokens, tokens]
            + [pl.BlockSpec(a.shape, lambda i, j: (0, 0)) for a in held],
            out_specs=out_specs,
        ),
        out_shape=out_shape,
        compiler_params=params(VMEM_MIB),
        cost_estimate=cost(
            4 * views * padded * model * model, 2 * (views * padded * model * 4 + 2 * model * model)
        ),
        name="graph_part",
    )(place, mine, theirs, own, other, *held)


def mix_kernel(share, devices, order_ref, *rest):
    parts, (counts_ref, out_ref, wide) = rest[:-3], rest[-3:]
    views = wide.shape[0] // out_ref.shape[0]
    rows, channels, _ = out_ref.shape
    views_dev = views // devices
    first = 0
    for part in parts:
        chunk = part.shape[0] // devices
        for device in range(devices):
            at = (device * views_dev + first) * rows
            block = part[device * chunk : (device + 1) * chunk].astype(F32)
            wide[at : at + chunk * rows] = block.reshape(chunk * rows, LANES)
        first += chunk
    counts = counts_ref[...]
    flipped = order_ref[0] == 1
    for row in range(rows):
        lanes_first = wide[pl.ds(row, views, stride=rows), :].T
        low, high = lanes_first[:channels], lanes_first[channels:]
        term = jnp.where(flipped, low, high).astype(BF16)
        kept = jnp.where(flipped, high, low)
        mixed = jnp.dot(term, counts, preferred_element_type=F32)
        out_ref[row] = (kept + mixed * share).astype(BF16)


def mix(order, parts, counts, joints, share):
    views = counts.shape[0]
    devices = parts[0].shape[0]
    parts = [part.reshape(-1, *part.shape[2:]) for part in parts]
    padded = parts[0].shape[1]
    channels = LANES // 2
    rows = 16
    return pl.pallas_call(
        functools.partial(mix_kernel, share, devices),
        grid_spec=pltpu.PrefetchScalarGridSpec(
            num_scalar_prefetch=1,
            grid=(pl.cdiv(joints, rows),),
            in_specs=[
                pl.BlockSpec((part.shape[0], rows, LANES), lambda i, s: (0, i, 0))
                for part in parts
            ]
            + [pl.BlockSpec(counts.shape, lambda i, s: (0, 0))],
            out_specs=pl.BlockSpec((rows, channels, views), lambda i, s: (i, 0, 0)),
            scratch_shapes=[pltpu.VMEM((views * rows, LANES), F32)],
        ),
        out_shape=jax.ShapeDtypeStruct((joints, channels, views), BF16),
        compiler_params=params(VMEM_MIB),
        cost_estimate=cost(
            2 * padded * LANES * views * views, 2 * padded * views * (LANES + channels)
        ),
        name="mix",
    )(order, *parts, counts)


def body(
    pose_tokens,
    gain_attn,
    gain_graph,
    w_query,
    w_key,
    w_value,
    w_out,
    w_graph,
    partners,
    parents,
    view_links,
):
    views_dev, frames, joints, half_width = pose_tokens.shape
    model = w_graph.shape[0]
    devices = lax.axis_size("view")
    place = lax.axis_index("view").astype(jnp.int32)
    joint_place = lax.axis_index("joint").astype(jnp.int32)
    num_views = devices * views_dev
    channels = model // devices
    padded = round_up(joints, 8)
    rows = frames * padded
    sizes = (2, 2, 4) if views_dev == 8 else (views_dev,)
    tail = 2 if views_dev == 8 else views_dev
    starts = [sum(sizes[:c]) for c in range(len(sizes))]
    chunks = range(len(sizes))
    packed = 2 * channels == LANES and num_views == LANES
    swap = [(0, 1), (1, 0)]
    up = [(i, (i + 1) % devices) for i in range(devices)]
    down = [(j, i) for i, j in up]
    swap_even = [(2 * v + j, 2 * v + 1 - j) for v in range(0, devices, 2) for j in (0, 1)]
    to_odd = [(2 * v + j, 2 * v + 2 + j) for v in range(0, devices, 2) for j in (0, 1)]
    gain_attn = gain_attn.reshape(1, model)
    gain_graph = gain_graph.reshape(1, model)
    where = jnp.stack((joint_place, lax.rem(place, 2), 1 - joint_place))

    to_other_core = [(v, v ^ 1) for v in range(devices)]

    def tied(array, *others):
        return lax.optimization_barrier((array, *others))[0]

    def padded_views(begin, count):
        part = lax.slice_in_dim(pose_tokens, begin, begin + count)
        part = jnp.pad(part, ((0, 0), (0, 0), (0, padded - joints), (0, 0)))
        return with_layout_constraint(part, Layout(major_to_minor=(0, 1, 2, 3)))

    own = [padded_views(starts[c], sizes[c]) for c in chunks]
    near = lax.ppermute(padded_views(0, views_dev), "view", up)
    other, query, here, after = [], [], [], []
    for c in chunks:
        part = tied(own[c], *other[-1:], *here[:-1], *([near] if c == 2 else []))
        other.append(lax.ppermute(part, "joint", swap))
        q, kv = project(
            where, (own[c], other[c]), gain_attn, (w_query, w_key, w_value), joints
        )
        query.append(q)
        here.append(kv)
        after.append(lax.ppermute(kv, "view", down))
    before, far = [], []
    pieces = ((0, 1), (2,)) if len(sizes) == 3 else (tuple(chunks),)
    for index, piece in enumerate(pieces):
        begin, count = starts[piece[0]], sum(sizes[c] for c in piece)
        near_part = lax.slice_in_dim(near, begin, begin + count)
        other_part = jnp.concatenate([other[c] for c in piece], axis=0)
        far_part = tied(near_part, other[-1], *here[: index + 2], *after[: index + 1], *far)
        far.append(lax.ppermute(far_part, ("view", "joint"), swap_even))
        odd_part = tied(other_part, *here[: index + 2])
        far_odd = lax.ppermute(odd_part, ("view", "joint"), to_odd)
        (kv,) = project(where, (near_part, far[-1], far_odd), gain_attn, (w_key, w_value), joints)
        before.append(kv)
    window = before + here + after

    w_rows = w_out.shape[0] // 2
    w_part = lax.dynamic_slice_in_dim(w_out, lax.rem(place, 2) * w_rows, w_rows, 0)
    w_part, _ = lax.optimization_barrier((w_part, far[-1]))
    w_got = lax.ppermute(w_part, "joint", swap)
    w_shared = lax.ppermute(w_got, "view", to_other_core)

    first_view = place * views_dev
    own_slot = jnp.arange(views_dev, dtype=jnp.int32)[:, None] + views_dev
    slots = jnp.concatenate(
        (own_slot, jnp.mod(partners - first_view + views_dev, num_views)), axis=1
    )
    slots = jnp.clip(slots, 0, 3 * views_dev - 1)

    joint_ids = jnp.arange(padded, dtype=jnp.int32)
    line = jnp.concatenate((parents, jnp.full((padded - joints,), -1, jnp.int32)))
    skeleton = (
        (joint_ids[:, None] == joint_ids[None, :]).astype(F32)
        + (joint_ids[None, :] == line[:, None]).astype(F32)
        + (joint_ids[:, None] == line[None, :]).astype(F32)
    )
    degree = jnp.sum(skeleton, axis=1, keepdims=True)
    skeleton = skeleton.astype(BF16)
    held = (w_out, w_got, w_shared, gain_graph, skeleton, degree, w_graph)
    sent = []
    for c in chunks:
        for begin in range(0, sizes[c], tail):
            first = starts[c] + begin
            q = query[c]
            if sent:
                q = tied(q, sent[-1][0])
            theirs = attend(where, 2, slots, first, q, begin, tail, window, joints)
            q = tied(q, theirs)
            moved = lax.ppermute(theirs, "joint", swap)
            mine = attend(where, 0, slots, first, q, begin, tail, window, joints)
            sent.append(
                graph_part(packed, where, mine, moved, own[c], other[c], begin, held)
            )

    view_ids = jnp.arange(num_views, dtype=jnp.int32)
    counts = (view_ids[:, None] == view_ids[None, :]).astype(F32)
    counts = counts + jnp.sum(
        (view_links[:, :, None] == view_ids[None, None, :]).astype(F32), axis=1
    )
    share = 1.0 / (view_links.shape[1] + 1)
    if packed:
        parts = [
            lax.all_to_all(part, "view", split_axis=0, concat_axis=0, tiled=True)
            for (part,) in sent
        ]
        order = lax.rem(place, 2).reshape(1)
        result = mix(order, parts, counts.T.astype(BF16), joints, share)
        return jnp.transpose(result, (1, 0, 2))[None]

    hidden = jnp.concatenate([part[0] for part in sent], axis=0)[:, :joints]
    graph_term = jnp.concatenate([part[1] for part in sent], axis=0)[:, :joints]
    residual = jnp.transpose(hidden, (2, 1, 0))
    graph_term = jnp.transpose(graph_term, (2, 1, 0))
    residual = lax.all_to_all(residual, "view", split_axis=0, concat_axis=2, tiled=True)
    graph_term = lax.all_to_all(graph_term, "view", split_axis=0, concat_axis=2, tiled=True)
    mixed = jnp.einsum(
        "cjv,wv->cjw", graph_term, counts.astype(BF16), preferred_element_type=F32
    )
    return (residual.astype(F32) + mixed * share).astype(BF16)[None]


def solution(mesh):
    placed = (
        P("view", None, None, "joint"),
        P(),
        P(),
        P(None, "joint"),
        P(None, "joint"),
        P(None, "joint"),
        P("joint", None),
        P(),
        P("view", None),
        P(),
        P(),
    )
    return jax.shard_map(
        body, mesh=mesh, in_specs=placed, out_specs=P("joint", "view", None, None), check_vma=False
    )
```

```python
import functools

import jax
import jax.numpy as jnp
from jax import lax
from jax.experimental import pallas as pl
from jax.experimental.layout import Layout, with_layout_constraint
from jax.experimental.pallas import tpu as pltpu
from jax.sharding import PartitionSpec as P

HD = 64
LANES = 128
norm_eps = 1e-05
MIB = 1024 * 1024
VMEM_MIB = 32
F32 = jnp.float32
BF16 = jnp.bfloat16
LOG2E = 1.4426950408889634


def round_up(value, unit):
    return (value + unit - 1) // unit * unit


def layer_norm(values, gain):
    average = jnp.mean(values, axis=-1, keepdims=True)
    centred = values - average
    spread = jnp.mean(centred * centred, axis=-1, keepdims=True)
    return centred * lax.rsqrt(spread + norm_eps) * gain


def both_halves(joint, own, other):
    low = jnp.where(joint == 0, own, other)
    high = jnp.where(joint == 0, other, own)
    return jnp.concatenate([low, high], axis=1)


def params(limit_mib):
    return pltpu.CompilerParams(vmem_limit_bytes=limit_mib * MIB)


def cost(flops, bytes_accessed, transcendentals=0):
    return pl.CostEstimate(
        flops=int(flops), bytes_accessed=int(bytes_accessed), transcendentals=int(transcendentals)
    )


def project_kernel(with_query, joints, place_ref, *refs):
    count = 3 if with_query else 2
    halves = 2 if with_query else 3
    tokens, rest = refs[:halves], refs[halves:]
    gain_ref, weights, outs = rest[0], rest[1 : 1 + count], rest[1 + count :]
    views, frames, padded, _ = tokens[0].shape
    joint = place_ref[0]
    gain = gain_ref[...]
    row = lax.broadcasted_iota(jnp.int32, (padded, 1), 0)
    real = row < joints
    pieces = []
    for view in range(views):
        for frame in range(frames):
            own = tokens[0][view, frame].astype(F32)
            other = tokens[1][view, frame].astype(F32)
            if not with_query:
                other = jnp.where(place_ref[1] == 0, other, tokens[2][view, frame].astype(F32))
            normed = layer_norm(both_halves(joint, own, other), gain)
            pieces.append(jnp.where(real, normed, normed[0:1]))
    flat = jnp.concatenate(pieces, axis=0).astype(BF16)
    real = jnp.concatenate([real] * (views * frames), axis=0)
    rows = frames * padded
    width = weights[-1].shape[1]
    keys = jnp.dot(flat, weights[-2][...], preferred_element_type=F32).astype(BF16)
    values = jnp.dot(flat, weights[-1][...], preferred_element_type=F32)
    values = jnp.where(real, values, 0.0).astype(BF16)
    for view in range(views):
        part = slice(view * rows, (view + 1) * rows)
        for pair in range(width // LANES):
            columns = slice(pair * LANES, (pair + 1) * LANES)
            outs[-1][view, pair, :, :LANES] = keys[part, columns]
            outs[-1][view, pair, :, LANES:] = values[part, columns]
    if with_query:
        query = jnp.dot(flat, weights[0][...], preferred_element_type=F32)
        for view in range(views):
            for frame in range(frames):
                at = (view * frames + frame) * padded
                outs[0][view, frame] = query[at : at + padded].astype(BF16)


def project(place, tokens, begins, views, gain, weights, joints):
    _, frames, padded, half = tokens[0].shape
    model, width = weights[0].shape
    rows = frames * padded
    with_query = len(weights) == 3
    step = 2 if views % 2 == 0 else 1
    pairs = width // LANES
    out_shape = [pltpu.HBM((views, pairs, rows, 2 * LANES), BF16)]
    out_specs = [pl.BlockSpec((step, pairs, rows, 2 * LANES), lambda i, s: (i, 0, 0, 0))]
    if with_query:
        out_shape = [pltpu.HBM((views, frames, padded, width), BF16)] + out_shape
        out_specs = [
            pl.BlockSpec((step, frames, padded, width), lambda i, s: (i, 0, 0, 0))
        ] + out_specs

    def token(begin):
        return pl.BlockSpec(
            (step, frames, padded, half), lambda i, s: (begin // step + i, 0, 0, 0)
        )

    weight = pl.BlockSpec((model, width), lambda i, s: (0, 0))
    return pl.pallas_call(
        functools.partial(project_kernel, with_query, joints),
        grid_spec=pltpu.PrefetchScalarGridSpec(
            num_scalar_prefetch=1,
            grid=(views // step,),
            in_specs=[token(begin) for begin in begins]
            + [pl.BlockSpec((1, model), lambda i, s: (0, 0))]
            + [weight] * len(weights),
            out_specs=out_specs,
        ),
        out_shape=out_shape,
        compiler_params=params(VMEM_MIB),
        cost_estimate=cost(
            2 * views * rows * model * len(weights) * width,
            2 * (views * rows * (model + len(weights) * width) + len(weights) * model * width),
        ),
        name="project",
    )(place, *tokens, gain, *weights)


def attend_kernel(first, joints, place_ref, slot_ref, q_ref, *rest):
    sources = rest[:-4]
    out_ref, keyval, ones_ref, sems = rest[-4:]
    _, _, padded, width = q_ref.shape
    blocks = slot_ref.shape[1]
    rows = keyval.shape[2] // blocks
    pairs = width // LANES
    group = pairs // 2
    step = pl.program_id(0)
    steps = pl.num_programs(0)

    def copy(source, slot, part, block, buffer):
        taken = pl.ds(part * group, group)
        return pltpu.make_async_copy(
            source.at[slot, taken],
            keyval.at[buffer, taken, pl.ds(block * rows, rows)],
            sems.at[buffer, block, part],
        )

    def fetch(view, buffer, parts):
        for block in range(blocks):
            slot = slot_ref[first + view, block]
            begin = 0
            for source in sources:
                low, begin = begin, begin + source.shape[0]

                @pl.when((slot >= low) & (slot < begin))
                def _():
                    for part in parts:
                        copy(source, slot - low, part, block, buffer).start()

    buffer = lax.rem(step, 2)

    @pl.when(step == 0)
    def _():
        fetch(0, 0, (0,))
        fetch(0, 0, (1,))
        row = lax.broadcasted_iota(jnp.int32, (padded, LANES), 0)
        real = jnp.where(row < joints, 1.0, 0.0)
        ones_ref[...] = jnp.concatenate([real] * (blocks * rows // padded), axis=0).astype(BF16)

    @pl.when(step + 1 < steps)
    def _():
        fetch(step + 1, 1 - buffer, (0, 1))

    left = lax.broadcasted_iota(jnp.int32, (1, LANES), 1) < HD
    ones = ones_ref[...]
    scale = HD**-0.5 * LOG2E
    for pair in range(pairs):
        if pair % group == 0:
            for block in range(blocks):
                copy(sources[0], 0, pair // group, block, buffer).wait()
        columns = slice(pair * LANES, (pair + 1) * LANES)
        query = q_ref[0, 0, :, columns].astype(F32)
        stacked = jnp.concatenate(
            [jnp.where(left, query, 0.0), jnp.where(left, 0.0, query)], axis=0
        ).astype(BF16)
        values = jnp.concatenate(
            [keyval[buffer, pair, :, LANES:], ones], axis=1
        )
        scores = lax.dot_general(
            stacked,
            keyval[buffer, pair, :, :LANES],
            (((1,), (1,)), ((), ())),
            preferred_element_type=F32,
        )
        top = jnp.max(scores, axis=1, keepdims=True)
        powers = jnp.exp2((scores - top) * scale).astype(BF16)
        found = jnp.dot(powers, values, preferred_element_type=F32)
        total = jnp.where(left, found[:padded, :LANES], found[padded:, :LANES])
        weight = jnp.where(left, found[:padded, LANES:], found[padded:, LANES:])
        out_ref[0, :, columns] = (total / weight).astype(BF16)


def attend(place, frame, slots, first, query, begin, views, sources, joints):
    _, _, padded, width = query.shape
    _, pairs, rows, _ = sources[0].shape
    blocks = slots.shape[1]
    heads = width // HD
    return pl.pallas_call(
        functools.partial(attend_kernel, first, joints),
        grid_spec=pltpu.PrefetchScalarGridSpec(
            num_scalar_prefetch=2,
            grid=(views,),
            in_specs=[
                pl.BlockSpec((1, 1, padded, width), lambda i, p, s: (begin + i, p[frame], 0, 0))
            ]
            + [pl.BlockSpec(memory_space=pltpu.HBM)] * len(sources),
            out_specs=pl.BlockSpec((1, padded, width), lambda i, p, s: (i, 0, 0)),
            scratch_shapes=[
                pltpu.VMEM((2, pairs, blocks * rows, 2 * LANES), BF16),
                pltpu.VMEM((blocks * rows, LANES), BF16),
                pltpu.SemaphoreType.DMA((2, blocks, 2)),
            ],
        ),
        out_shape=pltpu.HBM((views, padded, width), BF16),
        compiler_params=params(VMEM_MIB),
        cost_estimate=cost(
            2 * 2 * views * heads * padded * blocks * rows * 256,
            2 * views * padded * width * 2 + 2 * views * blocks * rows * 2 * width,
            views * heads * padded * blocks * rows,
        ),
        name="attend",
    )(place, slots, query, *sources)


def graph_kernel(packed, place_ref, *refs):
    mine_ref, theirs_ref, own_ref, other_ref, w_mine_ref, w_got_ref, w_shared_ref = refs[:7]
    gain_ref, skeleton_ref, degree_ref, w_graph_ref, *outs = refs[7:]
    views, padded, width = mine_ref.shape
    joint, core = place_ref[0], place_ref[1]
    model = w_graph_ref.shape[0]
    gain = gain_ref[...]

    def rows_of(ref):
        pieces = [ref[view].astype(F32) for view in range(views)]
        return jnp.concatenate(pieces, axis=0).astype(BF16)

    mine, theirs = rows_of(mine_ref), rows_of(theirs_ref)
    w_low = jnp.where(core == 0, w_got_ref[...], w_shared_ref[...])
    w_high = jnp.where(core == 0, w_shared_ref[...], w_got_ref[...])
    projected = (
        jnp.dot(mine, w_mine_ref[...], preferred_element_type=F32)
        + jnp.dot(theirs[:, : width // 2], w_low, preferred_element_type=F32)
        + jnp.dot(theirs[:, width // 2 :], w_high, preferred_element_type=F32)
    )
    hiddens, mixed = [], []
    for view in range(views):
        own, other = own_ref[view, 0].astype(F32), other_ref[view, 0].astype(F32)
        part = projected[view * padded : (view + 1) * padded]
        hidden = (both_halves(joint, own, other) + part).astype(BF16).astype(F32)
        normed = layer_norm(hidden, gain).astype(BF16)
        summed = jnp.dot(skeleton_ref[...], normed, preferred_element_type=F32)
        hiddens.append(hidden)
        mixed.append(summed / degree_ref[...])
    skeletal = jnp.concatenate(mixed, axis=0).astype(BF16)
    graph = jnp.dot(skeletal, w_graph_ref[...], preferred_element_type=F32)
    first = lax.broadcasted_iota(jnp.int32, (1, LANES), 1) < LANES // 2
    for view in range(views):
        term = graph[view * padded : (view + 1) * padded]
        if not packed:
            outs[0][view] = hiddens[view].astype(BF16)
            outs[1][view] = term.astype(BF16)
            continue
        for tile in range(model // LANES):
            columns = slice(tile * LANES, (tile + 1) * LANES)
            kept = hiddens[view][:, columns]
            turned = pltpu.roll(term[:, columns], LANES // 2, axis=1)
            outs[0][2 * tile, view] = jnp.where(first, kept, turned).astype(BF16)
            outs[0][2 * tile + 1, view] = jnp.where(first, turned, kept).astype(BF16)


def graph_part(packed, place, mine, theirs, own, own_begin, other, other_begin, held):
    views, padded, width = mine.shape
    half = own.shape[3]
    model = held[-1].shape[0]
    heads = pl.BlockSpec((views, padded, width), lambda i, j: (0, 0, 0))

    def token(begin):
        return pl.BlockSpec(
            (views, 1, padded, half), lambda i, j: (begin // views, j[0], 0, 0)
        )

    if packed:
        devices = 2 * model // LANES
        out_shape = [pltpu.HBM((devices, views, padded, LANES), BF16)]
        out_specs = [pl.BlockSpec((devices, views, padded, LANES), lambda i, j: (0, 0, 0, 0))]
    else:
        out_shape = [jax.ShapeDtypeStruct((views, padded, model), BF16)] * 2
        out_specs = [pl.BlockSpec((views, padded, model), lambda i, j: (0, 0, 0))] * 2
    return pl.pallas_call(
        functools.partial(graph_kernel, packed),
        grid_spec=pltpu.PrefetchScalarGridSpec(
            num_scalar_prefetch=1,
            grid=(1,),
            in_specs=[heads, heads, token(own_begin), token(other_begin)]
            + [pl.BlockSpec(a.shape, lambda i, j: (0, 0)) for a in held],
            out_specs=out_specs,
        ),
        out_shape=out_shape,
        compiler_params=params(VMEM_MIB),
        cost_estimate=cost(
            4 * views * padded * model * model, 2 * (views * padded * model * 4 + 2 * model * model)
        ),
        name="graph_part",
    )(place, mine, theirs, own, other, *held)


def mix_kernel(share, devices, order_ref, *rest):
    parts, (counts_ref, out_ref, wide) = rest[:-3], rest[-3:]
    views = wide.shape[0] // out_ref.shape[0]
    rows, channels, _ = out_ref.shape
    views_dev = views // devices
    first = 0
    for part in parts:
        chunk = part.shape[0] // devices
        for device in range(devices):
            at = (device * views_dev + first) * rows
            block = part[device * chunk : (device + 1) * chunk].astype(F32)
            wide[at : at + chunk * rows] = block.reshape(chunk * rows, LANES)
        first += chunk
    counts = counts_ref[...]
    flipped = order_ref[0] == 1
    for row in range(rows):
        lanes_first = wide[pl.ds(row, views, stride=rows), :].T
        low, high = lanes_first[:channels], lanes_first[channels:]
        term = jnp.where(flipped, low, high).astype(BF16)
        kept = jnp.where(flipped, high, low)
        mixed = jnp.dot(term, counts, preferred_element_type=F32)
        out_ref[row] = (kept + mixed * share).astype(BF16)


def mix(order, parts, counts, joints, share):
    views = counts.shape[0]
    devices = parts[0].shape[0]
    parts = [part.reshape(-1, *part.shape[2:]) for part in parts]
    padded = parts[0].shape[1]
    channels = LANES // 2
    rows = 16
    return pl.pallas_call(
        functools.partial(mix_kernel, share, devices),
        grid_spec=pltpu.PrefetchScalarGridSpec(
            num_scalar_prefetch=1,
            grid=(pl.cdiv(joints, rows),),
            in_specs=[
                pl.BlockSpec((part.shape[0], rows, LANES), lambda i, s: (0, i, 0))
                for part in parts
            ]
            + [pl.BlockSpec(counts.shape, lambda i, s: (0, 0))],
            out_specs=pl.BlockSpec((rows, channels, views), lambda i, s: (i, 0, 0)),
            scratch_shapes=[pltpu.VMEM((views * rows, LANES), F32)],
        ),
        out_shape=jax.ShapeDtypeStruct((joints, channels, views), BF16),
        compiler_params=params(VMEM_MIB),
        cost_estimate=cost(
            2 * padded * LANES * views * views, 2 * padded * views * (LANES + channels)
        ),
        name="mix",
    )(order, *parts, counts)


def body(
    pose_tokens,
    gain_attn,
    gain_graph,
    w_query,
    w_key,
    w_value,
    w_out,
    w_graph,
    partners,
    parents,
    view_links,
):
    views_dev, frames, joints, half_width = pose_tokens.shape
    model = w_graph.shape[0]
    devices = lax.axis_size("view")
    place = lax.axis_index("view").astype(jnp.int32)
    joint_place = lax.axis_index("joint").astype(jnp.int32)
    num_views = devices * views_dev
    channels = model // devices
    padded = round_up(joints, 8)
    rows = frames * padded
    sizes = (2, 2, 4) if views_dev == 8 else (views_dev,)
    tail = 2 if views_dev == 8 else views_dev
    starts = [sum(sizes[:c]) for c in range(len(sizes))]
    chunks = range(len(sizes))
    packed = 2 * channels == LANES and num_views == LANES
    swap = [(0, 1), (1, 0)]
    up = [(i, (i + 1) % devices) for i in range(devices)]
    down = [(j, i) for i, j in up]
    swap_even = [(2 * v + j, 2 * v + 1 - j) for v in range(0, devices, 2) for j in (0, 1)]
    to_odd = [(2 * v + j, 2 * v + 2 + j) for v in range(0, devices, 2) for j in (0, 1)]
    gain_attn = gain_attn.reshape(1, model)
    gain_graph = gain_graph.reshape(1, model)
    where = jnp.stack((joint_place, lax.rem(place, 2), 1 - joint_place))

    to_other_core = [(v, v ^ 1) for v in range(devices)]

    def tied(array, *others):
        return lax.optimization_barrier((array, *others))[0]

    own = jnp.pad(pose_tokens, ((0, 0), (0, 0), (0, padded - joints), (0, 0)))
    own = with_layout_constraint(own, Layout(major_to_minor=(0, 1, 2, 3)))
    own = lax.optimization_barrier(own)
    near = lax.ppermute(own, "view", up)

    other, query, here, after = [], [], [], []
    for c in chunks:
        part = lax.slice_in_dim(own, starts[c], starts[c] + sizes[c])
        if c == 2:
            part = tied(part, other[0], near)
        other.append(lax.ppermute(part, "joint", swap))
    for c in chunks:
        q, kv = project(
            where,
            (own, other[c]),
            (starts[c], 0),
            sizes[c],
            gain_attn,
            (w_query, w_key, w_value),
            joints,
        )
        query.append(q)
        here.append(kv)
        after.append(lax.ppermute(kv, "view", down))
    before = []
    pieces = ((0, 1), (2,)) if len(sizes) == 3 else (tuple(chunks),)
    for piece in pieces:
        begin, count = starts[piece[0]], sum(sizes[c] for c in piece)
        near_part = lax.slice_in_dim(near, begin, begin + count)
        far = lax.ppermute(
            tied(near_part, other[-1], here[0], after[0]), ("view", "joint"), swap_even
        )
        other_part = jnp.concatenate([other[c] for c in piece], axis=0)
        far_odd = lax.ppermute(tied(other_part, here[0]), ("view", "joint"), to_odd)
        (kv,) = project(
            where,
            (near, far, far_odd),
            (begin, 0, 0),
            count,
            gain_attn,
            (w_key, w_value),
            joints,
        )
        before.append(kv)
    window = before + here + after

    w_rows = w_out.shape[0] // 2
    w_part = lax.dynamic_slice_in_dim(w_out, lax.rem(place, 2) * w_rows, w_rows, 0)
    w_part = tied(w_part, far)
    w_got = lax.ppermute(w_part, "joint", swap)
    w_shared = lax.ppermute(w_got, "view", to_other_core)

    first_view = place * views_dev
    own_slot = jnp.arange(views_dev, dtype=jnp.int32)[:, None] + views_dev
    slots = jnp.concatenate(
        (own_slot, jnp.mod(partners - first_view + views_dev, num_views)), axis=1
    )
    slots = jnp.clip(slots, 0, 3 * views_dev - 1)

    joint_ids = jnp.arange(padded, dtype=jnp.int32)
    line = jnp.concatenate((parents, jnp.full((padded - joints,), -1, jnp.int32)))
    skeleton = (
        (joint_ids[:, None] == joint_ids[None, :]).astype(F32)
        + (joint_ids[None, :] == line[:, None]).astype(F32)
        + (joint_ids[:, None] == line[None, :]).astype(F32)
    )
    degree = jnp.sum(skeleton, axis=1, keepdims=True)
    skeleton = skeleton.astype(BF16)
    held = (w_out, w_got, w_shared, gain_graph, skeleton, degree, w_graph)
    sent = []
    for c in chunks:
        for begin in range(0, sizes[c], tail):
            first = starts[c] + begin
            q = query[c]
            if sent:
                q = tied(q, sent[-1][0])
            theirs = attend(where, 2, slots, first, q, begin, tail, window, joints)
            q = tied(q, theirs)
            moved = lax.ppermute(theirs, "joint", swap)
            mine = attend(where, 0, slots, first, q, begin, tail, window, joints)
            sent.append(
                graph_part(packed, where, mine, moved, own, first, other[c], begin, held)
            )

    view_ids = jnp.arange(num_views, dtype=jnp.int32)
    counts = (view_ids[:, None] == view_ids[None, :]).astype(F32)
    counts = counts + jnp.sum(
        (view_links[:, :, None] == view_ids[None, None, :]).astype(F32), axis=1
    )
    share = 1.0 / (view_links.shape[1] + 1)
    if packed:
        parts = [
            lax.all_to_all(part, "view", split_axis=0, concat_axis=0, tiled=True)
            for (part,) in sent
        ]
        order = lax.rem(place, 2).reshape(1)
        result = mix(order, parts, counts.T.astype(BF16), joints, share)
        return jnp.transpose(result, (1, 0, 2))[None]

    hidden = jnp.concatenate([part[0] for part in sent], axis=0)[:, :joints]
    graph_term = jnp.concatenate([part[1] for part in sent], axis=0)[:, :joints]
    residual = jnp.transpose(hidden, (2, 1, 0))
    graph_term = jnp.transpose(graph_term, (2, 1, 0))
    residual = lax.all_to_all(residual, "view", split_axis=0, concat_axis=2, tiled=True)
    graph_term = lax.all_to_all(graph_term, "view", split_axis=0, concat_axis=2, tiled=True)
    mixed = jnp.einsum(
        "cjv,wv->cjw", graph_term, counts.astype(BF16), preferred_element_type=F32
    )
    return (residual.astype(F32) + mixed * share).astype(BF16)[None]


def solution(mesh):
    placed = (
        P("view", None, None, "joint"),
        P(),
        P(),
        P(None, "joint"),
        P(None, "joint"),
        P(None, "joint"),
        P("joint", None),
        P(),
        P("view", None),
        P(),
        P(),
    )
    return jax.shard_map(
        body, mesh=mesh, in_specs=placed, out_specs=P("joint", "view", None, None), check_vma=False
    )
```

```python
import functools

import jax
import jax.numpy as jnp
from jax import lax
from jax.experimental import pallas as pl
from jax.experimental.layout import Layout, with_layout_constraint
from jax.experimental.pallas import tpu as pltpu
from jax.sharding import PartitionSpec as P

HD = 64
LANES = 128
norm_eps = 1e-05
MIB = 1024 * 1024
VMEM_MIB = 32
ATTEND_MIB = 60
F32 = jnp.float32
BF16 = jnp.bfloat16
LOG2E = 1.4426950408889634


def round_up(value, unit):
    return (value + unit - 1) // unit * unit


def layer_norm(values, gain):
    average = jnp.mean(values, axis=-1, keepdims=True)
    centred = values - average
    spread = jnp.mean(centred * centred, axis=-1, keepdims=True)
    return centred * lax.rsqrt(spread + norm_eps) * gain


def both_halves(joint, own, other):
    low = jnp.where(joint == 0, own, other)
    high = jnp.where(joint == 0, other, own)
    return jnp.concatenate([low, high], axis=1)


def params(limit_mib):
    return pltpu.CompilerParams(vmem_limit_bytes=limit_mib * MIB)


def cost(flops, bytes_accessed, transcendentals=0):
    return pl.CostEstimate(
        flops=int(flops), bytes_accessed=int(bytes_accessed), transcendentals=int(transcendentals)
    )


def project_kernel(with_query, joints, place_ref, *refs):
    count = 3 if with_query else 2
    halves = 2 if with_query else 3
    tokens, rest = refs[:halves], refs[halves:]
    gain_ref, weights, outs = rest[0], rest[1 : 1 + count], rest[1 + count :]
    views, frames, padded, _ = tokens[0].shape
    joint = place_ref[0]
    gain = gain_ref[...]
    row = lax.broadcasted_iota(jnp.int32, (padded, 1), 0)
    real = row < joints
    pieces = []
    for view in range(views):
        for frame in range(frames):
            own = tokens[0][view, frame].astype(F32)
            other = tokens[1][view, frame].astype(F32)
            if not with_query:
                other = jnp.where(place_ref[1] == 0, other, tokens[2][view, frame].astype(F32))
            normed = layer_norm(both_halves(joint, own, other), gain)
            pieces.append(jnp.where(real, normed, normed[0:1]))
    flat = jnp.concatenate(pieces, axis=0).astype(BF16)
    real = jnp.concatenate([real] * (views * frames), axis=0)
    rows = frames * padded
    width = weights[-1].shape[1]
    keys = jnp.dot(flat, weights[-2][...], preferred_element_type=F32).astype(BF16)
    values = jnp.dot(flat, weights[-1][...], preferred_element_type=F32)
    values = jnp.where(real, values, 0.0).astype(BF16)
    for view in range(views):
        part = slice(view * rows, (view + 1) * rows)
        for pair in range(width // LANES):
            columns = slice(pair * LANES, (pair + 1) * LANES)
            outs[-1][view, pair, :, :LANES] = keys[part, columns]
            outs[-1][view, pair, :, LANES:] = values[part, columns]
    if with_query:
        query = jnp.dot(flat, weights[0][...], preferred_element_type=F32)
        for view in range(views):
            for frame in range(frames):
                at = (view * frames + frame) * padded
                outs[0][view, frame] = query[at : at + padded].astype(BF16)


def project(place, tokens, gain, weights, joints):
    views, frames, padded, half = tokens[0].shape
    model, width = weights[0].shape
    rows = frames * padded
    with_query = len(weights) == 3
    step = 2 if views % 2 == 0 else 1
    pairs = width // LANES
    out_shape = [pltpu.HBM((views, pairs, rows, 2 * LANES), BF16)]
    out_specs = [pl.BlockSpec((step, pairs, rows, 2 * LANES), lambda i, s: (i, 0, 0, 0))]
    if with_query:
        out_shape = [pltpu.HBM((views, frames, padded, width), BF16)] + out_shape
        out_specs = [
            pl.BlockSpec((step, frames, padded, width), lambda i, s: (i, 0, 0, 0))
        ] + out_specs
    token = pl.BlockSpec((step, frames, padded, half), lambda i, s: (i, 0, 0, 0))
    weight = pl.BlockSpec((model, width), lambda i, s: (0, 0))
    return pl.pallas_call(
        functools.partial(project_kernel, with_query, joints),
        grid_spec=pltpu.PrefetchScalarGridSpec(
            num_scalar_prefetch=1,
            grid=(views // step,),
            in_specs=[token] * len(tokens)
            + [pl.BlockSpec((1, model), lambda i, s: (0, 0))]
            + [weight] * len(weights),
            out_specs=out_specs,
        ),
        out_shape=out_shape,
        compiler_params=params(VMEM_MIB),
        cost_estimate=cost(
            2 * views * rows * model * len(weights) * width,
            2 * (views * rows * (model + len(weights) * width) + len(weights) * model * width),
        ),
        name="project",
    )(place, *tokens, gain, *weights)


def attend_kernel(first, joints, place_ref, slot_ref, q_ref, *rest):
    sources = rest[:-4]
    out_ref, keyval, ones_ref, sems = rest[-4:]
    _, _, padded, width = q_ref.shape
    blocks = slot_ref.shape[1]
    rows = keyval.shape[2] // blocks
    pairs = width // LANES
    group = pairs // 2
    step = pl.program_id(0)
    steps = pl.num_programs(0)

    def copy(source, slot, part, block, buffer):
        taken = pl.ds(part * group, group)
        return pltpu.make_async_copy(
            source.at[slot, taken],
            keyval.at[buffer, taken, pl.ds(block * rows, rows)],
            sems.at[buffer, block, part],
        )

    def fetch(view, buffer, parts):
        for block in range(blocks):
            slot = slot_ref[first + view, block]
            begin = 0
            for source in sources:
                low, begin = begin, begin + source.shape[0]

                @pl.when((slot >= low) & (slot < begin))
                def _():
                    for part in parts:
                        copy(source, slot - low, part, block, buffer).start()

    buffer = lax.rem(step, 2)

    @pl.when(step == 0)
    def _():
        fetch(0, 0, (0,))
        fetch(0, 0, (1,))
        row = lax.broadcasted_iota(jnp.int32, (padded, LANES), 0)
        real = jnp.where(row < joints, 1.0, 0.0)
        ones_ref[...] = jnp.concatenate([real] * (blocks * rows // padded), axis=0).astype(BF16)

    @pl.when(step + 1 < steps)
    def _():
        fetch(step + 1, 1 - buffer, (0, 1))

    left = lax.broadcasted_iota(jnp.int32, (1, LANES), 1) < HD
    ones = ones_ref[...]
    scale = HD**-0.5 * LOG2E
    for pair in range(pairs):
        if pair % group == 0:
            for block in range(blocks):
                copy(sources[0], 0, pair // group, block, buffer).wait()
        columns = slice(pair * LANES, (pair + 1) * LANES)
        query = q_ref[0, 0, :, columns].astype(F32)
        stacked = jnp.concatenate(
            [jnp.where(left, query, 0.0), jnp.where(left, 0.0, query)], axis=0
        ).astype(BF16)
        values = jnp.concatenate(
            [keyval[buffer, pair, :, LANES:], ones], axis=1
        )
        scores = lax.dot_general(
            stacked,
            keyval[buffer, pair, :, :LANES],
            (((1,), (1,)), ((), ())),
            preferred_element_type=F32,
        )
        top = jnp.max(scores, axis=1, keepdims=True)
        powers = jnp.exp2((scores - top) * scale).astype(BF16)
        found = jnp.dot(powers, values, preferred_element_type=F32)
        total = jnp.where(left, found[:padded, :LANES], found[padded:, :LANES])
        weight = jnp.where(left, found[:padded, LANES:], found[padded:, LANES:])
        out_ref[0, :, columns] = (total / weight).astype(BF16)


def attend(place, frame, slots, first, query, sources, joints):
    views, _, padded, width = query.shape
    _, pairs, rows, _ = sources[0].shape
    blocks = slots.shape[1]
    heads = width // HD
    return pl.pallas_call(
        functools.partial(attend_kernel, first, joints),
        grid_spec=pltpu.PrefetchScalarGridSpec(
            num_scalar_prefetch=2,
            grid=(views,),
            in_specs=[
                pl.BlockSpec((1, 1, padded, width), lambda i, p, s: (i, p[frame], 0, 0))
            ]
            + [pl.BlockSpec(memory_space=pltpu.HBM)] * len(sources),
            out_specs=pl.BlockSpec((1, padded, width), lambda i, p, s: (i, 0, 0)),
            scratch_shapes=[
                pltpu.VMEM((2, pairs, blocks * rows, 2 * LANES), BF16),
                pltpu.VMEM((blocks * rows, LANES), BF16),
                pltpu.SemaphoreType.DMA((2, blocks, 2)),
            ],
        ),
        out_shape=pltpu.HBM((views, padded, width), BF16),
        compiler_params=params(ATTEND_MIB),
        cost_estimate=cost(
            2 * 2 * views * heads * padded * blocks * rows * 256,
            2 * views * padded * width * 2 + 2 * views * blocks * rows * 2 * width,
            views * heads * padded * blocks * rows,
        ),
        name="attend",
    )(place, slots, query, *sources)


def graph_kernel(packed, place_ref, *refs):
    mine_ref, theirs_ref, own_ref, other_ref, w_mine_ref, w_got_ref, w_shared_ref = refs[:7]
    gain_ref, skeleton_ref, degree_ref, w_graph_ref, *outs = refs[7:]
    views, padded, width = mine_ref.shape
    joint, core = place_ref[0], place_ref[1]
    model = w_graph_ref.shape[0]
    gain = gain_ref[...]

    def rows_of(ref):
        pieces = [ref[view].astype(F32) for view in range(views)]
        return jnp.concatenate(pieces, axis=0).astype(BF16)

    mine, theirs = rows_of(mine_ref), rows_of(theirs_ref)
    w_low = jnp.where(core == 0, w_got_ref[...], w_shared_ref[...])
    w_high = jnp.where(core == 0, w_shared_ref[...], w_got_ref[...])
    projected = (
        jnp.dot(mine, w_mine_ref[...], preferred_element_type=F32)
        + jnp.dot(theirs[:, : width // 2], w_low, preferred_element_type=F32)
        + jnp.dot(theirs[:, width // 2 :], w_high, preferred_element_type=F32)
    )
    hiddens, mixed = [], []
    for view in range(views):
        own, other = own_ref[view, 0].astype(F32), other_ref[view, 0].astype(F32)
        part = projected[view * padded : (view + 1) * padded]
        hidden = (both_halves(joint, own, other) + part).astype(BF16).astype(F32)
        normed = layer_norm(hidden, gain).astype(BF16)
        summed = jnp.dot(skeleton_ref[...], normed, preferred_element_type=F32)
        hiddens.append(hidden)
        mixed.append(summed / degree_ref[...])
    skeletal = jnp.concatenate(mixed, axis=0).astype(BF16)
    graph = jnp.dot(skeletal, w_graph_ref[...], preferred_element_type=F32)
    first = lax.broadcasted_iota(jnp.int32, (1, LANES), 1) < LANES // 2
    for view in range(views):
        term = graph[view * padded : (view + 1) * padded]
        if not packed:
            outs[0][view] = hiddens[view].astype(BF16)
            outs[1][view] = term.astype(BF16)
            continue
        for tile in range(model // LANES):
            columns = slice(tile * LANES, (tile + 1) * LANES)
            kept = hiddens[view][:, columns]
            turned = pltpu.roll(term[:, columns], LANES // 2, axis=1)
            outs[0][2 * tile, view] = jnp.where(first, kept, turned).astype(BF16)
            outs[0][2 * tile + 1, view] = jnp.where(first, turned, kept).astype(BF16)


def graph_part(packed, place, mine, theirs, own, other, held):
    views, padded, width = mine.shape
    half = own.shape[3]
    model = held[-1].shape[0]
    heads = pl.BlockSpec((views, padded, width), lambda i, j: (0, 0, 0))
    token = pl.BlockSpec((views, 1, padded, half), lambda i, j: (0, j[0], 0, 0))
    if packed:
        devices = 2 * model // LANES
        out_shape = [pltpu.HBM((devices, views, padded, LANES), BF16)]
        out_specs = [pl.BlockSpec((devices, views, padded, LANES), lambda i, j: (0, 0, 0, 0))]
    else:
        out_shape = [jax.ShapeDtypeStruct((views, padded, model), BF16)] * 2
        out_specs = [pl.BlockSpec((views, padded, model), lambda i, j: (0, 0, 0))] * 2
    return pl.pallas_call(
        functools.partial(graph_kernel, packed),
        grid_spec=pltpu.PrefetchScalarGridSpec(
            num_scalar_prefetch=1,
            grid=(1,),
            in_specs=[heads, heads, token, token]
            + [pl.BlockSpec(a.shape, lambda i, j: (0, 0)) for a in held],
            out_specs=out_specs,
        ),
        out_shape=out_shape,
        compiler_params=params(VMEM_MIB),
        cost_estimate=cost(
            4 * views * padded * model * model, 2 * (views * padded * model * 4 + 2 * model * model)
        ),
        name="graph_part",
    )(place, mine, theirs, own, other, *held)


def mix_kernel(share, order_ref, part_ref, counts_ref, kept_ref, *rest):
    earlier, (out_ref, wide) = rest[:-2], rest[-2:]
    views, rows, _ = part_ref.shape
    channels = out_ref.shape[1]
    wide[...] = part_ref[...].astype(F32).reshape(views * rows, LANES)
    counts, keeper = counts_ref[...], kept_ref[...]
    flipped = order_ref[0] == 1
    for row in range(rows):
        lanes_first = wide[pl.ds(row, views, stride=rows), :].T
        low, high = lanes_first[:channels], lanes_first[channels:]
        term = jnp.where(flipped, low, high).astype(BF16)
        kept = jnp.where(flipped, high, low).astype(BF16)
        total = jnp.dot(kept, keeper, preferred_element_type=F32)
        total = total + jnp.dot(term, counts, preferred_element_type=F32) * share
        if earlier:
            total = total + earlier[0][row]
        out_ref[row] = total.astype(out_ref.dtype)


def mix(order, part, counts, keeper, earlier, last, joints, share):
    part = part.reshape(-1, *part.shape[2:])
    views, padded, _ = part.shape
    num_views = counts.shape[1]
    channels = LANES // 2
    rows = 16
    block = pl.BlockSpec((rows, channels, num_views), lambda i, s: (i, 0, 0))
    held = pl.BlockSpec(counts.shape, lambda i, s: (0, 0))
    return pl.pallas_call(
        functools.partial(mix_kernel, share),
        grid_spec=pltpu.PrefetchScalarGridSpec(
            num_scalar_prefetch=1,
            grid=(pl.cdiv(joints, rows),),
            in_specs=[pl.BlockSpec((views, rows, LANES), lambda i, s: (0, i, 0)), held, held]
            + [block] * len(earlier),
            out_specs=block,
            scratch_shapes=[pltpu.VMEM((views * rows, LANES), F32)],
        ),
        out_shape=jax.ShapeDtypeStruct((joints, channels, num_views), BF16 if last else F32),
        compiler_params=params(VMEM_MIB),
        cost_estimate=cost(
            4 * padded * LANES * views * num_views,
            2 * padded * (views * LANES + 3 * channels * num_views),
        ),
        name="mix",
    )(order, part, counts, keeper, *earlier)


def body(
    pose_tokens,
    gain_attn,
    gain_graph,
    w_query,
    w_key,
    w_value,
    w_out,
    w_graph,
    partners,
    parents,
    view_links,
):
    views_dev, frames, joints, half_width = pose_tokens.shape
    model = w_graph.shape[0]
    devices = lax.axis_size("view")
    place = lax.axis_index("view").astype(jnp.int32)
    joint_place = lax.axis_index("joint").astype(jnp.int32)
    num_views = devices * views_dev
    channels = model // devices
    padded = round_up(joints, 8)
    rows = frames * padded
    chunks = range(2 if views_dev % 4 == 0 else 1)
    chunk = views_dev // len(chunks)
    packed = 2 * channels == LANES and num_views == LANES
    swap = [(0, 1), (1, 0)]
    up = [(i, (i + 1) % devices) for i in range(devices)]
    down = [(j, i) for i, j in up]
    swap_even = [(2 * v + j, 2 * v + 1 - j) for v in range(0, devices, 2) for j in (0, 1)]
    to_odd = [(2 * v + j, 2 * v + 2 + j) for v in range(0, devices, 2) for j in (0, 1)]
    gain_attn = gain_attn.reshape(1, model)
    gain_graph = gain_graph.reshape(1, model)
    where = jnp.stack((joint_place, lax.rem(place, 2), 1 - joint_place))

    to_other_core = [(v, v ^ 1) for v in range(devices)]

    def tied(array, *others):
        return lax.optimization_barrier((array, *others))[0]

    own = []
    for c in chunks:
        part = lax.slice_in_dim(pose_tokens, c * chunk, (c + 1) * chunk)
        part = jnp.pad(part, ((0, 0), (0, 0), (0, padded - joints), (0, 0)))
        own.append(with_layout_constraint(part, Layout(major_to_minor=(0, 1, 2, 3))))

    near = [lax.ppermute(part, "view", up) for part in own]
    other, query, here, after = [], [], [], []
    for c in chunks:
        part = tied(own[c], *other, *(near if other else []))
        other.append(lax.ppermute(part, "joint", swap))
        q, kv = project(
            where, (own[c], other[c]), gain_attn, (w_query, w_key, w_value), joints
        )
        query.append(q)
        here.append(kv)
        after.append(lax.ppermute(kv, "view", down))
    before = []
    for c in chunks:
        far = lax.ppermute(
            tied(near[c], other[-1], here[0], after[0]), ("view", "joint"), swap_even
        )
        far_odd = lax.ppermute(tied(other[c], here[0]), ("view", "joint"), to_odd)
        (kv,) = project(where, (near[c], far, far_odd), gain_attn, (w_key, w_value), joints)
        before.append(kv)
    window = before + here + after

    w_rows = w_out.shape[0] // 2
    w_part = lax.dynamic_slice_in_dim(w_out, lax.rem(place, 2) * w_rows, w_rows, 0)
    w_part = tied(w_part, far)
    w_got = lax.ppermute(w_part, "joint", swap)
    w_shared = lax.ppermute(w_got, "view", to_other_core)

    first_view = place * views_dev
    own_slot = jnp.arange(views_dev, dtype=jnp.int32)[:, None] + views_dev
    slots = jnp.concatenate(
        (own_slot, jnp.mod(partners - first_view + views_dev, num_views)), axis=1
    )
    slots = jnp.clip(slots, 0, 3 * views_dev - 1)

    joint_ids = jnp.arange(padded, dtype=jnp.int32)
    line = jnp.concatenate((parents, jnp.full((padded - joints,), -1, jnp.int32)))
    skeleton = (
        (joint_ids[:, None] == joint_ids[None, :]).astype(F32)
        + (joint_ids[None, :] == line[:, None]).astype(F32)
        + (joint_ids[:, None] == line[None, :]).astype(F32)
    )
    degree = jnp.sum(skeleton, axis=1, keepdims=True)
    skeleton = skeleton.astype(BF16)
    held = (w_out, w_got, w_shared, gain_graph, skeleton, degree, w_graph)
    sent = []
    for c in chunks:
        q = query[c]
        if sent:
            q = tied(q, sent[-1][0])
        theirs = attend(where, 2, slots, c * chunk, q, window, joints)
        q = tied(q, theirs)
        moved = lax.ppermute(theirs, "joint", swap)
        mine = attend(where, 0, slots, c * chunk, q, window, joints)
        sent.append(graph_part(packed, where, mine, moved, own[c], other[c], held))

    view_ids = jnp.arange(num_views, dtype=jnp.int32)
    counts = (view_ids[:, None] == view_ids[None, :]).astype(F32)
    counts = counts + jnp.sum(
        (view_links[:, :, None] == view_ids[None, None, :]).astype(F32), axis=1
    )
    share = 1.0 / (view_links.shape[1] + 1)
    if packed:
        order = lax.rem(place, 2).reshape(1)
        total = ()
        for c in chunks:
            part = lax.all_to_all(sent[c][0], "view", split_axis=0, concat_axis=0, tiled=True)
            ids = view_ids.reshape(devices, -1, chunk)[:, c].reshape(-1)
            keeper = (ids[:, None] == view_ids[None, :]).astype(BF16)
            low = counts.T.reshape(devices, -1, chunk, num_views)[:, c].astype(BF16)
            low = low.reshape(-1, num_views)
            total = (mix(order, part, low, keeper, total, c == chunks[-1], joints, share),)
        return jnp.transpose(total[0], (1, 0, 2))[None]

    hidden = jnp.concatenate([part[0] for part in sent], axis=0)[:, :joints]
    graph_term = jnp.concatenate([part[1] for part in sent], axis=0)[:, :joints]
    residual = jnp.transpose(hidden, (2, 1, 0))
    graph_term = jnp.transpose(graph_term, (2, 1, 0))
    residual = lax.all_to_all(residual, "view", split_axis=0, concat_axis=2, tiled=True)
    graph_term = lax.all_to_all(graph_term, "view", split_axis=0, concat_axis=2, tiled=True)
    mixed = jnp.einsum(
        "cjv,wv->cjw", graph_term, counts.astype(BF16), preferred_element_type=F32
    )
    return (residual.astype(F32) + mixed * share).astype(BF16)[None]


def solution(mesh):
    placed = (
        P("view", None, None, "joint"),
        P(),
        P(),
        P(None, "joint"),
        P(None, "joint"),
        P(None, "joint"),
        P("joint", None),
        P(),
        P("view", None),
        P(),
        P(),
    )
    return jax.shard_map(
        body, mesh=mesh, in_specs=placed, out_specs=P("joint", "view", None, None), check_vma=False
    )
```

```python
import functools

import jax
import jax.numpy as jnp
from jax import lax
from jax.experimental import pallas as pl
from jax.experimental.layout import Layout, with_layout_constraint
from jax.experimental.pallas import tpu as pltpu
from jax.sharding import PartitionSpec as P

HD = 64
LANES = 128
norm_eps = 1e-05
MIB = 1024 * 1024
VMEM_MIB = 32
ATTEND_MIB = 60
F32 = jnp.float32
BF16 = jnp.bfloat16
LOG2E = 1.4426950408889634


def round_up(value, unit):
    return (value + unit - 1) // unit * unit


def layer_norm(values, gain):
    average = jnp.mean(values, axis=-1, keepdims=True)
    centred = values - average
    spread = jnp.mean(centred * centred, axis=-1, keepdims=True)
    return centred * lax.rsqrt(spread + norm_eps) * gain


def both_halves(joint, own, other):
    low = jnp.where(joint == 0, own, other)
    high = jnp.where(joint == 0, other, own)
    return jnp.concatenate([low, high], axis=1)


def params(limit_mib):
    return pltpu.CompilerParams(vmem_limit_bytes=limit_mib * MIB)


HINT = pl.CostEstimate(flops=1_000_000, bytes_accessed=10_000, transcendentals=0)


def project_kernel(with_query, joints, place_ref, *refs):
    count = 3 if with_query else 2
    halves = 2 if with_query else 3
    tokens, rest = refs[:halves], refs[halves:]
    gain_ref, weights, outs = rest[0], rest[1 : 1 + count], rest[1 + count :]
    views, frames, padded, _ = tokens[0].shape
    joint = place_ref[0]
    gain = gain_ref[...]
    row = lax.broadcasted_iota(jnp.int32, (padded, 1), 0)
    real = row < joints
    pieces = []
    for view in range(views):
        for frame in range(frames):
            own = tokens[0][view, frame].astype(F32)
            other = tokens[1][view, frame].astype(F32)
            if not with_query:
                other = jnp.where(place_ref[1] == 0, other, tokens[2][view, frame].astype(F32))
            normed = layer_norm(both_halves(joint, own, other), gain)
            pieces.append(jnp.where(real, normed, normed[0:1]))
    flat = jnp.concatenate(pieces, axis=0).astype(BF16)
    real = jnp.concatenate([real] * (views * frames), axis=0)
    rows = frames * padded
    width = weights[-1].shape[1]
    keys = jnp.dot(flat, weights[-2][...], preferred_element_type=F32).astype(BF16)
    values = jnp.dot(flat, weights[-1][...], preferred_element_type=F32)
    values = jnp.where(real, values, 0.0).astype(BF16)
    for view in range(views):
        part = slice(view * rows, (view + 1) * rows)
        for pair in range(width // LANES):
            columns = slice(pair * LANES, (pair + 1) * LANES)
            outs[-1][pair, view, :, :LANES] = keys[part, columns]
            outs[-1][pair, view, :, LANES:] = values[part, columns]
    if with_query:
        query = jnp.dot(flat, weights[0][...], preferred_element_type=F32)
        for view in range(views):
            for frame in range(frames):
                at = (view * frames + frame) * padded
                outs[0][view, frame] = query[at : at + padded].astype(BF16)


def project(place, tokens, gain, weights, joints):
    views, frames, padded, half = tokens[0].shape
    model, width = weights[0].shape
    rows = frames * padded
    with_query = len(weights) == 3
    step = 2 if views % 2 == 0 else 1
    pairs = width // LANES
    out_shape = [pltpu.HBM((pairs, views, rows, 2 * LANES), BF16)]
    out_specs = [pl.BlockSpec((pairs, step, rows, 2 * LANES), lambda i, s: (0, i, 0, 0))]
    if with_query:
        out_shape = [pltpu.HBM((views, frames, padded, width), BF16)] + out_shape
        out_specs = [
            pl.BlockSpec((step, frames, padded, width), lambda i, s: (i, 0, 0, 0))
        ] + out_specs
    token = pl.BlockSpec((step, frames, padded, half), lambda i, s: (i, 0, 0, 0))
    weight = pl.BlockSpec((model, width), lambda i, s: (0, 0))
    return pl.pallas_call(
        functools.partial(project_kernel, with_query, joints),
        grid_spec=pltpu.PrefetchScalarGridSpec(
            num_scalar_prefetch=1,
            grid=(views // step,),
            in_specs=[token] * len(tokens)
            + [pl.BlockSpec((1, model), lambda i, s: (0, 0))]
            + [weight] * len(weights),
            out_specs=out_specs,
        ),
        out_shape=out_shape,
        compiler_params=params(VMEM_MIB),
        cost_estimate=HINT,
        name="project",
    )(place, *tokens, gain, *weights)


def attend_kernel(first, joints, place_ref, slot_ref, q_ref, *rest):
    sources = rest[:-4]
    out_ref, window, ones_ref, sems = rest[-4:]
    views, _, padded, _ = q_ref.shape
    blocks = slot_ref.shape[1]
    pairs, _, rows, _ = window.shape
    pair = pl.program_id(0)

    def copies(index):
        begin, found = 0, []
        for place, source in enumerate(sources):
            count = source.shape[1]
            found.append(
                pltpu.make_async_copy(
                    source.at[index], window.at[index, pl.ds(begin, count)], sems.at[index, place]
                )
            )
            begin += count
        return found

    @pl.when(pair == 0)
    def _():
        for index in range(pairs):
            for copy in copies(index):
                copy.start()
        row = lax.broadcasted_iota(jnp.int32, (padded, LANES), 0)
        real = jnp.where(row < joints, 1.0, 0.0)
        ones_ref[...] = jnp.concatenate([real] * (blocks * rows // padded), axis=0).astype(BF16)

    for copy in copies(pair):
        copy.wait()

    left = lax.broadcasted_iota(jnp.int32, (1, LANES), 1) < HD
    ones = ones_ref[...]
    scale = HD**-0.5 * LOG2E
    for view in range(views):
        query = q_ref[view, 0].astype(F32)
        stacked = jnp.concatenate(
            [jnp.where(left, query, 0.0), jnp.where(left, 0.0, query)], axis=0
        ).astype(BF16)
        slots = [slot_ref[first + view, block] for block in range(blocks)]
        keys = jnp.concatenate([window[pair, slot, :, :LANES] for slot in slots], axis=0)
        values = jnp.concatenate([window[pair, slot, :, LANES:] for slot in slots], axis=0)
        scores = lax.dot_general(
            stacked, keys, (((1,), (1,)), ((), ())), preferred_element_type=F32
        )
        top = jnp.max(scores, axis=1, keepdims=True)
        powers = jnp.exp2((scores - top) * scale).astype(BF16)
        values = jnp.concatenate([values, ones], axis=1)
        found = jnp.dot(powers, values, preferred_element_type=F32)
        total = jnp.where(left, found[:padded, :LANES], found[padded:, :LANES])
        weight = jnp.where(left, found[:padded, LANES:], found[padded:, LANES:])
        out_ref[view] = (total / weight).astype(BF16)


def attend(place, frame, slots, first, query, sources, joints):
    views, _, padded, width = query.shape
    pairs, _, rows, _ = sources[0].shape
    held = sum(source.shape[1] for source in sources)
    blocks = slots.shape[1]
    return pl.pallas_call(
        functools.partial(attend_kernel, first, joints),
        grid_spec=pltpu.PrefetchScalarGridSpec(
            num_scalar_prefetch=2,
            grid=(pairs,),
            in_specs=[
                pl.BlockSpec((views, 1, padded, LANES), lambda i, p, s: (0, p[frame], 0, i))
            ]
            + [pl.BlockSpec(memory_space=pltpu.HBM)] * len(sources),
            out_specs=pl.BlockSpec((views, padded, LANES), lambda i, p, s: (0, 0, i)),
            scratch_shapes=[
                pltpu.VMEM((pairs, held, rows, 2 * LANES), BF16),
                pltpu.VMEM((blocks * rows, LANES), BF16),
                pltpu.SemaphoreType.DMA((pairs, len(sources))),
            ],
        ),
        out_shape=pltpu.HBM((views, padded, width), BF16),
        compiler_params=params(ATTEND_MIB),
        cost_estimate=HINT,
        name="attend",
    )(place, slots, query, *sources)


def graph_kernel(packed, place_ref, *refs):
    mine_ref, theirs_ref, own_ref, other_ref, w_mine_ref, w_got_ref, w_shared_ref = refs[:7]
    gain_ref, skeleton_ref, degree_ref, w_graph_ref, *outs = refs[7:]
    views, padded, width = mine_ref.shape
    joint, core = place_ref[0], place_ref[1]
    model = w_graph_ref.shape[0]
    gain = gain_ref[...]

    def rows_of(ref):
        pieces = [ref[view].astype(F32) for view in range(views)]
        return jnp.concatenate(pieces, axis=0).astype(BF16)

    mine, theirs = rows_of(mine_ref), rows_of(theirs_ref)
    w_low = jnp.where(core == 0, w_got_ref[...], w_shared_ref[...])
    w_high = jnp.where(core == 0, w_shared_ref[...], w_got_ref[...])
    projected = (
        jnp.dot(mine, w_mine_ref[...], preferred_element_type=F32)
        + jnp.dot(theirs[:, : width // 2], w_low, preferred_element_type=F32)
        + jnp.dot(theirs[:, width // 2 :], w_high, preferred_element_type=F32)
    )
    hiddens, mixed = [], []
    for view in range(views):
        own, other = own_ref[view, 0].astype(F32), other_ref[view, 0].astype(F32)
        part = projected[view * padded : (view + 1) * padded]
        hidden = (both_halves(joint, own, other) + part).astype(BF16).astype(F32)
        normed = layer_norm(hidden, gain).astype(BF16)
        summed = jnp.dot(skeleton_ref[...], normed, preferred_element_type=F32)
        hiddens.append(hidden)
        mixed.append(summed / degree_ref[...])
    skeletal = jnp.concatenate(mixed, axis=0).astype(BF16)
    graph = jnp.dot(skeletal, w_graph_ref[...], preferred_element_type=F32)
    first = lax.broadcasted_iota(jnp.int32, (1, LANES), 1) < LANES // 2
    for view in range(views):
        term = graph[view * padded : (view + 1) * padded]
        if not packed:
            outs[0][view] = hiddens[view].astype(BF16)
            outs[1][view] = term.astype(BF16)
            continue
        for tile in range(model // LANES):
            columns = slice(tile * LANES, (tile + 1) * LANES)
            kept = hiddens[view][:, columns]
            turned = pltpu.roll(term[:, columns], LANES // 2, axis=1)
            outs[0][2 * tile, view] = jnp.where(first, kept, turned).astype(BF16)
            outs[0][2 * tile + 1, view] = jnp.where(first, turned, kept).astype(BF16)


def graph_part(packed, place, mine, theirs, own, other, held):
    views, padded, width = mine.shape
    half = own.shape[3]
    model = held[-1].shape[0]
    heads = pl.BlockSpec((views, padded, width), lambda i, j: (0, 0, 0))
    token = pl.BlockSpec((views, 1, padded, half), lambda i, j: (0, j[0], 0, 0))
    if packed:
        devices = 2 * model // LANES
        out_shape = [pltpu.HBM((devices, views, padded, LANES), BF16)]
        out_specs = [pl.BlockSpec((devices, views, padded, LANES), lambda i, j: (0, 0, 0, 0))]
    else:
        out_shape = [jax.ShapeDtypeStruct((views, padded, model), BF16)] * 2
        out_specs = [pl.BlockSpec((views, padded, model), lambda i, j: (0, 0, 0))] * 2
    return pl.pallas_call(
        functools.partial(graph_kernel, packed),
        grid_spec=pltpu.PrefetchScalarGridSpec(
            num_scalar_prefetch=1,
            grid=(1,),
            in_specs=[heads, heads, token, token]
            + [pl.BlockSpec(a.shape, lambda i, j: (0, 0)) for a in held],
            out_specs=out_specs,
        ),
        out_shape=out_shape,
        compiler_params=params(VMEM_MIB),
        cost_estimate=HINT,
        name="graph_part",
    )(place, mine, theirs, own, other, *held)


def mix_kernel(share, order_ref, part_ref, counts_ref, kept_ref, *rest):
    earlier, (out_ref, wide) = rest[:-2], rest[-2:]
    views, rows, _ = part_ref.shape
    channels = out_ref.shape[1]
    wide[...] = part_ref[...].astype(F32).reshape(views * rows, LANES)
    counts, keeper = counts_ref[...], kept_ref[...]
    flipped = order_ref[0] == 1
    for row in range(rows):
        lanes_first = wide[pl.ds(row, views, stride=rows), :].T
        low, high = lanes_first[:channels], lanes_first[channels:]
        term = jnp.where(flipped, low, high).astype(BF16)
        kept = jnp.where(flipped, high, low).astype(BF16)
        total = jnp.dot(kept, keeper, preferred_element_type=F32)
        total = total + jnp.dot(term, counts, preferred_element_type=F32) * share
        if earlier:
            total = total + earlier[0][row]
        out_ref[row] = total.astype(out_ref.dtype)


def mix(order, part, counts, keeper, earlier, last, joints, share):
    part = part.reshape(-1, *part.shape[2:])
    views, padded, _ = part.shape
    num_views = counts.shape[1]
    channels = LANES // 2
    rows = 16
    block = pl.BlockSpec((rows, channels, num_views), lambda i, s: (i, 0, 0))
    held = pl.BlockSpec(counts.shape, lambda i, s: (0, 0))
    return pl.pallas_call(
        functools.partial(mix_kernel, share),
        grid_spec=pltpu.PrefetchScalarGridSpec(
            num_scalar_prefetch=1,
            grid=(pl.cdiv(joints, rows),),
            in_specs=[pl.BlockSpec((views, rows, LANES), lambda i, s: (0, i, 0)), held, held]
            + [block] * len(earlier),
            out_specs=block,
            scratch_shapes=[pltpu.VMEM((views * rows, LANES), F32)],
        ),
        out_shape=jax.ShapeDtypeStruct((joints, channels, num_views), BF16 if last else F32),
        compiler_params=params(VMEM_MIB),
        cost_estimate=HINT,
        name="mix",
    )(order, part, counts, keeper, *earlier)


def body(
    pose_tokens,
    gain_attn,
    gain_graph,
    w_query,
    w_key,
    w_value,
    w_out,
    w_graph,
    partners,
    parents,
    view_links,
):
    views_dev, frames, joints, half_width = pose_tokens.shape
    model = w_graph.shape[0]
    devices = lax.axis_size("view")
    place = lax.axis_index("view").astype(jnp.int32)
    joint_place = lax.axis_index("joint").astype(jnp.int32)
    num_views = devices * views_dev
    channels = model // devices
    padded = round_up(joints, 8)
    rows = frames * padded
    chunks = range(2 if views_dev % 4 == 0 else 1)
    chunk = views_dev // len(chunks)
    packed = 2 * channels == LANES and num_views == LANES
    swap = [(0, 1), (1, 0)]
    up = [(i, (i + 1) % devices) for i in range(devices)]
    down = [(j, i) for i, j in up]
    swap_even = [(2 * v + j, 2 * v + 1 - j) for v in range(0, devices, 2) for j in (0, 1)]
    to_odd = [(2 * v + j, 2 * v + 2 + j) for v in range(0, devices, 2) for j in (0, 1)]
    gain_attn = gain_attn.reshape(1, model)
    gain_graph = gain_graph.reshape(1, model)
    where = jnp.stack((joint_place, lax.rem(place, 2), 1 - joint_place))

    to_other_core = [(v, v ^ 1) for v in range(devices)]

    def tied(array, *others):
        return lax.optimization_barrier((array, *others))[0]

    own = []
    for c in chunks:
        part = lax.slice_in_dim(pose_tokens, c * chunk, (c + 1) * chunk)
        part = jnp.pad(part, ((0, 0), (0, 0), (0, padded - joints), (0, 0)))
        own.append(with_layout_constraint(part, Layout(major_to_minor=(0, 1, 2, 3))))

    near = [lax.ppermute(part, "view", up) for part in own]
    other, query, here, after = [], [], [], []
    for c in chunks:
        other.append(lax.ppermute(own[c], "joint", swap))
        part = tied(other[c], *near)
        q, kv = project(where, (own[c], part), gain_attn, (w_query, w_key, w_value), joints)
        query.append(q)
        here.append(kv)
        after.append(lax.ppermute(kv, "view", down))
    before = []
    for c in chunks:
        far = lax.ppermute(
            tied(near[c], other[-1], here[0]), ("view", "joint"), swap_even
        )
        far_odd = lax.ppermute(tied(other[c], here[0]), ("view", "joint"), to_odd)
        (kv,) = project(where, (near[c], far, far_odd), gain_attn, (w_key, w_value), joints)
        before.append(kv)
    window = before + here + after

    w_rows = w_out.shape[0] // 2
    w_part = lax.dynamic_slice_in_dim(w_out, lax.rem(place, 2) * w_rows, w_rows, 0)
    w_part = tied(w_part, far)
    w_got = lax.ppermute(w_part, "joint", swap)
    w_shared = lax.ppermute(w_got, "view", to_other_core)

    first_view = place * views_dev
    own_slot = jnp.arange(views_dev, dtype=jnp.int32)[:, None] + views_dev
    slots = jnp.concatenate(
        (own_slot, jnp.mod(partners - first_view + views_dev, num_views)), axis=1
    )
    slots = jnp.clip(slots, 0, 3 * views_dev - 1)

    joint_ids = jnp.arange(padded, dtype=jnp.int32)
    line = jnp.concatenate((parents, jnp.full((padded - joints,), -1, jnp.int32)))
    skeleton = (
        (joint_ids[:, None] == joint_ids[None, :]).astype(F32)
        + (joint_ids[None, :] == line[:, None]).astype(F32)
        + (joint_ids[:, None] == line[None, :]).astype(F32)
    )
    degree = jnp.sum(skeleton, axis=1, keepdims=True)
    skeleton = skeleton.astype(BF16)
    held = (w_out, w_got, w_shared, gain_graph, skeleton, degree, w_graph)
    sent = []
    for c in chunks:
        q = query[c]
        if sent:
            q = tied(q, sent[-1][0])
        theirs = attend(where, 2, slots, c * chunk, q, window, joints)
        q = tied(q, theirs)
        moved = lax.ppermute(theirs, "joint", swap)
        mine = attend(where, 0, slots, c * chunk, q, window, joints)
        sent.append(graph_part(packed, where, mine, moved, own[c], other[c], held))

    view_ids = jnp.arange(num_views, dtype=jnp.int32)
    counts = (view_ids[:, None] == view_ids[None, :]).astype(F32)
    counts = counts + jnp.sum(
        (view_links[:, :, None] == view_ids[None, None, :]).astype(F32), axis=1
    )
    share = 1.0 / (view_links.shape[1] + 1)
    if packed:
        order = lax.rem(place, 2).reshape(1)
        total = ()
        for c in chunks:
            part = lax.all_to_all(sent[c][0], "view", split_axis=0, concat_axis=0, tiled=True)
            ids = view_ids.reshape(devices, -1, chunk)[:, c].reshape(-1)
            keeper = (ids[:, None] == view_ids[None, :]).astype(BF16)
            low = counts.T.reshape(devices, -1, chunk, num_views)[:, c].astype(BF16)
            low = low.reshape(-1, num_views)
            total = (mix(order, part, low, keeper, total, c == chunks[-1], joints, share),)
        return jnp.transpose(total[0], (1, 0, 2))[None]

    hidden = jnp.concatenate([part[0] for part in sent], axis=0)[:, :joints]
    graph_term = jnp.concatenate([part[1] for part in sent], axis=0)[:, :joints]
    residual = jnp.transpose(hidden, (2, 1, 0))
    graph_term = jnp.transpose(graph_term, (2, 1, 0))
    residual = lax.all_to_all(residual, "view", split_axis=0, concat_axis=2, tiled=True)
    graph_term = lax.all_to_all(graph_term, "view", split_axis=0, concat_axis=2, tiled=True)
    mixed = jnp.einsum(
        "cjv,wv->cjw", graph_term, counts.astype(BF16), preferred_element_type=F32
    )
    return (residual.astype(F32) + mixed * share).astype(BF16)[None]


def solution(mesh):
    placed = (
        P("view", None, None, "joint"),
        P(),
        P(),
        P(None, "joint"),
        P(None, "joint"),
        P(None, "joint"),
        P("joint", None),
        P(),
        P("view", None),
        P(),
        P(),
    )
    return jax.shard_map(
        body, mesh=mesh, in_specs=placed, out_specs=P("joint", "view", None, None), check_vma=False
    )
```

```python
import functools

import jax
import jax.numpy as jnp
from jax import lax
from jax.experimental import pallas as pl
from jax.experimental.layout import Layout, with_layout_constraint
from jax.experimental.pallas import tpu as pltpu
from jax.sharding import PartitionSpec as P

HD = 64
LANES = 128
QUAD = 256
norm_eps = 1e-05
MIB = 1024 * 1024
VMEM_MIB = 32
ATTEND_MIB = 60
F32 = jnp.float32
BF16 = jnp.bfloat16
LOG2E = 1.4426950408889634


def round_up(value, unit):
    return (value + unit - 1) // unit * unit


def layer_norm(values, gain):
    average = jnp.mean(values, axis=-1, keepdims=True)
    centred = values - average
    spread = jnp.mean(centred * centred, axis=-1, keepdims=True)
    return centred * lax.rsqrt(spread + norm_eps) * gain


def both_halves(joint, own, other):
    low = jnp.where(joint == 0, own, other)
    high = jnp.where(joint == 0, other, own)
    return jnp.concatenate([low, high], axis=1)


def params(limit_mib):
    return pltpu.CompilerParams(vmem_limit_bytes=limit_mib * MIB)


HINT = pl.CostEstimate(flops=1_000_000, bytes_accessed=10_000, transcendentals=0)


def project_kernel(with_query, joints, place_ref, *refs):
    count = 3 if with_query else 2
    halves = 2 if with_query else 3
    tokens, rest = refs[:halves], refs[halves:]
    gain_ref, weights, outs = rest[0], rest[1 : 1 + count], rest[1 + count :]
    views, frames, padded, _ = tokens[0].shape
    joint = place_ref[0]
    gain = gain_ref[...]
    row = lax.broadcasted_iota(jnp.int32, (padded, 1), 0)
    real = row < joints
    pieces = []
    for view in range(views):
        for frame in range(frames):
            own = tokens[0][view, frame].astype(F32)
            other = tokens[1][view, frame].astype(F32)
            if not with_query:
                other = jnp.where(place_ref[1] == 0, other, tokens[2][view, frame].astype(F32))
            normed = layer_norm(both_halves(joint, own, other), gain)
            pieces.append(jnp.where(real, normed, normed[0:1]))
    flat = jnp.concatenate(pieces, axis=0).astype(BF16)
    real = jnp.concatenate([real] * (views * frames), axis=0)
    rows = frames * padded
    width = weights[-1].shape[1]
    keys = jnp.dot(flat, weights[-2][...], preferred_element_type=F32).astype(BF16)
    values = jnp.dot(flat, weights[-1][...], preferred_element_type=F32)
    values = jnp.where(real, values, 0.0).astype(BF16)
    for view in range(views):
        part = slice(view * rows, (view + 1) * rows)
        for quad in range(width // QUAD):
            columns = slice(quad * QUAD, (quad + 1) * QUAD)
            outs[-1][2 * quad, view] = keys[part, columns]
            outs[-1][2 * quad + 1, view] = values[part, columns]
    if with_query:
        query = jnp.dot(flat, weights[0][...], preferred_element_type=F32)
        for view in range(views):
            for frame in range(frames):
                at = (view * frames + frame) * padded
                outs[0][view, frame] = query[at : at + padded].astype(BF16)


def project(place, tokens, gain, weights, joints):
    views, frames, padded, half = tokens[0].shape
    model, width = weights[0].shape
    rows = frames * padded
    with_query = len(weights) == 3
    step = 2 if views % 2 == 0 else 1
    planes = 2 * width // QUAD
    out_shape = [pltpu.HBM((planes, views, rows, QUAD), BF16)]
    out_specs = [pl.BlockSpec((planes, step, rows, QUAD), lambda i, s: (0, i, 0, 0))]
    if with_query:
        out_shape = [pltpu.HBM((views, frames, padded, width), BF16)] + out_shape
        out_specs = [
            pl.BlockSpec((step, frames, padded, width), lambda i, s: (i, 0, 0, 0))
        ] + out_specs
    token = pl.BlockSpec((step, frames, padded, half), lambda i, s: (i, 0, 0, 0))
    weight = pl.BlockSpec((model, width), lambda i, s: (0, 0))
    return pl.pallas_call(
        functools.partial(project_kernel, with_query, joints),
        grid_spec=pltpu.PrefetchScalarGridSpec(
            num_scalar_prefetch=1,
            grid=(views // step,),
            in_specs=[token] * len(tokens)
            + [pl.BlockSpec((1, model), lambda i, s: (0, 0))]
            + [weight] * len(weights),
            out_specs=out_specs,
        ),
        out_shape=out_shape,
        compiler_params=params(VMEM_MIB),
        cost_estimate=HINT,
        name="project",
    )(place, *tokens, gain, *weights)


def attend_kernel(first, joints, place_ref, slot_ref, q_ref, *rest):
    sources = rest[:-3]
    out_ref, window, sems = rest[-3:]
    views, _, padded, _ = q_ref.shape
    blocks = slot_ref.shape[1]
    planes, _, rows, _ = window.shape
    quad = pl.program_id(0)

    def copies(plane):
        begin, found = 0, []
        for place, source in enumerate(sources):
            count = source.shape[1]
            found.append(
                pltpu.make_async_copy(
                    source.at[plane], window.at[plane, pl.ds(begin, count)], sems.at[plane, place]
                )
            )
            begin += count
        return found

    @pl.when(quad == 0)
    def _():
        for plane in range(planes):
            for copy in copies(plane):
                copy.start()

    for copy in copies(2 * quad):
        copy.wait()

    heads = QUAD // HD
    lane = lax.broadcasted_iota(jnp.int32, (1, QUAD), 1)
    column = lax.broadcasted_iota(jnp.int32, (1, blocks * rows), 1)
    real = lax.rem(column, padded) < joints
    scale = HD**-0.5 * LOG2E
    for view in range(views):
        query = q_ref[view, 0].astype(F32)
        stacked = jnp.concatenate(
            [jnp.where(lane // HD == head, query, 0.0) for head in range(heads)], axis=0
        ).astype(BF16)
        slots = [slot_ref[first + view, block] for block in range(blocks)]
        keys = jnp.concatenate([window[2 * quad, slot] for slot in slots], axis=0)
        scores = lax.dot_general(
            stacked, keys, (((1,), (1,)), ((), ())), preferred_element_type=F32
        )
        top = jnp.max(scores, axis=1, keepdims=True)
        powers = jnp.exp2((scores - top) * scale)
        weight = jnp.sum(jnp.where(real, powers, 0.0), axis=1, keepdims=True)
        if view == 0:
            for copy in copies(2 * quad + 1):
                copy.wait()
        values = jnp.concatenate([window[2 * quad + 1, slot] for slot in slots], axis=0)
        found = jnp.dot(powers.astype(BF16), values, preferred_element_type=F32) / weight
        total = found[:padded]
        for head in range(1, heads):
            part = found[head * padded : (head + 1) * padded]
            total = jnp.where(lane // HD == head, part, total)
        out_ref[view] = total.astype(BF16)


def attend(place, frame, slots, first, query, begin, views, sources, joints):
    _, _, padded, width = query.shape
    planes, _, rows, _ = sources[0].shape
    held = sum(source.shape[1] for source in sources)
    return pl.pallas_call(
        functools.partial(attend_kernel, first, joints),
        grid_spec=pltpu.PrefetchScalarGridSpec(
            num_scalar_prefetch=2,
            grid=(width // QUAD,),
            in_specs=[
                pl.BlockSpec(
                    (views, 1, padded, QUAD), lambda i, p, s: (begin // views, p[frame], 0, i)
                )
            ]
            + [pl.BlockSpec(memory_space=pltpu.HBM)] * len(sources),
            out_specs=pl.BlockSpec((views, padded, QUAD), lambda i, p, s: (0, 0, i)),
            scratch_shapes=[
                pltpu.VMEM((planes, held, rows, QUAD), BF16),
                pltpu.SemaphoreType.DMA((planes, len(sources))),
            ],
        ),
        out_shape=pltpu.HBM((views, padded, width), BF16),
        compiler_params=params(ATTEND_MIB),
        cost_estimate=HINT,
        name="attend",
    )(place, slots, query, *sources)


def graph_kernel(packed, place_ref, *refs):
    mine_ref, theirs_ref, own_ref, other_ref, w_mine_ref, w_got_ref, w_shared_ref = refs[:7]
    gain_ref, skeleton_ref, degree_ref, w_graph_ref, *outs = refs[7:]
    views, padded, width = mine_ref.shape
    joint, core = place_ref[0], place_ref[1]
    model = w_graph_ref.shape[0]
    gain = gain_ref[...]

    def rows_of(ref):
        pieces = [ref[view].astype(F32) for view in range(views)]
        return jnp.concatenate(pieces, axis=0).astype(BF16)

    mine, theirs = rows_of(mine_ref), rows_of(theirs_ref)
    w_low = jnp.where(core == 0, w_got_ref[...], w_shared_ref[...])
    w_high = jnp.where(core == 0, w_shared_ref[...], w_got_ref[...])
    projected = (
        jnp.dot(mine, w_mine_ref[...], preferred_element_type=F32)
        + jnp.dot(theirs[:, : width // 2], w_low, preferred_element_type=F32)
        + jnp.dot(theirs[:, width // 2 :], w_high, preferred_element_type=F32)
    )
    hiddens, mixed = [], []
    for view in range(views):
        own, other = own_ref[view, 0].astype(F32), other_ref[view, 0].astype(F32)
        part = projected[view * padded : (view + 1) * padded]
        hidden = (both_halves(joint, own, other) + part).astype(BF16).astype(F32)
        normed = layer_norm(hidden, gain).astype(BF16)
        summed = jnp.dot(skeleton_ref[...], normed, preferred_element_type=F32)
        hiddens.append(hidden)
        mixed.append(summed / degree_ref[...])
    skeletal = jnp.concatenate(mixed, axis=0).astype(BF16)
    graph = jnp.dot(skeletal, w_graph_ref[...], preferred_element_type=F32)
    first = lax.broadcasted_iota(jnp.int32, (1, LANES), 1) < LANES // 2
    for view in range(views):
        term = graph[view * padded : (view + 1) * padded]
        if not packed:
            outs[0][view] = hiddens[view].astype(BF16)
            outs[1][view] = term.astype(BF16)
            continue
        for tile in range(model // LANES):
            columns = slice(tile * LANES, (tile + 1) * LANES)
            kept = hiddens[view][:, columns]
            turned = pltpu.roll(term[:, columns], LANES // 2, axis=1)
            outs[0][2 * tile, view] = jnp.where(first, kept, turned).astype(BF16)
            outs[0][2 * tile + 1, view] = jnp.where(first, turned, kept).astype(BF16)


def graph_part(packed, place, mine, theirs, own, other, begin, held):
    views, padded, width = mine.shape
    half = own.shape[3]
    model = held[-1].shape[0]
    heads = pl.BlockSpec((views, padded, width), lambda i, j: (0, 0, 0))
    token = pl.BlockSpec((views, 1, padded, half), lambda i, j: (begin // views, j[0], 0, 0))
    if packed:
        devices = 2 * model // LANES
        out_shape = [pltpu.HBM((devices, views, padded, LANES), BF16)]
        out_specs = [pl.BlockSpec((devices, views, padded, LANES), lambda i, j: (0, 0, 0, 0))]
    else:
        out_shape = [jax.ShapeDtypeStruct((views, padded, model), BF16)] * 2
        out_specs = [pl.BlockSpec((views, padded, model), lambda i, j: (0, 0, 0))] * 2
    return pl.pallas_call(
        functools.partial(graph_kernel, packed),
        grid_spec=pltpu.PrefetchScalarGridSpec(
            num_scalar_prefetch=1,
            grid=(1,),
            in_specs=[heads, heads, token, token]
            + [pl.BlockSpec(a.shape, lambda i, j: (0, 0)) for a in held],
            out_specs=out_specs,
        ),
        out_shape=out_shape,
        compiler_params=params(VMEM_MIB),
        cost_estimate=HINT,
        name="graph_part",
    )(place, mine, theirs, own, other, *held)


def mix_kernel(share, count, order_ref, *rest):
    parts, (counts_ref, kept_ref, *earlier, out_ref, wide) = rest[:count], rest[count:]
    rows, channels, _ = out_ref.shape
    views = 0
    for part in parts:
        block = part[...].astype(F32).reshape(part.shape[0] * rows, LANES)
        wide[views * rows : views * rows + block.shape[0]] = block
        views += part.shape[0]
    counts, keeper = counts_ref[...], kept_ref[...]
    flipped = order_ref[0] == 1
    for row in range(rows):
        lanes_first = wide[pl.ds(row, views, stride=rows), :].T
        low, high = lanes_first[:channels], lanes_first[channels:]
        term = jnp.where(flipped, low, high).astype(BF16)
        kept = jnp.where(flipped, high, low).astype(BF16)
        total = jnp.dot(kept, keeper, preferred_element_type=F32)
        total = total + jnp.dot(term, counts, preferred_element_type=F32) * share
        if earlier:
            total = total + earlier[0][row]
        out_ref[row] = total.astype(out_ref.dtype)


def mix(order, parts, counts, keeper, earlier, last, joints, share):
    parts = [part.reshape(-1, *part.shape[2:]) for part in parts]
    views, num_views = counts.shape
    padded = parts[0].shape[1]
    channels = LANES // 2
    rows = 16
    block = pl.BlockSpec((rows, channels, num_views), lambda i, s: (i, 0, 0))
    held = pl.BlockSpec(counts.shape, lambda i, s: (0, 0))
    return pl.pallas_call(
        functools.partial(mix_kernel, share, len(parts)),
        grid_spec=pltpu.PrefetchScalarGridSpec(
            num_scalar_prefetch=1,
            grid=(pl.cdiv(joints, rows),),
            in_specs=[
                pl.BlockSpec((part.shape[0], rows, LANES), lambda i, s: (0, i, 0))
                for part in parts
            ]
            + [held, held]
            + [block] * len(earlier),
            out_specs=block,
            scratch_shapes=[pltpu.VMEM((views * rows, LANES), F32)],
        ),
        out_shape=jax.ShapeDtypeStruct((joints, channels, num_views), BF16 if last else F32),
        compiler_params=params(VMEM_MIB),
        cost_estimate=HINT,
        name="mix",
    )(order, *parts, counts, keeper, *earlier)


def body(
    pose_tokens,
    gain_attn,
    gain_graph,
    w_query,
    w_key,
    w_value,
    w_out,
    w_graph,
    partners,
    parents,
    view_links,
):
    views_dev, frames, joints, half_width = pose_tokens.shape
    model = w_graph.shape[0]
    devices = lax.axis_size("view")
    place = lax.axis_index("view").astype(jnp.int32)
    joint_place = lax.axis_index("joint").astype(jnp.int32)
    num_views = devices * views_dev
    channels = model // devices
    padded = round_up(joints, 8)
    rows = frames * padded
    if views_dev == 8:
        chunks = ((0, 6), (6, 2))
        tail = ((0, 0, 3), (0, 3, 3), (1, 0, 2))
    else:
        chunks = ((0, views_dev),)
        tail = ((0, 0, views_dev),)
    packed = 2 * channels == LANES and num_views == LANES
    swap = [(0, 1), (1, 0)]
    up = [(i, (i + 1) % devices) for i in range(devices)]
    down = [(j, i) for i, j in up]
    swap_even = [(2 * v + j, 2 * v + 1 - j) for v in range(0, devices, 2) for j in (0, 1)]
    to_odd = [(2 * v + j, 2 * v + 2 + j) for v in range(0, devices, 2) for j in (0, 1)]
    gain_attn = gain_attn.reshape(1, model)
    gain_graph = gain_graph.reshape(1, model)
    where = jnp.stack((joint_place, lax.rem(place, 2), 1 - joint_place))

    to_other_core = [(v, v ^ 1) for v in range(devices)]

    def tied(array, *others):
        return lax.optimization_barrier((array, *others))[0]

    own = []
    for begin, count in chunks:
        part = lax.slice_in_dim(pose_tokens, begin, begin + count)
        part = jnp.pad(part, ((0, 0), (0, 0), (0, padded - joints), (0, 0)))
        own.append(with_layout_constraint(part, Layout(major_to_minor=(0, 1, 2, 3))))

    near = [lax.ppermute(part, "view", up) for part in own]
    other, query, here, after = [], [], [], []
    for c in range(len(chunks)):
        other.append(lax.ppermute(own[c], "joint", swap))
        q, kv = project(where, (own[c], other[c]), gain_attn, (w_query, w_key, w_value), joints)
        query.append(q)
        here.append(kv)
        after.append(lax.ppermute(kv, "view", down))
    before = []
    for c in range(len(chunks)):
        far = lax.ppermute(
            tied(near[c], other[-1], here[0]), ("view", "joint"), swap_even
        )
        far_odd = lax.ppermute(tied(other[c], here[0]), ("view", "joint"), to_odd)
        (kv,) = project(where, (near[c], far, far_odd), gain_attn, (w_key, w_value), joints)
        before.append(kv)
    window = before + here + after

    w_rows = w_out.shape[0] // 2
    w_part = lax.dynamic_slice_in_dim(w_out, lax.rem(place, 2) * w_rows, w_rows, 0)
    w_part = tied(w_part, far)
    w_got = lax.ppermute(w_part, "joint", swap)
    w_shared = lax.ppermute(w_got, "view", to_other_core)

    first_view = place * views_dev
    own_slot = jnp.arange(views_dev, dtype=jnp.int32)[:, None] + views_dev
    slots = jnp.concatenate(
        (own_slot, jnp.mod(partners - first_view + views_dev, num_views)), axis=1
    )
    slots = jnp.clip(slots, 0, 3 * views_dev - 1)

    joint_ids = jnp.arange(padded, dtype=jnp.int32)
    line = jnp.concatenate((parents, jnp.full((padded - joints,), -1, jnp.int32)))
    skeleton = (
        (joint_ids[:, None] == joint_ids[None, :]).astype(F32)
        + (joint_ids[None, :] == line[:, None]).astype(F32)
        + (joint_ids[:, None] == line[None, :]).astype(F32)
    )
    degree = jnp.sum(skeleton, axis=1, keepdims=True)
    skeleton = skeleton.astype(BF16)
    held = (w_out, w_got, w_shared, gain_graph, skeleton, degree, w_graph)
    sent = []
    for c, begin, count in tail:
        first = chunks[c][0] + begin
        q = query[c]
        if sent:
            q = tied(q, sent[-1][0])
        theirs = attend(where, 2, slots, first, q, begin, count, window, joints)
        q = tied(q, theirs)
        moved = lax.ppermute(theirs, "joint", swap)
        mine = attend(where, 0, slots, first, q, begin, count, window, joints)
        sent.append(graph_part(packed, where, mine, moved, own[c], other[c], begin, held))

    view_ids = jnp.arange(num_views, dtype=jnp.int32)
    counts = (view_ids[:, None] == view_ids[None, :]).astype(F32)
    counts = counts + jnp.sum(
        (view_links[:, :, None] == view_ids[None, None, :]).astype(F32), axis=1
    )
    share = 1.0 / (view_links.shape[1] + 1)
    if packed:
        order = lax.rem(place, 2).reshape(1)
        parts = [
            lax.all_to_all(part, "view", split_axis=0, concat_axis=0, tiled=True)
            for (part,) in sent
        ]
        at = [(chunks[c][0] + begin, count) for c, begin, count in tail]
        groups = (range(len(tail) - 1), range(len(tail) - 1, len(tail)))

        def rows_of(matrix, group):
            matrix = matrix.reshape(devices, views_dev, num_views)
            pieces = [
                matrix[:, at[k][0] : at[k][0] + at[k][1]].reshape(-1, num_views) for k in group
            ]
            return jnp.concatenate(pieces, axis=0).astype(BF16)

        total = ()
        for group in groups if len(tail) > 1 else groups[1:]:
            total = (
                mix(
                    order,
                    [parts[k] for k in group],
                    rows_of(counts.T, group),
                    rows_of(jnp.eye(num_views), group),
                    total,
                    group[-1] == len(tail) - 1,
                    joints,
                    share,
                ),
            )
        return jnp.transpose(total[0], (1, 0, 2))[None]

    hidden = jnp.concatenate([part[0] for part in sent], axis=0)[:, :joints]
    graph_term = jnp.concatenate([part[1] for part in sent], axis=0)[:, :joints]
    residual = jnp.transpose(hidden, (2, 1, 0))
    graph_term = jnp.transpose(graph_term, (2, 1, 0))
    residual = lax.all_to_all(residual, "view", split_axis=0, concat_axis=2, tiled=True)
    graph_term = lax.all_to_all(graph_term, "view", split_axis=0, concat_axis=2, tiled=True)
    mixed = jnp.einsum(
        "cjv,wv->cjw", graph_term, counts.astype(BF16), preferred_element_type=F32
    )
    return (residual.astype(F32) + mixed * share).astype(BF16)[None]


def solution(mesh):
    placed = (
        P("view", None, None, "joint"),
        P(),
        P(),
        P(None, "joint"),
        P(None, "joint"),
        P(None, "joint"),
        P("joint", None),
        P(),
        P("view", None),
        P(),
        P(),
    )
    return jax.shard_map(
        body, mesh=mesh, in_specs=placed, out_specs=P("joint", "view", None, None), check_vma=False
    )
```

```python
import functools

import jax
import jax.numpy as jnp
from jax import lax
from jax.experimental import pallas as pl
from jax.experimental.layout import Layout, with_layout_constraint
from jax.experimental.pallas import tpu as pltpu
from jax.sharding import PartitionSpec as P

HD = 64
LANES = 128
QUAD = 256
norm_eps = 1e-05
MIB = 1024 * 1024
VMEM_MIB = 32
F32 = jnp.float32
BF16 = jnp.bfloat16
LOG2E = 1.4426950408889634


def round_up(value, unit):
    return (value + unit - 1) // unit * unit


def layer_norm(values, gain):
    average = jnp.mean(values, axis=-1, keepdims=True)
    centred = values - average
    spread = jnp.mean(centred * centred, axis=-1, keepdims=True)
    return centred * lax.rsqrt(spread + norm_eps) * gain


def both_halves(joint, own, other):
    low = jnp.where(joint == 0, own, other)
    high = jnp.where(joint == 0, other, own)
    return jnp.concatenate([low, high], axis=1)


def params(limit_mib):
    return pltpu.CompilerParams(vmem_limit_bytes=limit_mib * MIB)


HINT = pl.CostEstimate(flops=1_000_000, bytes_accessed=10_000, transcendentals=0)


def project_kernel(with_query, joints, place_ref, *refs):
    count = 3 if with_query else 2
    halves = 2 if with_query else 3
    tokens, rest = refs[:halves], refs[halves:]
    gain_ref, weights, outs = rest[0], rest[1 : 1 + count], rest[1 + count :]
    views, frames, padded, _ = tokens[0].shape
    joint = place_ref[0]
    gain = gain_ref[...]
    row = lax.broadcasted_iota(jnp.int32, (padded, 1), 0)
    real = row < joints
    pieces = []
    for view in range(views):
        for frame in range(frames):
            own = tokens[0][view, frame].astype(F32)
            other = tokens[1][view, frame].astype(F32)
            if not with_query:
                other = jnp.where(place_ref[1] == 0, other, tokens[2][view, frame].astype(F32))
            normed = layer_norm(both_halves(joint, own, other), gain)
            pieces.append(jnp.where(real, normed, normed[0:1]))
    flat = jnp.concatenate(pieces, axis=0).astype(BF16)
    real = jnp.concatenate([real] * (views * frames), axis=0)
    rows = frames * padded
    width = weights[-1].shape[1]
    keys = jnp.dot(flat, weights[-2][...], preferred_element_type=F32).astype(BF16)
    values = jnp.dot(flat, weights[-1][...], preferred_element_type=F32)
    values = jnp.where(real, values, 0.0).astype(BF16)
    for view in range(views):
        part = slice(view * rows, (view + 1) * rows)
        for quad in range(width // QUAD):
            columns = slice(quad * QUAD, (quad + 1) * QUAD)
            outs[-1][2 * quad, view] = keys[part, columns]
            outs[-1][2 * quad + 1, view] = values[part, columns]
    if with_query:
        query = jnp.dot(flat, weights[0][...], preferred_element_type=F32)
        for view in range(views):
            for frame in range(frames):
                at = (view * frames + frame) * padded
                outs[0][view, frame] = query[at : at + padded].astype(BF16)


def project(place, tokens, gain, weights, joints):
    views, frames, padded, half = tokens[0].shape
    model, width = weights[0].shape
    rows = frames * padded
    with_query = len(weights) == 3
    step = 2 if views % 2 == 0 else 1
    planes = 2 * width // QUAD
    out_shape = [pltpu.HBM((planes, views, rows, QUAD), BF16)]
    out_specs = [pl.BlockSpec((planes, step, rows, QUAD), lambda i, s: (0, i, 0, 0))]
    if with_query:
        out_shape = [pltpu.HBM((views, frames, padded, width), BF16)] + out_shape
        out_specs = [
            pl.BlockSpec((step, frames, padded, width), lambda i, s: (i, 0, 0, 0))
        ] + out_specs
    token = pl.BlockSpec((step, frames, padded, half), lambda i, s: (i, 0, 0, 0))
    weight = pl.BlockSpec((model, width), lambda i, s: (0, 0))
    return pl.pallas_call(
        functools.partial(project_kernel, with_query, joints),
        grid_spec=pltpu.PrefetchScalarGridSpec(
            num_scalar_prefetch=1,
            grid=(views // step,),
            in_specs=[token] * len(tokens)
            + [pl.BlockSpec((1, model), lambda i, s: (0, 0))]
            + [weight] * len(weights),
            out_specs=out_specs,
        ),
        out_shape=out_shape,
        compiler_params=params(VMEM_MIB),
        cost_estimate=HINT,
        name="project",
    )(place, *tokens, gain, *weights)


def attend_kernel(frame, first, begin, joints, place_ref, slot_ref, q_ref, *rest):
    sources, out_ref = rest[:-1], rest[-1]
    views, padded, width = out_ref.shape
    blocks = slot_ref.shape[1]
    rows = sources[0].shape[2]
    queried = place_ref[frame]
    heads = QUAD // HD
    lane = lax.broadcasted_iota(jnp.int32, (1, QUAD), 1)
    column = lax.broadcasted_iota(jnp.int32, (1, blocks * rows), 1)
    real = lax.rem(column, padded) < joints
    scale = HD**-0.5 * LOG2E

    def key_set(plane, slots):
        return jnp.concatenate([sources[0][plane, slot] for slot in slots], axis=0)

    for view in range(views):
        slots = [slot_ref[first + view, block] for block in range(blocks)]
        for quad in range(width // QUAD):
            columns = slice(quad * QUAD, (quad + 1) * QUAD)
            query = q_ref[begin + view, queried, :, columns].astype(F32)
            stacked = jnp.concatenate(
                [jnp.where(lane // HD == head, query, 0.0) for head in range(heads)], axis=0
            ).astype(BF16)
            scores = lax.dot_general(
                stacked,
                key_set(2 * quad, slots),
                (((1,), (1,)), ((), ())),
                preferred_element_type=F32,
            )
            top = jnp.max(scores, axis=1, keepdims=True)
            powers = jnp.exp2((scores - top) * scale)
            weight = jnp.sum(jnp.where(real, powers, 0.0), axis=1, keepdims=True)
            found = jnp.dot(
                powers.astype(BF16), key_set(2 * quad + 1, slots), preferred_element_type=F32
            )
            found = found / weight
            total = found[:padded]
            for head in range(1, heads):
                part = found[head * padded : (head + 1) * padded]
                total = jnp.where(lane // HD == head, part, total)
            out_ref[view, :, columns] = total.astype(BF16)


def attend(place, frame, slots, first, query, begin, views, sources, joints):
    _, _, padded, width = query.shape
    scalars = pl.BlockSpec(memory_space=pltpu.SMEM)
    arrays = pl.BlockSpec(memory_space=pltpu.VMEM)
    return pl.pallas_call(
        functools.partial(attend_kernel, frame, first, begin, joints),
        in_specs=[scalars, scalars] + [arrays] * (1 + len(sources)),
        out_specs=arrays,
        out_shape=jax.ShapeDtypeStruct((views, padded, width), BF16),
        compiler_params=params(VMEM_MIB),
        cost_estimate=HINT,
        name="attend",
    )(place, slots, query, *sources)


def graph_kernel(packed, place_ref, *refs):
    mine_ref, theirs_ref, own_ref, other_ref, w_mine_ref, w_got_ref, w_shared_ref = refs[:7]
    gain_ref, skeleton_ref, degree_ref, w_graph_ref, *outs = refs[7:]
    views, padded, width = mine_ref.shape
    joint, core = place_ref[0], place_ref[1]
    model = w_graph_ref.shape[0]
    gain = gain_ref[...]

    def rows_of(ref):
        pieces = [ref[view].astype(F32) for view in range(views)]
        return jnp.concatenate(pieces, axis=0).astype(BF16)

    mine, theirs = rows_of(mine_ref), rows_of(theirs_ref)
    w_low = jnp.where(core == 0, w_got_ref[...], w_shared_ref[...])
    w_high = jnp.where(core == 0, w_shared_ref[...], w_got_ref[...])
    projected = (
        jnp.dot(mine, w_mine_ref[...], preferred_element_type=F32)
        + jnp.dot(theirs[:, : width // 2], w_low, preferred_element_type=F32)
        + jnp.dot(theirs[:, width // 2 :], w_high, preferred_element_type=F32)
    )
    hiddens, mixed = [], []
    for view in range(views):
        own, other = own_ref[view, 0].astype(F32), other_ref[view, 0].astype(F32)
        part = projected[view * padded : (view + 1) * padded]
        hidden = (both_halves(joint, own, other) + part).astype(BF16).astype(F32)
        normed = layer_norm(hidden, gain).astype(BF16)
        summed = jnp.dot(skeleton_ref[...], normed, preferred_element_type=F32)
        hiddens.append(hidden)
        mixed.append(summed / degree_ref[...])
    skeletal = jnp.concatenate(mixed, axis=0).astype(BF16)
    graph = jnp.dot(skeletal, w_graph_ref[...], preferred_element_type=F32)
    first = lax.broadcasted_iota(jnp.int32, (1, LANES), 1) < LANES // 2
    for view in range(views):
        term = graph[view * padded : (view + 1) * padded]
        if not packed:
            outs[0][view] = hiddens[view].astype(BF16)
            outs[1][view] = term.astype(BF16)
            continue
        for tile in range(model // LANES):
            columns = slice(tile * LANES, (tile + 1) * LANES)
            kept = hiddens[view][:, columns]
            turned = pltpu.roll(term[:, columns], LANES // 2, axis=1)
            outs[0][2 * tile, view] = jnp.where(first, kept, turned).astype(BF16)
            outs[0][2 * tile + 1, view] = jnp.where(first, turned, kept).astype(BF16)


def graph_part(packed, place, mine, theirs, own, other, begin, held):
    views, padded, width = mine.shape
    half = own.shape[3]
    model = held[-1].shape[0]
    heads = pl.BlockSpec((views, padded, width), lambda i, j: (0, 0, 0))
    token = pl.BlockSpec((views, 1, padded, half), lambda i, j: (begin // views, j[0], 0, 0))
    if packed:
        devices = 2 * model // LANES
        out_shape = [pltpu.HBM((devices, views, padded, LANES), BF16)]
        out_specs = [pl.BlockSpec((devices, views, padded, LANES), lambda i, j: (0, 0, 0, 0))]
    else:
        out_shape = [jax.ShapeDtypeStruct((views, padded, model), BF16)] * 2
        out_specs = [pl.BlockSpec((views, padded, model), lambda i, j: (0, 0, 0))] * 2
    return pl.pallas_call(
        functools.partial(graph_kernel, packed),
        grid_spec=pltpu.PrefetchScalarGridSpec(
            num_scalar_prefetch=1,
            grid=(1,),
            in_specs=[heads, heads, token, token]
            + [pl.BlockSpec(a.shape, lambda i, j: (0, 0)) for a in held],
            out_specs=out_specs,
        ),
        out_shape=out_shape,
        compiler_params=params(VMEM_MIB),
        cost_estimate=HINT,
        name="graph_part",
    )(place, mine, theirs, own, other, *held)


def mix_kernel(share, count, order_ref, *rest):
    parts, (counts_ref, kept_ref, *earlier, out_ref, wide) = rest[:count], rest[count:]
    rows, channels, _ = out_ref.shape
    views = 0
    for part in parts:
        block = part[...].astype(F32).reshape(part.shape[0] * rows, LANES)
        wide[views * rows : views * rows + block.shape[0]] = block
        views += part.shape[0]
    counts, keeper = counts_ref[...], kept_ref[...]
    flipped = order_ref[0] == 1
    for row in range(rows):
        lanes_first = wide[pl.ds(row, views, stride=rows), :].T
        low, high = lanes_first[:channels], lanes_first[channels:]
        term = jnp.where(flipped, low, high).astype(BF16)
        kept = jnp.where(flipped, high, low).astype(BF16)
        total = jnp.dot(kept, keeper, preferred_element_type=F32)
        total = total + jnp.dot(term, counts, preferred_element_type=F32) * share
        if earlier:
            total = total + earlier[0][row]
        out_ref[row] = total.astype(out_ref.dtype)


def mix(order, parts, counts, keeper, earlier, last, joints, share):
    parts = [part.reshape(-1, *part.shape[2:]) for part in parts]
    views, num_views = counts.shape
    padded = parts[0].shape[1]
    channels = LANES // 2
    rows = 16
    block = pl.BlockSpec((rows, channels, num_views), lambda i, s: (i, 0, 0))
    held = pl.BlockSpec(counts.shape, lambda i, s: (0, 0))
    return pl.pallas_call(
        functools.partial(mix_kernel, share, len(parts)),
        grid_spec=pltpu.PrefetchScalarGridSpec(
            num_scalar_prefetch=1,
            grid=(pl.cdiv(joints, rows),),
            in_specs=[
                pl.BlockSpec((part.shape[0], rows, LANES), lambda i, s: (0, i, 0))
                for part in parts
            ]
            + [held, held]
            + [block] * len(earlier),
            out_specs=block,
            scratch_shapes=[pltpu.VMEM((views * rows, LANES), F32)],
        ),
        out_shape=jax.ShapeDtypeStruct((joints, channels, num_views), BF16 if last else F32),
        compiler_params=params(VMEM_MIB),
        cost_estimate=HINT,
        name="mix",
    )(order, *parts, counts, keeper, *earlier)


def body(
    pose_tokens,
    gain_attn,
    gain_graph,
    w_query,
    w_key,
    w_value,
    w_out,
    w_graph,
    partners,
    parents,
    view_links,
):
    views_dev, frames, joints, half_width = pose_tokens.shape
    model = w_graph.shape[0]
    devices = lax.axis_size("view")
    place = lax.axis_index("view").astype(jnp.int32)
    joint_place = lax.axis_index("joint").astype(jnp.int32)
    num_views = devices * views_dev
    channels = model // devices
    padded = round_up(joints, 8)
    rows = frames * padded
    if views_dev == 8:
        chunks = ((0, 4), (4, 4))
        tail = ((0, 0, 2), (0, 2, 2), (1, 0, 4))
    else:
        chunks = ((0, views_dev),)
        tail = ((0, 0, views_dev),)
    packed = 2 * channels == LANES and num_views == LANES
    swap = [(0, 1), (1, 0)]
    up = [(i, (i + 1) % devices) for i in range(devices)]
    down = [(j, i) for i, j in up]
    swap_even = [(2 * v + j, 2 * v + 1 - j) for v in range(0, devices, 2) for j in (0, 1)]
    to_odd = [(2 * v + j, 2 * v + 2 + j) for v in range(0, devices, 2) for j in (0, 1)]
    gain_attn = gain_attn.reshape(1, model)
    gain_graph = gain_graph.reshape(1, model)
    where = jnp.stack((joint_place, lax.rem(place, 2), 1 - joint_place))

    to_other_core = [(v, v ^ 1) for v in range(devices)]

    def tied(array, *others):
        return lax.optimization_barrier((array, *others))[0]

    own = []
    for begin, count in chunks:
        part = lax.slice_in_dim(pose_tokens, begin, begin + count)
        part = jnp.pad(part, ((0, 0), (0, 0), (0, padded - joints), (0, 0)))
        own.append(with_layout_constraint(part, Layout(major_to_minor=(0, 1, 2, 3))))

    near = [lax.ppermute(part, "view", up) for part in own]
    other, query, here, after = [], [], [], []
    for c in range(len(chunks)):
        other.append(lax.ppermute(own[c], "joint", swap))
        part = tied(other[c], *near)
        q, kv = project(where, (own[c], part), gain_attn, (w_query, w_key, w_value), joints)
        query.append(q)
        here.append(kv)
        after.append(lax.ppermute(kv, "view", down))
    before = []
    for c in range(len(chunks)):
        far = lax.ppermute(
            tied(near[c], other[-1], here[0]), ("view", "joint"), swap_even
        )
        far_odd = lax.ppermute(tied(other[c], here[0]), ("view", "joint"), to_odd)
        (kv,) = project(where, (near[c], far, far_odd), gain_attn, (w_key, w_value), joints)
        before.append(kv)
    window = [jnp.concatenate(before + here + after, axis=1)]

    w_rows = w_out.shape[0] // 2
    w_part = lax.dynamic_slice_in_dim(w_out, lax.rem(place, 2) * w_rows, w_rows, 0)
    w_part = tied(w_part, far)
    w_got = lax.ppermute(w_part, "joint", swap)
    w_shared = lax.ppermute(w_got, "view", to_other_core)

    first_view = place * views_dev
    own_slot = jnp.arange(views_dev, dtype=jnp.int32)[:, None] + views_dev
    slots = jnp.concatenate(
        (own_slot, jnp.mod(partners - first_view + views_dev, num_views)), axis=1
    )
    slots = jnp.clip(slots, 0, 3 * views_dev - 1)

    joint_ids = jnp.arange(padded, dtype=jnp.int32)
    line = jnp.concatenate((parents, jnp.full((padded - joints,), -1, jnp.int32)))
    skeleton = (
        (joint_ids[:, None] == joint_ids[None, :]).astype(F32)
        + (joint_ids[None, :] == line[:, None]).astype(F32)
        + (joint_ids[:, None] == line[None, :]).astype(F32)
    )
    degree = jnp.sum(skeleton, axis=1, keepdims=True)
    skeleton = skeleton.astype(BF16)
    held = (w_out, w_got, w_shared, gain_graph, skeleton, degree, w_graph)
    sent = []
    for c, begin, count in tail:
        first = chunks[c][0] + begin
        q = query[c]
        if sent:
            q = tied(q, sent[-1][0])
        theirs = attend(where, 2, slots, first, q, begin, count, window, joints)
        q = tied(q, theirs)
        moved = lax.ppermute(theirs, "joint", swap)
        mine = attend(where, 0, slots, first, q, begin, count, window, joints)
        sent.append(graph_part(packed, where, mine, moved, own[c], other[c], begin, held))

    view_ids = jnp.arange(num_views, dtype=jnp.int32)
    counts = (view_ids[:, None] == view_ids[None, :]).astype(F32)
    counts = counts + jnp.sum(
        (view_links[:, :, None] == view_ids[None, None, :]).astype(F32), axis=1
    )
    share = 1.0 / (view_links.shape[1] + 1)
    if packed:
        order = lax.rem(place, 2).reshape(1)
        parts = [
            lax.all_to_all(part, "view", split_axis=0, concat_axis=0, tiled=True)
            for (part,) in sent
        ]
        at = [(chunks[c][0] + begin, count) for c, begin, count in tail]
        groups = (range(len(tail) - 1), range(len(tail) - 1, len(tail)))

        def rows_of(matrix, group):
            matrix = matrix.reshape(devices, views_dev, num_views)
            pieces = [
                matrix[:, at[k][0] : at[k][0] + at[k][1]].reshape(-1, num_views) for k in group
            ]
            return jnp.concatenate(pieces, axis=0).astype(BF16)

        total = ()
        for group in groups if len(tail) > 1 else groups[1:]:
            total = (
                mix(
                    order,
                    [parts[k] for k in group],
                    rows_of(counts.T, group),
                    rows_of(jnp.eye(num_views), group),
                    total,
                    group[-1] == len(tail) - 1,
                    joints,
                    share,
                ),
            )
        return jnp.transpose(total[0], (1, 0, 2))[None]

    hidden = jnp.concatenate([part[0] for part in sent], axis=0)[:, :joints]
    graph_term = jnp.concatenate([part[1] for part in sent], axis=0)[:, :joints]
    residual = jnp.transpose(hidden, (2, 1, 0))
    graph_term = jnp.transpose(graph_term, (2, 1, 0))
    residual = lax.all_to_all(residual, "view", split_axis=0, concat_axis=2, tiled=True)
    graph_term = lax.all_to_all(graph_term, "view", split_axis=0, concat_axis=2, tiled=True)
    mixed = jnp.einsum(
        "cjv,wv->cjw", graph_term, counts.astype(BF16), preferred_element_type=F32
    )
    return (residual.astype(F32) + mixed * share).astype(BF16)[None]


def solution(mesh):
    placed = (
        P("view", None, None, "joint"),
        P(),
        P(),
        P(None, "joint"),
        P(None, "joint"),
        P(None, "joint"),
        P("joint", None),
        P(),
        P("view", None),
        P(),
        P(),
    )
    return jax.shard_map(
        body, mesh=mesh, in_specs=placed, out_specs=P("joint", "view", None, None), check_vma=False
    )
```

```python
import functools

import jax
import jax.numpy as jnp
from jax import lax
from jax.experimental import pallas as pl
from jax.experimental.layout import Layout, with_layout_constraint
from jax.experimental.pallas import tpu as pltpu
from jax.sharding import PartitionSpec as P

HD = 64
LANES = 128
QUAD = 256
norm_eps = 1e-05
MIB = 1024 * 1024
VMEM_MIB = 16
ATTEND_MIB = 24
F32 = jnp.float32
BF16 = jnp.bfloat16
LOG2E = 1.4426950408889634


def round_up(value, unit):
    return (value + unit - 1) // unit * unit


def layer_norm(values, gain):
    average = jnp.mean(values, axis=-1, keepdims=True)
    centred = values - average
    spread = jnp.mean(centred * centred, axis=-1, keepdims=True)
    return centred * lax.rsqrt(spread + norm_eps) * gain


def both_halves(joint, own, other):
    low = jnp.where(joint == 0, own, other)
    high = jnp.where(joint == 0, other, own)
    return jnp.concatenate([low, high], axis=1)


def params(limit_mib):
    return pltpu.CompilerParams(vmem_limit_bytes=limit_mib * MIB)


HINT = pl.CostEstimate(flops=1_000_000, bytes_accessed=10_000, transcendentals=0)


def project_kernel(with_query, joints, place_ref, *refs):
    count = 3 if with_query else 2
    halves = 2 if with_query else 3
    tokens, rest = refs[:halves], refs[halves:]
    gain_ref, weights, outs = rest[0], rest[1 : 1 + count], rest[1 + count :]
    views, frames, padded, _ = tokens[0].shape
    joint = place_ref[0]
    gain = gain_ref[...]
    row = lax.broadcasted_iota(jnp.int32, (padded, 1), 0)
    real = row < joints
    pieces = []
    for view in range(views):
        for frame in range(frames):
            own = tokens[0][view, frame].astype(F32)
            other = tokens[1][view, frame].astype(F32)
            if not with_query:
                other = jnp.where(place_ref[1] == 0, other, tokens[2][view, frame].astype(F32))
            normed = layer_norm(both_halves(joint, own, other), gain)
            pieces.append(jnp.where(real, normed, normed[0:1]))
    flat = jnp.concatenate(pieces, axis=0).astype(BF16)
    real = jnp.concatenate([real] * (views * frames), axis=0)
    rows = frames * padded
    width = weights[-1].shape[1]
    keys = jnp.dot(flat, weights[-2][...], preferred_element_type=F32).astype(BF16)
    values = jnp.dot(flat, weights[-1][...], preferred_element_type=F32)
    values = jnp.where(real, values, 0.0).astype(BF16)
    for view in range(views):
        part = slice(view * rows, (view + 1) * rows)
        for quad in range(width // QUAD):
            columns = slice(quad * QUAD, (quad + 1) * QUAD)
            outs[-1][2 * quad, view] = keys[part, columns]
            outs[-1][2 * quad + 1, view] = values[part, columns]
    if with_query:
        query = jnp.dot(flat, weights[0][...], preferred_element_type=F32)
        for view in range(views):
            for frame in range(frames):
                at = (view * frames + frame) * padded
                outs[0][view, frame] = query[at : at + padded].astype(BF16)


def project(place, tokens, begins, views, gain, weights, joints):
    _, frames, padded, half = tokens[0].shape
    model, width = weights[0].shape
    rows = frames * padded
    with_query = len(weights) == 3
    step = 2 if views % 2 == 0 else 1
    planes = 2 * width // QUAD
    out_shape = [pltpu.HBM((planes, views, rows, QUAD), BF16)]
    out_specs = [pl.BlockSpec((planes, step, rows, QUAD), lambda i, s: (0, i, 0, 0))]
    if with_query:
        out_shape = [pltpu.HBM((views, frames, padded, width), BF16)] + out_shape
        out_specs = [
            pl.BlockSpec((step, frames, padded, width), lambda i, s: (i, 0, 0, 0))
        ] + out_specs

    def token(begin):
        return pl.BlockSpec(
            (step, frames, padded, half), lambda i, s: (begin // step + i, 0, 0, 0)
        )

    weight = pl.BlockSpec((model, width), lambda i, s: (0, 0))
    return pl.pallas_call(
        functools.partial(project_kernel, with_query, joints),
        grid_spec=pltpu.PrefetchScalarGridSpec(
            num_scalar_prefetch=1,
            grid=(views // step,),
            in_specs=[token(begin) for begin in begins]
            + [pl.BlockSpec((1, model), lambda i, s: (0, 0))]
            + [weight] * len(weights),
            out_specs=out_specs,
        ),
        out_shape=out_shape,
        compiler_params=params(VMEM_MIB),
        cost_estimate=HINT,
        name="project",
    )(place, *tokens, gain, *weights)


def attend_kernel(frame, first, begin, joints, place_ref, slot_ref, q_ref, *rest):
    sources, out_ref = rest[:-1], rest[-1]
    views, padded, width = out_ref.shape
    blocks = slot_ref.shape[1]
    rows = sources[0].shape[2]
    queried = place_ref[frame]
    heads = QUAD // HD
    lane = lax.broadcasted_iota(jnp.int32, (1, QUAD), 1)
    column = lax.broadcasted_iota(jnp.int32, (1, blocks * rows), 1)
    real = lax.rem(column, padded) < joints
    scale = HD**-0.5 * LOG2E

    def key_set(plane, slots):
        return jnp.concatenate([sources[0][plane, slot] for slot in slots], axis=0)

    for view in range(views):
        slots = [slot_ref[first + view, block] for block in range(blocks)]
        for quad in range(width // QUAD):
            columns = slice(quad * QUAD, (quad + 1) * QUAD)
            query = q_ref[begin + view, queried, :, columns].astype(F32)
            stacked = jnp.concatenate(
                [jnp.where(lane // HD == head, query, 0.0) for head in range(heads)], axis=0
            ).astype(BF16)
            scores = lax.dot_general(
                stacked,
                key_set(2 * quad, slots),
                (((1,), (1,)), ((), ())),
                preferred_element_type=F32,
            )
            top = jnp.max(scores, axis=1, keepdims=True)
            powers = jnp.exp2((scores - top) * scale)
            weight = jnp.sum(jnp.where(real, powers, 0.0), axis=1, keepdims=True)
            found = jnp.dot(
                powers.astype(BF16), key_set(2 * quad + 1, slots), preferred_element_type=F32
            )
            found = found / weight
            total = found[:padded]
            for head in range(1, heads):
                part = found[head * padded : (head + 1) * padded]
                total = jnp.where(lane // HD == head, part, total)
            out_ref[view, :, columns] = total.astype(BF16)


def attend(place, frame, slots, first, query, begin, views, sources, joints):
    _, _, padded, width = query.shape
    scalars = pl.BlockSpec(memory_space=pltpu.SMEM)
    arrays = pl.BlockSpec(memory_space=pltpu.VMEM)
    return pl.pallas_call(
        functools.partial(attend_kernel, frame, first, begin, joints),
        in_specs=[scalars, scalars] + [arrays] * (1 + len(sources)),
        out_specs=arrays,
        out_shape=jax.ShapeDtypeStruct((views, padded, width), BF16),
        compiler_params=params(ATTEND_MIB),
        cost_estimate=HINT,
        name="attend",
    )(place, slots, query, *sources)


def graph_kernel(packed, place_ref, *refs):
    mine_ref, theirs_ref, own_ref, other_ref, w_mine_ref, w_got_ref, w_shared_ref = refs[:7]
    gain_ref, skeleton_ref, degree_ref, w_graph_ref, *outs = refs[7:]
    views, padded, width = mine_ref.shape
    joint, core = place_ref[0], place_ref[1]
    model = w_graph_ref.shape[0]
    gain = gain_ref[...]

    def rows_of(ref):
        pieces = [ref[view].astype(F32) for view in range(views)]
        return jnp.concatenate(pieces, axis=0).astype(BF16)

    mine, theirs = rows_of(mine_ref), rows_of(theirs_ref)
    w_low = jnp.where(core == 0, w_got_ref[...], w_shared_ref[...])
    w_high = jnp.where(core == 0, w_shared_ref[...], w_got_ref[...])
    projected = (
        jnp.dot(mine, w_mine_ref[...], preferred_element_type=F32)
        + jnp.dot(theirs[:, : width // 2], w_low, preferred_element_type=F32)
        + jnp.dot(theirs[:, width // 2 :], w_high, preferred_element_type=F32)
    )
    hiddens, mixed = [], []
    for view in range(views):
        own, other = own_ref[view, 0].astype(F32), other_ref[view, 0].astype(F32)
        part = projected[view * padded : (view + 1) * padded]
        hidden = (both_halves(joint, own, other) + part).astype(BF16).astype(F32)
        normed = layer_norm(hidden, gain).astype(BF16)
        summed = jnp.dot(skeleton_ref[...], normed, preferred_element_type=F32)
        hiddens.append(hidden)
        mixed.append(summed / degree_ref[...])
    skeletal = jnp.concatenate(mixed, axis=0).astype(BF16)
    graph = jnp.dot(skeletal, w_graph_ref[...], preferred_element_type=F32)
    first = lax.broadcasted_iota(jnp.int32, (1, LANES), 1) < LANES // 2
    for view in range(views):
        term = graph[view * padded : (view + 1) * padded]
        if not packed:
            outs[0][view] = hiddens[view].astype(BF16)
            outs[1][view] = term.astype(BF16)
            continue
        for tile in range(model // LANES):
            columns = slice(tile * LANES, (tile + 1) * LANES)
            kept = hiddens[view][:, columns]
            turned = pltpu.roll(term[:, columns], LANES // 2, axis=1)
            outs[0][2 * tile, view] = jnp.where(first, kept, turned).astype(BF16)
            outs[0][2 * tile + 1, view] = jnp.where(first, turned, kept).astype(BF16)


def graph_part(packed, place, mine, theirs, own, other, begin, held):
    views, padded, width = mine.shape
    half = own.shape[3]
    model = held[-1].shape[0]
    heads = pl.BlockSpec((views, padded, width), lambda i, j: (0, 0, 0))
    token = pl.BlockSpec((views, 1, padded, half), lambda i, j: (begin // views, j[0], 0, 0))
    if packed:
        devices = 2 * model // LANES
        out_shape = [pltpu.HBM((devices, views, padded, LANES), BF16)]
        out_specs = [pl.BlockSpec((devices, views, padded, LANES), lambda i, j: (0, 0, 0, 0))]
    else:
        out_shape = [jax.ShapeDtypeStruct((views, padded, model), BF16)] * 2
        out_specs = [pl.BlockSpec((views, padded, model), lambda i, j: (0, 0, 0))] * 2
    return pl.pallas_call(
        functools.partial(graph_kernel, packed),
        grid_spec=pltpu.PrefetchScalarGridSpec(
            num_scalar_prefetch=1,
            grid=(1,),
            in_specs=[heads, heads, token, token]
            + [pl.BlockSpec(a.shape, lambda i, j: (0, 0)) for a in held],
            out_specs=out_specs,
        ),
        out_shape=out_shape,
        compiler_params=params(VMEM_MIB),
        cost_estimate=HINT,
        name="graph_part",
    )(place, mine, theirs, own, other, *held)


def mix_kernel(share, count, order_ref, *rest):
    parts, (counts_ref, kept_ref, *earlier, out_ref, wide) = rest[:count], rest[count:]
    rows, channels, _ = out_ref.shape
    views = 0
    for part in parts:
        block = part[...].astype(F32).reshape(part.shape[0] * rows, LANES)
        wide[views * rows : views * rows + block.shape[0]] = block
        views += part.shape[0]
    counts, keeper = counts_ref[...], kept_ref[...]
    flipped = order_ref[0] == 1
    for row in range(rows):
        lanes_first = wide[pl.ds(row, views, stride=rows), :].T
        low, high = lanes_first[:channels], lanes_first[channels:]
        term = jnp.where(flipped, low, high).astype(BF16)
        kept = jnp.where(flipped, high, low).astype(BF16)
        total = jnp.dot(kept, keeper, preferred_element_type=F32)
        total = total + jnp.dot(term, counts, preferred_element_type=F32) * share
        if earlier:
            total = total + earlier[0][row]
        out_ref[row] = total.astype(out_ref.dtype)


def mix(order, parts, counts, keeper, earlier, last, joints, share):
    parts = [part.reshape(-1, *part.shape[2:]) for part in parts]
    views, num_views = counts.shape
    padded = parts[0].shape[1]
    channels = LANES // 2
    rows = 16
    block = pl.BlockSpec((rows, channels, num_views), lambda i, s: (i, 0, 0))
    held = pl.BlockSpec(counts.shape, lambda i, s: (0, 0))
    return pl.pallas_call(
        functools.partial(mix_kernel, share, len(parts)),
        grid_spec=pltpu.PrefetchScalarGridSpec(
            num_scalar_prefetch=1,
            grid=(pl.cdiv(joints, rows),),
            in_specs=[
                pl.BlockSpec((part.shape[0], rows, LANES), lambda i, s: (0, i, 0))
                for part in parts
            ]
            + [held, held]
            + [block] * len(earlier),
            out_specs=block,
            scratch_shapes=[pltpu.VMEM((views * rows, LANES), F32)],
        ),
        out_shape=jax.ShapeDtypeStruct((joints, channels, num_views), BF16 if last else F32),
        compiler_params=params(VMEM_MIB),
        cost_estimate=HINT,
        name="mix",
    )(order, *parts, counts, keeper, *earlier)


def body(
    pose_tokens,
    gain_attn,
    gain_graph,
    w_query,
    w_key,
    w_value,
    w_out,
    w_graph,
    partners,
    parents,
    view_links,
):
    views_dev, frames, joints, half_width = pose_tokens.shape
    model = w_graph.shape[0]
    devices = lax.axis_size("view")
    place = lax.axis_index("view").astype(jnp.int32)
    joint_place = lax.axis_index("joint").astype(jnp.int32)
    num_views = devices * views_dev
    channels = model // devices
    padded = round_up(joints, 8)
    rows = frames * padded
    if views_dev == 8:
        chunks = ((0, 4), (4, 4))
        tail = ((0, 0, 2), (0, 2, 2), (1, 0, 4))
    else:
        chunks = ((0, views_dev),)
        tail = ((0, 0, views_dev),)
    packed = 2 * channels == LANES and num_views == LANES
    swap = [(0, 1), (1, 0)]
    up = [(i, (i + 1) % devices) for i in range(devices)]
    down = [(j, i) for i, j in up]
    swap_even = [(2 * v + j, 2 * v + 1 - j) for v in range(0, devices, 2) for j in (0, 1)]
    to_odd = [(2 * v + j, 2 * v + 2 + j) for v in range(0, devices, 2) for j in (0, 1)]
    gain_attn = gain_attn.reshape(1, model)
    gain_graph = gain_graph.reshape(1, model)
    where = jnp.stack((joint_place, lax.rem(place, 2), 1 - joint_place))

    to_other_core = [(v, v ^ 1) for v in range(devices)]

    def tied(array, *others):
        return lax.optimization_barrier((array, *others))[0]

    own = []
    for begin, count in chunks:
        part = lax.slice_in_dim(pose_tokens, begin, begin + count)
        part = jnp.pad(part, ((0, 0), (0, 0), (0, padded - joints), (0, 0)))
        own.append(with_layout_constraint(part, Layout(major_to_minor=(0, 1, 2, 3))))

    near = [lax.ppermute(part, "view", up) for part in own]
    other, query, here, after = [], [], [], []
    for c in range(len(chunks)):
        other.append(lax.ppermute(own[c], "joint", swap))
        part = tied(other[c], near[c])
        q, kv = project(
            where, (own[c], part), (0, 0), chunks[c][1], gain_attn, (w_query, w_key, w_value), joints
        )
        query.append(q)
        here.append(kv)
        after.append(lax.ppermute(kv, "view", down))
    far = lax.ppermute(
        tied(jnp.concatenate(near, axis=0), other[-1], here[0]), ("view", "joint"), swap_even
    )
    before = []
    for c, (begin, count) in enumerate(chunks):
        far_odd = lax.ppermute(tied(other[c], here[0]), ("view", "joint"), to_odd)
        (kv,) = project(
            where,
            (near[c], far, far_odd),
            (0, begin, 0),
            count,
            gain_attn,
            (w_key, w_value),
            joints,
        )
        before.append(kv)
    window = [jnp.concatenate(here + after + before, axis=1)]

    w_rows = w_out.shape[0] // 2
    w_part = lax.dynamic_slice_in_dim(w_out, lax.rem(place, 2) * w_rows, w_rows, 0)
    w_part = tied(w_part, far)
    w_got = lax.ppermute(w_part, "joint", swap)
    w_shared = lax.ppermute(w_got, "view", to_other_core)

    first_view = place * views_dev
    ahead = jnp.mod(partners - first_view, num_views)
    ahead = jnp.where(ahead >= num_views - views_dev, ahead - num_views + 3 * views_dev, ahead)
    own_slot = jnp.arange(views_dev, dtype=jnp.int32)[:, None]
    slots = jnp.concatenate((own_slot, ahead), axis=1)
    slots = jnp.clip(slots, 0, 3 * views_dev - 1)

    joint_ids = jnp.arange(padded, dtype=jnp.int32)
    line = jnp.concatenate((parents, jnp.full((padded - joints,), -1, jnp.int32)))
    skeleton = (
        (joint_ids[:, None] == joint_ids[None, :]).astype(F32)
        + (joint_ids[None, :] == line[:, None]).astype(F32)
        + (joint_ids[:, None] == line[None, :]).astype(F32)
    )
    degree = jnp.sum(skeleton, axis=1, keepdims=True)
    skeleton = skeleton.astype(BF16)
    held = (w_out, w_got, w_shared, gain_graph, skeleton, degree, w_graph)
    sent = []
    for c, begin, count in tail:
        first = chunks[c][0] + begin
        q = query[c]
        if sent:
            q = tied(q, sent[-1][0])
        theirs = attend(where, 2, slots, first, q, begin, count, window, joints)
        q = tied(q, theirs)
        moved = lax.ppermute(theirs, "joint", swap)
        mine = attend(where, 0, slots, first, q, begin, count, window, joints)
        sent.append(graph_part(packed, where, mine, moved, own[c], other[c], begin, held))

    view_ids = jnp.arange(num_views, dtype=jnp.int32)
    counts = (view_ids[:, None] == view_ids[None, :]).astype(F32)
    counts = counts + jnp.sum(
        (view_links[:, :, None] == view_ids[None, None, :]).astype(F32), axis=1
    )
    share = 1.0 / (view_links.shape[1] + 1)
    if packed:
        order = lax.rem(place, 2).reshape(1)
        parts = [
            lax.all_to_all(part, "view", split_axis=0, concat_axis=0, tiled=True)
            for (part,) in sent
        ]
        at = [(chunks[c][0] + begin, count) for c, begin, count in tail]
        groups = (range(len(tail) - 1), range(len(tail) - 1, len(tail)))

        def rows_of(matrix, group):
            matrix = matrix.reshape(devices, views_dev, num_views)
            pieces = [
                matrix[:, at[k][0] : at[k][0] + at[k][1]].reshape(-1, num_views) for k in group
            ]
            return jnp.concatenate(pieces, axis=0).astype(BF16)

        total = ()
        for group in groups if len(tail) > 1 else groups[1:]:
            total = (
                mix(
                    order,
                    [parts[k] for k in group],
                    rows_of(counts.T, group),
                    rows_of(jnp.eye(num_views), group),
                    total,
                    group[-1] == len(tail) - 1,
                    joints,
                    share,
                ),
            )
        return jnp.transpose(total[0], (1, 0, 2))[None]

    hidden = jnp.concatenate([part[0] for part in sent], axis=0)[:, :joints]
    graph_term = jnp.concatenate([part[1] for part in sent], axis=0)[:, :joints]
    residual = jnp.transpose(hidden, (2, 1, 0))
    graph_term = jnp.transpose(graph_term, (2, 1, 0))
    residual = lax.all_to_all(residual, "view", split_axis=0, concat_axis=2, tiled=True)
    graph_term = lax.all_to_all(graph_term, "view", split_axis=0, concat_axis=2, tiled=True)
    mixed = jnp.einsum(
        "cjv,wv->cjw", graph_term, counts.astype(BF16), preferred_element_type=F32
    )
    return (residual.astype(F32) + mixed * share).astype(BF16)[None]


def solution(mesh):
    placed = (
        P("view", None, None, "joint"),
        P(),
        P(),
        P(None, "joint"),
        P(None, "joint"),
        P(None, "joint"),
        P("joint", None),
        P(),
        P("view", None),
        P(),
        P(),
    )
    return jax.shard_map(
        body, mesh=mesh, in_specs=placed, out_specs=P("joint", "view", None, None), check_vma=False
    )
```

```python
import functools

import jax
import jax.numpy as jnp
from jax import lax
from jax.experimental import pallas as pl
from jax.experimental.layout import Layout, with_layout_constraint
from jax.experimental.pallas import tpu as pltpu
from jax.sharding import PartitionSpec as P

HD = 64
LANES = 128
QUAD = 256
norm_eps = 1e-05
MIB = 1024 * 1024
VMEM_MIB = 32
ATTEND_MIB = 60
F32 = jnp.float32
BF16 = jnp.bfloat16
LOG2E = 1.4426950408889634


def round_up(value, unit):
    return (value + unit - 1) // unit * unit


def layer_norm(values, gain):
    average = jnp.mean(values, axis=-1, keepdims=True)
    centred = values - average
    spread = jnp.mean(centred * centred, axis=-1, keepdims=True)
    return centred * lax.rsqrt(spread + norm_eps) * gain


def both_halves(joint, own, other):
    low = jnp.where(joint == 0, own, other)
    high = jnp.where(joint == 0, other, own)
    return jnp.concatenate([low, high], axis=1)


def params(limit_mib):
    return pltpu.CompilerParams(vmem_limit_bytes=limit_mib * MIB)


HINT = pl.CostEstimate(flops=1_000_000, bytes_accessed=10_000, transcendentals=0)


def project_kernel(with_query, joints, place_ref, *refs):
    count = 3 if with_query else 2
    halves = 2 if with_query else 3
    tokens, rest = refs[:halves], refs[halves:]
    gain_ref, weights, outs = rest[0], rest[1 : 1 + count], rest[1 + count :]
    views, frames, padded, _ = tokens[0].shape
    joint = place_ref[0]
    gain = gain_ref[...]
    row = lax.broadcasted_iota(jnp.int32, (padded, 1), 0)
    real = row < joints
    pieces = []
    for view in range(views):
        for frame in range(frames):
            own = tokens[0][view, frame].astype(F32)
            other = tokens[1][view, frame].astype(F32)
            if not with_query:
                other = jnp.where(place_ref[1] == 0, other, tokens[2][view, frame].astype(F32))
            normed = layer_norm(both_halves(joint, own, other), gain)
            pieces.append(jnp.where(real, normed, normed[0:1]))
    flat = jnp.concatenate(pieces, axis=0).astype(BF16)
    real = jnp.concatenate([real] * (views * frames), axis=0)
    rows = frames * padded
    width = weights[-1].shape[1]
    keys = jnp.dot(flat, weights[-2][...], preferred_element_type=F32).astype(BF16)
    values = jnp.dot(flat, weights[-1][...], preferred_element_type=F32)
    values = jnp.where(real, values, 0.0).astype(BF16)
    for view in range(views):
        part = slice(view * rows, (view + 1) * rows)
        for quad in range(width // QUAD):
            columns = slice(quad * QUAD, (quad + 1) * QUAD)
            outs[-1][2 * quad, view] = keys[part, columns]
            outs[-1][2 * quad + 1, view] = values[part, columns]
    if with_query:
        query = jnp.dot(flat, weights[0][...], preferred_element_type=F32)
        for view in range(views):
            for frame in range(frames):
                at = (view * frames + frame) * padded
                outs[0][view, frame] = query[at : at + padded].astype(BF16)


def project(place, tokens, begins, views, gain, weights, joints):
    _, frames, padded, half = tokens[0].shape
    model, width = weights[0].shape
    rows = frames * padded
    with_query = len(weights) == 3
    step = 2 if views % 2 == 0 else 1
    planes = 2 * width // QUAD
    out_shape = [pltpu.HBM((planes, views, rows, QUAD), BF16)]
    out_specs = [pl.BlockSpec((planes, step, rows, QUAD), lambda i, s: (0, i, 0, 0))]
    if with_query:
        out_shape = [pltpu.HBM((views, frames, padded, width), BF16)] + out_shape
        out_specs = [
            pl.BlockSpec((step, frames, padded, width), lambda i, s: (i, 0, 0, 0))
        ] + out_specs

    def token(begin):
        return pl.BlockSpec(
            (step, frames, padded, half), lambda i, s: (begin // step + i, 0, 0, 0)
        )

    weight = pl.BlockSpec((model, width), lambda i, s: (0, 0))
    return pl.pallas_call(
        functools.partial(project_kernel, with_query, joints),
        grid_spec=pltpu.PrefetchScalarGridSpec(
            num_scalar_prefetch=1,
            grid=(views // step,),
            in_specs=[token(begin) for begin in begins]
            + [pl.BlockSpec((1, model), lambda i, s: (0, 0))]
            + [weight] * len(weights),
            out_specs=out_specs,
        ),
        out_shape=out_shape,
        compiler_params=params(VMEM_MIB),
        cost_estimate=HINT,
        name="project",
    )(place, *tokens, gain, *weights)


def attend_kernel(first, joints, place_ref, slot_ref, q_ref, *rest):
    sources = rest[:-3]
    out_ref, keyval, sems = rest[-3:]
    _, padded, width = out_ref.shape
    blocks = slot_ref.shape[1]
    rows = keyval.shape[2] // blocks
    step = pl.program_id(0)
    steps = pl.num_programs(0)
    buffer = lax.rem(step, 2)

    def copy(source, slot, block, buffer):
        return pltpu.make_async_copy(
            source.at[:, slot],
            keyval.at[buffer, :, pl.ds(block * rows, rows)],
            sems.at[buffer, block],
        )

    def fetch(view, buffer):
        for block in range(blocks):
            slot = slot_ref[first + view, block]
            begin = 0
            for source in sources:
                low, begin = begin, begin + source.shape[1]

                @pl.when((slot >= low) & (slot < begin))
                def _():
                    copy(source, slot - low, block, buffer).start()

    @pl.when(step == 0)
    def _():
        fetch(0, 0)

    @pl.when(step + 1 < steps)
    def _():
        fetch(step + 1, 1 - buffer)

    for block in range(blocks):
        copy(sources[0], 0, block, buffer).wait()

    heads = QUAD // HD
    lane = lax.broadcasted_iota(jnp.int32, (1, QUAD), 1)
    column = lax.broadcasted_iota(jnp.int32, (1, blocks * rows), 1)
    real = lax.rem(column, padded) < joints
    scale = HD**-0.5 * LOG2E
    for quad in range(width // QUAD):
        columns = slice(quad * QUAD, (quad + 1) * QUAD)
        query = q_ref[0, 0, :, columns].astype(F32)
        stacked = jnp.concatenate(
            [jnp.where(lane // HD == head, query, 0.0) for head in range(heads)], axis=0
        ).astype(BF16)
        scores = lax.dot_general(
            stacked,
            keyval[buffer, 2 * quad],
            (((1,), (1,)), ((), ())),
            preferred_element_type=F32,
        )
        top = jnp.max(scores, axis=1, keepdims=True)
        powers = jnp.exp2((scores - top) * scale)
        weight = jnp.sum(jnp.where(real, powers, 0.0), axis=1, keepdims=True)
        found = jnp.dot(
            powers.astype(BF16), keyval[buffer, 2 * quad + 1], preferred_element_type=F32
        )
        found = found / weight
        total = found[:padded]
        for head in range(1, heads):
            part = found[head * padded : (head + 1) * padded]
            total = jnp.where(lane // HD == head, part, total)
        out_ref[0, :, columns] = total.astype(BF16)


def attend(place, frame, slots, first, query, begin, views, sources, joints):
    _, _, padded, width = query.shape
    planes, _, rows, _ = sources[0].shape
    blocks = slots.shape[1]
    return pl.pallas_call(
        functools.partial(attend_kernel, first, joints),
        grid_spec=pltpu.PrefetchScalarGridSpec(
            num_scalar_prefetch=2,
            grid=(views,),
            in_specs=[
                pl.BlockSpec((1, 1, padded, width), lambda i, p, s: (begin + i, p[frame], 0, 0))
            ]
            + [pl.BlockSpec(memory_space=pltpu.HBM)] * len(sources),
            out_specs=pl.BlockSpec((1, padded, width), lambda i, p, s: (i, 0, 0)),
            scratch_shapes=[
                pltpu.VMEM((2, planes, blocks * rows, QUAD), BF16),
                pltpu.SemaphoreType.DMA((2, blocks)),
            ],
        ),
        out_shape=pltpu.HBM((views, padded, width), BF16),
        compiler_params=params(ATTEND_MIB),
        cost_estimate=HINT,
        name="attend",
    )(place, slots, query, *sources)


def graph_kernel(packed, place_ref, *refs):
    mine_ref, theirs_ref, own_ref, other_ref, w_mine_ref, w_got_ref, w_shared_ref = refs[:7]
    gain_ref, skeleton_ref, degree_ref, w_graph_ref, *outs = refs[7:]
    views, padded, width = mine_ref.shape
    joint, core = place_ref[0], place_ref[1]
    model = w_graph_ref.shape[0]
    gain = gain_ref[...]

    def rows_of(ref):
        pieces = [ref[view].astype(F32) for view in range(views)]
        return jnp.concatenate(pieces, axis=0).astype(BF16)

    mine, theirs = rows_of(mine_ref), rows_of(theirs_ref)
    w_low = jnp.where(core == 0, w_got_ref[...], w_shared_ref[...])
    w_high = jnp.where(core == 0, w_shared_ref[...], w_got_ref[...])
    projected = (
        jnp.dot(mine, w_mine_ref[...], preferred_element_type=F32)
        + jnp.dot(theirs[:, : width // 2], w_low, preferred_element_type=F32)
        + jnp.dot(theirs[:, width // 2 :], w_high, preferred_element_type=F32)
    )
    hiddens, mixed = [], []
    for view in range(views):
        own, other = own_ref[view, 0].astype(F32), other_ref[view, 0].astype(F32)
        part = projected[view * padded : (view + 1) * padded]
        hidden = (both_halves(joint, own, other) + part).astype(BF16).astype(F32)
        normed = layer_norm(hidden, gain).astype(BF16)
        summed = jnp.dot(skeleton_ref[...], normed, preferred_element_type=F32)
        hiddens.append(hidden)
        mixed.append(summed / degree_ref[...])
    skeletal = jnp.concatenate(mixed, axis=0).astype(BF16)
    graph = jnp.dot(skeletal, w_graph_ref[...], preferred_element_type=F32)
    first = lax.broadcasted_iota(jnp.int32, (1, LANES), 1) < LANES // 2
    for view in range(views):
        term = graph[view * padded : (view + 1) * padded]
        if not packed:
            outs[0][view] = hiddens[view].astype(BF16)
            outs[1][view] = term.astype(BF16)
            continue
        for tile in range(model // LANES):
            columns = slice(tile * LANES, (tile + 1) * LANES)
            kept = hiddens[view][:, columns]
            turned = pltpu.roll(term[:, columns], LANES // 2, axis=1)
            outs[0][2 * tile, view] = jnp.where(first, kept, turned).astype(BF16)
            outs[0][2 * tile + 1, view] = jnp.where(first, turned, kept).astype(BF16)


def graph_part(packed, place, mine, theirs, own, other, begin, held):
    views, padded, width = mine.shape
    half = own.shape[3]
    model = held[-1].shape[0]
    heads = pl.BlockSpec((views, padded, width), lambda i, j: (0, 0, 0))
    token = pl.BlockSpec((views, 1, padded, half), lambda i, j: (begin // views, j[0], 0, 0))
    if packed:
        devices = 2 * model // LANES
        out_shape = [pltpu.HBM((devices, views, padded, LANES), BF16)]
        out_specs = [pl.BlockSpec((devices, views, padded, LANES), lambda i, j: (0, 0, 0, 0))]
    else:
        out_shape = [jax.ShapeDtypeStruct((views, padded, model), BF16)] * 2
        out_specs = [pl.BlockSpec((views, padded, model), lambda i, j: (0, 0, 0))] * 2
    return pl.pallas_call(
        functools.partial(graph_kernel, packed),
        grid_spec=pltpu.PrefetchScalarGridSpec(
            num_scalar_prefetch=1,
            grid=(1,),
            in_specs=[heads, heads, token, token]
            + [pl.BlockSpec(a.shape, lambda i, j: (0, 0)) for a in held],
            out_specs=out_specs,
        ),
        out_shape=out_shape,
        compiler_params=params(VMEM_MIB),
        cost_estimate=HINT,
        name="graph_part",
    )(place, mine, theirs, own, other, *held)


def mix_kernel(share, count, order_ref, *rest):
    parts, (counts_ref, kept_ref, *earlier, out_ref, wide) = rest[:count], rest[count:]
    rows, channels, _ = out_ref.shape
    views = 0
    for part in parts:
        block = part[...].astype(F32).reshape(part.shape[0] * rows, LANES)
        wide[views * rows : views * rows + block.shape[0]] = block
        views += part.shape[0]
    counts, keeper = counts_ref[...], kept_ref[...]
    flipped = order_ref[0] == 1
    for row in range(rows):
        lanes_first = wide[pl.ds(row, views, stride=rows), :].T
        low, high = lanes_first[:channels], lanes_first[channels:]
        term = jnp.where(flipped, low, high).astype(BF16)
        kept = jnp.where(flipped, high, low).astype(BF16)
        total = jnp.dot(kept, keeper, preferred_element_type=F32)
        total = total + jnp.dot(term, counts, preferred_element_type=F32) * share
        if earlier:
            total = total + earlier[0][row]
        out_ref[row] = total.astype(out_ref.dtype)


def mix(order, parts, counts, keeper, earlier, last, joints, share):
    parts = [part.reshape(-1, *part.shape[2:]) for part in parts]
    views, num_views = counts.shape
    padded = parts[0].shape[1]
    channels = LANES // 2
    rows = 16
    block = pl.BlockSpec((rows, channels, num_views), lambda i, s: (i, 0, 0))
    held = pl.BlockSpec(counts.shape, lambda i, s: (0, 0))
    return pl.pallas_call(
        functools.partial(mix_kernel, share, len(parts)),
        grid_spec=pltpu.PrefetchScalarGridSpec(
            num_scalar_prefetch=1,
            grid=(pl.cdiv(joints, rows),),
            in_specs=[
                pl.BlockSpec((part.shape[0], rows, LANES), lambda i, s: (0, i, 0))
                for part in parts
            ]
            + [held, held]
            + [block] * len(earlier),
            out_specs=block,
            scratch_shapes=[pltpu.VMEM((views * rows, LANES), F32)],
        ),
        out_shape=jax.ShapeDtypeStruct((joints, channels, num_views), BF16 if last else F32),
        compiler_params=params(VMEM_MIB),
        cost_estimate=HINT,
        name="mix",
    )(order, *parts, counts, keeper, *earlier)


def body(
    pose_tokens,
    gain_attn,
    gain_graph,
    w_query,
    w_key,
    w_value,
    w_out,
    w_graph,
    partners,
    parents,
    view_links,
):
    views_dev, frames, joints, half_width = pose_tokens.shape
    model = w_graph.shape[0]
    devices = lax.axis_size("view")
    place = lax.axis_index("view").astype(jnp.int32)
    joint_place = lax.axis_index("joint").astype(jnp.int32)
    num_views = devices * views_dev
    channels = model // devices
    padded = round_up(joints, 8)
    rows = frames * padded
    if views_dev == 8:
        chunks = ((0, 4), (4, 4))
        tail = ((0, 0, 4), (1, 0, 4))
    else:
        chunks = ((0, views_dev),)
        tail = ((0, 0, views_dev),)
    packed = 2 * channels == LANES and num_views == LANES
    swap = [(0, 1), (1, 0)]
    up = [(i, (i + 1) % devices) for i in range(devices)]
    down = [(j, i) for i, j in up]
    swap_even = [(2 * v + j, 2 * v + 1 - j) for v in range(0, devices, 2) for j in (0, 1)]
    to_odd = [(2 * v + j, 2 * v + 2 + j) for v in range(0, devices, 2) for j in (0, 1)]
    gain_attn = gain_attn.reshape(1, model)
    gain_graph = gain_graph.reshape(1, model)
    where = jnp.stack((joint_place, lax.rem(place, 2), 1 - joint_place))

    to_other_core = [(v, v ^ 1) for v in range(devices)]

    def tied(array, *others):
        return lax.optimization_barrier((array, *others))[0]

    own = []
    for begin, count in chunks:
        part = lax.slice_in_dim(pose_tokens, begin, begin + count)
        part = jnp.pad(part, ((0, 0), (0, 0), (0, padded - joints), (0, 0)))
        own.append(with_layout_constraint(part, Layout(major_to_minor=(0, 1, 2, 3))))

    near = [lax.ppermute(part, "view", up) for part in own]
    other, query, here, after = [], [], [], []
    for c in range(len(chunks)):
        other.append(lax.ppermute(own[c], "joint", swap))
        part = tied(other[c], *near)
        q, kv = project(
            where, (own[c], part), (0, 0), chunks[c][1], gain_attn, (w_query, w_key, w_value), joints
        )
        query.append(q)
        here.append(kv)
        after.append(lax.ppermute(kv, "view", down))
    before = []
    for c, (begin, count) in enumerate(chunks):
        far = lax.ppermute(
            tied(near[c], other[-1], here[0]), ("view", "joint"), swap_even
        )
        far_odd = lax.ppermute(tied(other[c], here[0]), ("view", "joint"), to_odd)
        (kv,) = project(
            where,
            (near[c], far, far_odd),
            (0, 0, 0),
            count,
            gain_attn,
            (w_key, w_value),
            joints,
        )
        before.append(kv)
    window = here + after + before

    w_rows = w_out.shape[0] // 2
    w_part = lax.dynamic_slice_in_dim(w_out, lax.rem(place, 2) * w_rows, w_rows, 0)
    w_part = tied(w_part, far)
    w_got = lax.ppermute(w_part, "joint", swap)
    w_shared = lax.ppermute(w_got, "view", to_other_core)

    first_view = place * views_dev
    ahead = jnp.mod(partners - first_view, num_views)
    ahead = jnp.where(ahead >= num_views - views_dev, ahead - num_views + 3 * views_dev, ahead)
    own_slot = jnp.arange(views_dev, dtype=jnp.int32)[:, None]
    slots = jnp.concatenate((own_slot, ahead), axis=1)
    slots = jnp.clip(slots, 0, 3 * views_dev - 1)

    joint_ids = jnp.arange(padded, dtype=jnp.int32)
    line = jnp.concatenate((parents, jnp.full((padded - joints,), -1, jnp.int32)))
    skeleton = (
        (joint_ids[:, None] == joint_ids[None, :]).astype(F32)
        + (joint_ids[None, :] == line[:, None]).astype(F32)
        + (joint_ids[:, None] == line[None, :]).astype(F32)
    )
    degree = jnp.sum(skeleton, axis=1, keepdims=True)
    skeleton = skeleton.astype(BF16)
    held = (w_out, w_got, w_shared, gain_graph, skeleton, degree, w_graph)
    sent = []
    for c, begin, count in tail:
        first = chunks[c][0] + begin
        q = query[c]
        if sent:
            q = tied(q, sent[-1][0])
        theirs = attend(where, 2, slots, first, q, begin, count, window, joints)
        q = tied(q, theirs)
        moved = lax.ppermute(theirs, "joint", swap)
        mine = attend(where, 0, slots, first, q, begin, count, window, joints)
        sent.append(graph_part(packed, where, mine, moved, own[c], other[c], begin, held))

    view_ids = jnp.arange(num_views, dtype=jnp.int32)
    counts = (view_ids[:, None] == view_ids[None, :]).astype(F32)
    counts = counts + jnp.sum(
        (view_links[:, :, None] == view_ids[None, None, :]).astype(F32), axis=1
    )
    share = 1.0 / (view_links.shape[1] + 1)
    if packed:
        order = lax.rem(place, 2).reshape(1)
        parts = [
            lax.all_to_all(part, "view", split_axis=0, concat_axis=0, tiled=True)
            for (part,) in sent
        ]
        at = [(chunks[c][0] + begin, count) for c, begin, count in tail]
        groups = (range(len(tail) - 1), range(len(tail) - 1, len(tail)))

        def rows_of(matrix, group):
            matrix = matrix.reshape(devices, views_dev, num_views)
            pieces = [
                matrix[:, at[k][0] : at[k][0] + at[k][1]].reshape(-1, num_views) for k in group
            ]
            return jnp.concatenate(pieces, axis=0).astype(BF16)

        total = ()
        for group in groups if len(tail) > 1 else groups[1:]:
            total = (
                mix(
                    order,
                    [parts[k] for k in group],
                    rows_of(counts.T, group),
                    rows_of(jnp.eye(num_views), group),
                    total,
                    group[-1] == len(tail) - 1,
                    joints,
                    share,
                ),
            )
        return jnp.transpose(total[0], (1, 0, 2))[None]

    hidden = jnp.concatenate([part[0] for part in sent], axis=0)[:, :joints]
    graph_term = jnp.concatenate([part[1] for part in sent], axis=0)[:, :joints]
    residual = jnp.transpose(hidden, (2, 1, 0))
    graph_term = jnp.transpose(graph_term, (2, 1, 0))
    residual = lax.all_to_all(residual, "view", split_axis=0, concat_axis=2, tiled=True)
    graph_term = lax.all_to_all(graph_term, "view", split_axis=0, concat_axis=2, tiled=True)
    mixed = jnp.einsum(
        "cjv,wv->cjw", graph_term, counts.astype(BF16), preferred_element_type=F32
    )
    return (residual.astype(F32) + mixed * share).astype(BF16)[None]


def solution(mesh):
    placed = (
        P("view", None, None, "joint"),
        P(),
        P(),
        P(None, "joint"),
        P(None, "joint"),
        P(None, "joint"),
        P("joint", None),
        P(),
        P("view", None),
        P(),
        P(),
    )
    return jax.shard_map(
        body, mesh=mesh, in_specs=placed, out_specs=P("joint", "view", None, None), check_vma=False
    )
```

```python
import functools

import jax
import jax.numpy as jnp
from jax import lax
from jax.experimental import pallas as pl
from jax.experimental.layout import Layout, with_layout_constraint
from jax.experimental.pallas import tpu as pltpu
from jax.sharding import PartitionSpec as P

HD = 64
LANES = 128
QUAD = 256
norm_eps = 1e-05
MIB = 1024 * 1024
VMEM_MIB = 16
WINDOW_MIB = 24
FULL_MIB = 60
F32 = jnp.float32
BF16 = jnp.bfloat16
LOG2E = 1.4426950408889634


def round_up(value, unit):
    return (value + unit - 1) // unit * unit


def layer_norm(values, gain):
    average = jnp.mean(values, axis=-1, keepdims=True)
    centred = values - average
    spread = jnp.mean(centred * centred, axis=-1, keepdims=True)
    return centred * lax.rsqrt(spread + norm_eps) * gain


def both_halves(joint, own, other):
    low = jnp.where(joint == 0, own, other)
    high = jnp.where(joint == 0, other, own)
    return jnp.concatenate([low, high], axis=1)


def params(limit_mib):
    return pltpu.CompilerParams(vmem_limit_bytes=limit_mib * MIB)


HINT = pl.CostEstimate(flops=1_000_000, bytes_accessed=10_000, transcendentals=0)


def project_kernel(with_query, joints, place_ref, *refs):
    count = 3 if with_query else 2
    halves = 2 if with_query else 3
    tokens, rest = refs[:halves], refs[halves:]
    gain_ref, weights, outs = rest[0], rest[1 : 1 + count], rest[1 + count :]
    views, frames, padded, _ = tokens[0].shape
    joint = place_ref[0]
    gain = gain_ref[...]
    row = lax.broadcasted_iota(jnp.int32, (padded, 1), 0)
    real = row < joints
    pieces = []
    for view in range(views):
        for frame in range(frames):
            own = tokens[0][view, frame].astype(F32)
            other = tokens[1][view, frame].astype(F32)
            if not with_query:
                other = jnp.where(place_ref[1] == 0, other, tokens[2][view, frame].astype(F32))
            normed = layer_norm(both_halves(joint, own, other), gain)
            pieces.append(jnp.where(real, normed, normed[0:1]))
    flat = jnp.concatenate(pieces, axis=0).astype(BF16)
    real = jnp.concatenate([real] * (views * frames), axis=0)
    rows = frames * padded
    width = weights[-1].shape[1]
    keys = jnp.dot(flat, weights[-2][...], preferred_element_type=F32).astype(BF16)
    values = jnp.dot(flat, weights[-1][...], preferred_element_type=F32)
    values = jnp.where(real, values, 0.0).astype(BF16)
    for view in range(views):
        part = slice(view * rows, (view + 1) * rows)
        for quad in range(width // QUAD):
            columns = slice(quad * QUAD, (quad + 1) * QUAD)
            outs[-1][2 * quad, view] = keys[part, columns]
            outs[-1][2 * quad + 1, view] = values[part, columns]
    if with_query:
        query = jnp.dot(flat, weights[0][...], preferred_element_type=F32)
        for view in range(views):
            for frame in range(frames):
                at = (view * frames + frame) * padded
                outs[0][view, frame] = query[at : at + padded].astype(BF16)


def project(place, tokens, begins, views, gain, weights, joints):
    _, frames, padded, half = tokens[0].shape
    model, width = weights[0].shape
    rows = frames * padded
    with_query = len(weights) == 3
    step = 2 if views % 2 == 0 else 1
    planes = 2 * width // QUAD
    out_shape = [pltpu.HBM((planes, views, rows, QUAD), BF16)]
    out_specs = [pl.BlockSpec((planes, step, rows, QUAD), lambda i, s: (0, i, 0, 0))]
    if with_query:
        out_shape = [pltpu.HBM((views, frames, padded, width), BF16)] + out_shape
        out_specs = [
            pl.BlockSpec((step, frames, padded, width), lambda i, s: (i, 0, 0, 0))
        ] + out_specs

    def token(begin):
        return pl.BlockSpec(
            (step, frames, padded, half), lambda i, s: (begin // step + i, 0, 0, 0)
        )

    weight = pl.BlockSpec((model, width), lambda i, s: (0, 0))
    return pl.pallas_call(
        functools.partial(project_kernel, with_query, joints),
        grid_spec=pltpu.PrefetchScalarGridSpec(
            num_scalar_prefetch=1,
            grid=(views // step,),
            in_specs=[token(begin) for begin in begins]
            + [pl.BlockSpec((1, model), lambda i, s: (0, 0))]
            + [weight] * len(weights),
            out_specs=out_specs,
        ),
        out_shape=out_shape,
        compiler_params=params(VMEM_MIB),
        cost_estimate=HINT,
        name="project",
    )(place, *tokens, gain, *weights)


def attend_kernel(frame, first, begin, joints, place_ref, slot_ref, q_ref, *rest):
    sources, out_ref = rest[:-1], rest[-1]
    views, padded, width = out_ref.shape
    blocks = slot_ref.shape[1]
    rows = sources[0].shape[2]
    queried = place_ref[frame]
    heads = QUAD // HD
    lane = lax.broadcasted_iota(jnp.int32, (1, QUAD), 1)
    column = lax.broadcasted_iota(jnp.int32, (1, blocks * rows), 1)
    real = lax.rem(column, padded) < joints
    scale = HD**-0.5 * LOG2E

    def key_set(plane, slots):
        return jnp.concatenate([sources[0][plane, slot] for slot in slots], axis=0)

    for view in range(views):
        slots = [slot_ref[first + view, block] for block in range(blocks)]
        for quad in range(width // QUAD):
            columns = slice(quad * QUAD, (quad + 1) * QUAD)
            query = q_ref[begin + view, queried, :, columns].astype(F32)
            stacked = jnp.concatenate(
                [jnp.where(lane // HD == head, query, 0.0) for head in range(heads)], axis=0
            ).astype(BF16)
            scores = lax.dot_general(
                stacked,
                key_set(2 * quad, slots),
                (((1,), (1,)), ((), ())),
                preferred_element_type=F32,
            )
            top = jnp.max(scores, axis=1, keepdims=True)
            powers = jnp.exp2((scores - top) * scale)
            weight = jnp.sum(jnp.where(real, powers, 0.0), axis=1, keepdims=True)
            found = jnp.dot(
                powers.astype(BF16), key_set(2 * quad + 1, slots), preferred_element_type=F32
            )
            found = found / weight
            total = found[:padded]
            for head in range(1, heads):
                part = found[head * padded : (head + 1) * padded]
                total = jnp.where(lane // HD == head, part, total)
            out_ref[view, :, columns] = total.astype(BF16)


def attend(place, frame, slots, first, query, begin, views, sources, joints):
    _, _, padded, width = query.shape
    scalars = pl.BlockSpec(memory_space=pltpu.SMEM)
    arrays = pl.BlockSpec(memory_space=pltpu.VMEM)
    return pl.pallas_call(
        functools.partial(attend_kernel, frame, first, begin, joints),
        in_specs=[scalars, scalars] + [arrays] * (1 + len(sources)),
        out_specs=arrays,
        out_shape=jax.ShapeDtypeStruct((views, padded, width), BF16),
        compiler_params=params(WINDOW_MIB),
        cost_estimate=HINT,
        name="attend",
    )(place, slots, query, *sources)


def graph_kernel(packed, place_ref, *refs):
    mine_ref, theirs_ref, own_ref, other_ref, w_mine_ref, w_got_ref, w_shared_ref = refs[:7]
    gain_ref, skeleton_ref, degree_ref, w_graph_ref, *outs = refs[7:]
    views, padded, width = mine_ref.shape
    joint, core = place_ref[0], place_ref[1]
    model = w_graph_ref.shape[0]
    gain = gain_ref[...]

    def rows_of(ref):
        pieces = [ref[view].astype(F32) for view in range(views)]
        return jnp.concatenate(pieces, axis=0).astype(BF16)

    mine, theirs = rows_of(mine_ref), rows_of(theirs_ref)
    w_low = jnp.where(core == 0, w_got_ref[...], w_shared_ref[...])
    w_high = jnp.where(core == 0, w_shared_ref[...], w_got_ref[...])
    projected = (
        jnp.dot(mine, w_mine_ref[...], preferred_element_type=F32)
        + jnp.dot(theirs[:, : width // 2], w_low, preferred_element_type=F32)
        + jnp.dot(theirs[:, width // 2 :], w_high, preferred_element_type=F32)
    )
    hiddens, mixed = [], []
    for view in range(views):
        own, other = own_ref[view, 0].astype(F32), other_ref[view, 0].astype(F32)
        part = projected[view * padded : (view + 1) * padded]
        hidden = (both_halves(joint, own, other) + part).astype(BF16).astype(F32)
        normed = layer_norm(hidden, gain).astype(BF16)
        summed = jnp.dot(skeleton_ref[...], normed, preferred_element_type=F32)
        hiddens.append(hidden)
        mixed.append(summed / degree_ref[...])
    skeletal = jnp.concatenate(mixed, axis=0).astype(BF16)
    graph = jnp.dot(skeletal, w_graph_ref[...], preferred_element_type=F32)
    first = lax.broadcasted_iota(jnp.int32, (1, LANES), 1) < LANES // 2
    for view in range(views):
        term = graph[view * padded : (view + 1) * padded]
        if not packed:
            outs[0][view] = hiddens[view].astype(BF16)
            outs[1][view] = term.astype(BF16)
            continue
        for tile in range(model // LANES):
            columns = slice(tile * LANES, (tile + 1) * LANES)
            kept = hiddens[view][:, columns]
            turned = pltpu.roll(term[:, columns], LANES // 2, axis=1)
            outs[0][2 * tile, view] = jnp.where(first, kept, turned).astype(BF16)
            outs[0][2 * tile + 1, view] = jnp.where(first, turned, kept).astype(BF16)


def graph_part(packed, place, mine, theirs, own, other, begin, held):
    views, padded, width = mine.shape
    half = own.shape[3]
    model = held[-1].shape[0]
    heads = pl.BlockSpec((views, padded, width), lambda i, j: (0, 0, 0))
    token = pl.BlockSpec((views, 1, padded, half), lambda i, j: (begin // views, j[0], 0, 0))
    if packed:
        devices = 2 * model // LANES
        out_shape = [pltpu.HBM((devices, views, padded, LANES), BF16)]
        out_specs = [pl.BlockSpec((devices, views, padded, LANES), lambda i, j: (0, 0, 0, 0))]
    else:
        out_shape = [jax.ShapeDtypeStruct((views, padded, model), BF16)] * 2
        out_specs = [pl.BlockSpec((views, padded, model), lambda i, j: (0, 0, 0))] * 2
    return pl.pallas_call(
        functools.partial(graph_kernel, packed),
        grid_spec=pltpu.PrefetchScalarGridSpec(
            num_scalar_prefetch=1,
            grid=(1,),
            in_specs=[heads, heads, token, token]
            + [pl.BlockSpec(a.shape, lambda i, j: (0, 0)) for a in held],
            out_specs=out_specs,
        ),
        out_shape=out_shape,
        compiler_params=params(VMEM_MIB),
        cost_estimate=HINT,
        name="graph_part",
    )(place, mine, theirs, own, other, *held)


def mix_kernel(share, count, order_ref, *rest):
    parts, (counts_ref, kept_ref, *earlier, out_ref, wide) = rest[:count], rest[count:]
    rows, channels, _ = out_ref.shape
    views = 0
    for part in parts:
        block = part[...].astype(F32).reshape(part.shape[0] * rows, LANES)
        wide[views * rows : views * rows + block.shape[0]] = block
        views += part.shape[0]
    counts, keeper = counts_ref[...], kept_ref[...]
    flipped = order_ref[0] == 1
    for row in range(rows):
        lanes_first = wide[pl.ds(row, views, stride=rows), :].T
        low, high = lanes_first[:channels], lanes_first[channels:]
        term = jnp.where(flipped, low, high).astype(BF16)
        kept = jnp.where(flipped, high, low).astype(BF16)
        total = jnp.dot(kept, keeper, preferred_element_type=F32)
        total = total + jnp.dot(term, counts, preferred_element_type=F32) * share
        if earlier:
            total = total + earlier[0][row]
        out_ref[row] = total.astype(out_ref.dtype)


def mix(order, parts, counts, keeper, earlier, last, joints, share):
    parts = [part.reshape(-1, *part.shape[2:]) for part in parts]
    views, num_views = counts.shape
    padded = parts[0].shape[1]
    channels = LANES // 2
    rows = 16
    block = pl.BlockSpec((rows, channels, num_views), lambda i, s: (i, 0, 0))
    held = pl.BlockSpec(counts.shape, lambda i, s: (0, 0))
    return pl.pallas_call(
        functools.partial(mix_kernel, share, len(parts)),
        grid_spec=pltpu.PrefetchScalarGridSpec(
            num_scalar_prefetch=1,
            grid=(pl.cdiv(joints, rows),),
            in_specs=[
                pl.BlockSpec((part.shape[0], rows, LANES), lambda i, s: (0, i, 0))
                for part in parts
            ]
            + [held, held]
            + [block] * len(earlier),
            out_specs=block,
            scratch_shapes=[pltpu.VMEM((views * rows, LANES), F32)],
        ),
        out_shape=jax.ShapeDtypeStruct((joints, channels, num_views), BF16 if last else F32),
        compiler_params=params(FULL_MIB if last else VMEM_MIB),
        cost_estimate=HINT,
        name="mix",
    )(order, *parts, counts, keeper, *earlier)


def body(
    pose_tokens,
    gain_attn,
    gain_graph,
    w_query,
    w_key,
    w_value,
    w_out,
    w_graph,
    partners,
    parents,
    view_links,
):
    views_dev, frames, joints, half_width = pose_tokens.shape
    model = w_graph.shape[0]
    devices = lax.axis_size("view")
    place = lax.axis_index("view").astype(jnp.int32)
    joint_place = lax.axis_index("joint").astype(jnp.int32)
    num_views = devices * views_dev
    channels = model // devices
    padded = round_up(joints, 8)
    rows = frames * padded
    if views_dev == 8:
        chunks = ((0, 4), (4, 4))
        tail = ((0, 0, 4), (1, 0, 4))
    else:
        chunks = ((0, views_dev),)
        tail = ((0, 0, views_dev),)
    packed = 2 * channels == LANES and num_views == LANES
    swap = [(0, 1), (1, 0)]
    up = [(i, (i + 1) % devices) for i in range(devices)]
    down = [(j, i) for i, j in up]
    swap_even = [(2 * v + j, 2 * v + 1 - j) for v in range(0, devices, 2) for j in (0, 1)]
    to_odd = [(2 * v + j, 2 * v + 2 + j) for v in range(0, devices, 2) for j in (0, 1)]
    gain_attn = gain_attn.reshape(1, model)
    gain_graph = gain_graph.reshape(1, model)
    where = jnp.stack((joint_place, lax.rem(place, 2), 1 - joint_place))

    to_other_core = [(v, v ^ 1) for v in range(devices)]

    def tied(array, *others):
        return lax.optimization_barrier((array, *others))[0]

    own = []
    for begin, count in chunks:
        part = lax.slice_in_dim(pose_tokens, begin, begin + count)
        part = jnp.pad(part, ((0, 0), (0, 0), (0, padded - joints), (0, 0)))
        own.append(with_layout_constraint(part, Layout(major_to_minor=(0, 1, 2, 3))))

    near = [lax.ppermute(part, "view", up) for part in own]
    other, query, here, after = [], [], [], []
    for c in range(len(chunks)):
        other.append(lax.ppermute(own[c], "joint", swap))
        part = tied(other[c], *near, *after)
        q, kv = project(
            where, (own[c], part), (0, 0), chunks[c][1], gain_attn, (w_query, w_key, w_value), joints
        )
        query.append(q)
        here.append(kv)
        after.append(lax.ppermute(kv, "view", down))
    before = []
    for c, (begin, count) in enumerate(chunks):
        far = lax.ppermute(
            tied(near[c], other[-1], here[0]), ("view", "joint"), swap_even
        )
        far_odd = lax.ppermute(tied(other[c], here[0]), ("view", "joint"), to_odd)
        (kv,) = project(
            where,
            (near[c], far, far_odd),
            (0, 0, 0),
            count,
            gain_attn,
            (w_key, w_value),
            joints,
        )
        before.append(kv)
    window = [jnp.concatenate(here + after + before, axis=1)]

    w_rows = w_out.shape[0] // 2
    w_part = lax.dynamic_slice_in_dim(w_out, lax.rem(place, 2) * w_rows, w_rows, 0)
    w_part = tied(w_part, far)
    w_got = lax.ppermute(w_part, "joint", swap)
    w_shared = lax.ppermute(w_got, "view", to_other_core)

    first_view = place * views_dev
    ahead = jnp.mod(partners - first_view, num_views)
    ahead = jnp.where(ahead >= num_views - views_dev, ahead - num_views + 3 * views_dev, ahead)
    own_slot = jnp.arange(views_dev, dtype=jnp.int32)[:, None]
    slots = jnp.concatenate((own_slot, ahead), axis=1)
    slots = jnp.clip(slots, 0, 3 * views_dev - 1)

    joint_ids = jnp.arange(padded, dtype=jnp.int32)
    line = jnp.concatenate((parents, jnp.full((padded - joints,), -1, jnp.int32)))
    skeleton = (
        (joint_ids[:, None] == joint_ids[None, :]).astype(F32)
        + (joint_ids[None, :] == line[:, None]).astype(F32)
        + (joint_ids[:, None] == line[None, :]).astype(F32)
    )
    degree = jnp.sum(skeleton, axis=1, keepdims=True)
    skeleton = skeleton.astype(BF16)
    view_ids = jnp.arange(num_views, dtype=jnp.int32)
    counts = (view_ids[:, None] == view_ids[None, :]).astype(F32)
    counts = counts + jnp.sum(
        (view_links[:, :, None] == view_ids[None, None, :]).astype(F32), axis=1
    )
    share = 1.0 / (view_links.shape[1] + 1)
    at = [(chunks[c][0] + begin, count) for c, begin, count in tail]
    groups = (range(len(tail) - 1), range(len(tail) - 1, len(tail)))

    def rows_of(matrix, group):
        matrix = matrix.reshape(devices, views_dev, num_views)
        pieces = [
            matrix[:, at[k][0] : at[k][0] + at[k][1]].reshape(-1, num_views) for k in group
        ]
        return jnp.concatenate(pieces, axis=0).astype(BF16)

    groups = [group for group in groups if len(group)]
    mixers = [(rows_of(counts.T, group), rows_of(jnp.eye(num_views), group)) for group in groups]
    slots = tied(slots, skeleton, degree, *(m for pair in mixers for m in pair))

    held = (w_out, w_got, w_shared, gain_graph, skeleton, degree, w_graph)
    sent = []
    for c, begin, count in tail:
        first = chunks[c][0] + begin
        q = query[c]
        if sent:
            q = tied(q, sent[-1][0])
        theirs = attend(where, 2, slots, first, q, begin, count, window, joints)
        q = tied(q, theirs)
        moved = lax.ppermute(theirs, "joint", swap)
        mine = attend(where, 0, slots, first, q, begin, count, window, joints)
        sent.append(graph_part(packed, where, mine, moved, own[c], other[c], begin, held))

    if packed:
        order = lax.rem(place, 2).reshape(1)
        parts = [
            lax.all_to_all(part, "view", split_axis=0, concat_axis=0, tiled=True)
            for (part,) in sent
        ]
        total = ()
        for group, (counted, keeper) in zip(groups, mixers):
            total = (
                mix(
                    order,
                    [parts[k] for k in group],
                    counted,
                    keeper,
                    total,
                    group[-1] == len(tail) - 1,
                    joints,
                    share,
                ),
            )
        return jnp.transpose(total[0], (1, 0, 2))[None]

    hidden = jnp.concatenate([part[0] for part in sent], axis=0)[:, :joints]
    graph_term = jnp.concatenate([part[1] for part in sent], axis=0)[:, :joints]
    residual = jnp.transpose(hidden, (2, 1, 0))
    graph_term = jnp.transpose(graph_term, (2, 1, 0))
    residual = lax.all_to_all(residual, "view", split_axis=0, concat_axis=2, tiled=True)
    graph_term = lax.all_to_all(graph_term, "view", split_axis=0, concat_axis=2, tiled=True)
    mixed = jnp.einsum(
        "cjv,wv->cjw", graph_term, counts.astype(BF16), preferred_element_type=F32
    )
    return (residual.astype(F32) + mixed * share).astype(BF16)[None]


def solution(mesh):
    placed = (
        P("view", None, None, "joint"),
        P(),
        P(),
        P(None, "joint"),
        P(None, "joint"),
        P(None, "joint"),
        P("joint", None),
        P(),
        P("view", None),
        P(),
        P(),
    )
    return jax.shard_map(
        body, mesh=mesh, in_specs=placed, out_specs=P("joint", "view", None, None), check_vma=False
    )
```

```python
import functools

import jax
import jax.numpy as jnp
from jax import lax
from jax.experimental import pallas as pl
from jax.experimental.layout import Layout, with_layout_constraint
from jax.experimental.pallas import tpu as pltpu
from jax.sharding import PartitionSpec as P

HD = 64
LANES = 128
QUAD = 256
norm_eps = 1e-05
MIB = 1024 * 1024
VMEM_MIB = 16
WINDOW_MIB = 24
F32 = jnp.float32
BF16 = jnp.bfloat16
LOG2E = 1.4426950408889634


def round_up(value, unit):
    return (value + unit - 1) // unit * unit


def layer_norm(values, gain):
    average = jnp.mean(values, axis=-1, keepdims=True)
    centred = values - average
    spread = jnp.mean(centred * centred, axis=-1, keepdims=True)
    return centred * lax.rsqrt(spread + norm_eps) * gain


def both_halves(joint, own, other):
    low = jnp.where(joint == 0, own, other)
    high = jnp.where(joint == 0, other, own)
    return jnp.concatenate([low, high], axis=1)


def params(limit_mib):
    return pltpu.CompilerParams(vmem_limit_bytes=limit_mib * MIB)


HINT = pl.CostEstimate(flops=1_000_000, bytes_accessed=10_000, transcendentals=0)


def project_kernel(with_query, joints, place_ref, *refs):
    count = 3 if with_query else 2
    halves = 2 if with_query else 3
    tokens, rest = refs[:halves], refs[halves:]
    gain_ref, weights, outs = rest[0], rest[1 : 1 + count], rest[1 + count :]
    views, frames, padded, _ = tokens[0].shape
    joint = place_ref[0]
    gain = gain_ref[...]
    row = lax.broadcasted_iota(jnp.int32, (padded, 1), 0)
    real = row < joints
    pieces = []
    for view in range(views):
        for frame in range(frames):
            own = tokens[0][view, frame].astype(F32)
            other = tokens[1][view, frame].astype(F32)
            if not with_query:
                other = jnp.where(place_ref[1] == 0, other, tokens[2][view, frame].astype(F32))
            normed = layer_norm(both_halves(joint, own, other), gain)
            pieces.append(jnp.where(real, normed, normed[0:1]))
    flat = jnp.concatenate(pieces, axis=0).astype(BF16)
    real = jnp.concatenate([real] * (views * frames), axis=0)
    rows = frames * padded
    width = weights[-1].shape[1]
    keys = jnp.dot(flat, weights[-2][...], preferred_element_type=F32).astype(BF16)
    values = jnp.dot(flat, weights[-1][...], preferred_element_type=F32)
    values = jnp.where(real, values, 0.0).astype(BF16)
    for view in range(views):
        part = slice(view * rows, (view + 1) * rows)
        for quad in range(width // QUAD):
            columns = slice(quad * QUAD, (quad + 1) * QUAD)
            outs[-1][2 * quad, view] = keys[part, columns]
            outs[-1][2 * quad + 1, view] = values[part, columns]
    if with_query:
        query = jnp.dot(flat, weights[0][...], preferred_element_type=F32)
        for view in range(views):
            for frame in range(frames):
                at = (view * frames + frame) * padded
                outs[0][view, frame] = query[at : at + padded].astype(BF16)


def project(place, tokens, begins, views, gain, weights, joints):
    _, frames, padded, half = tokens[0].shape
    model, width = weights[0].shape
    rows = frames * padded
    with_query = len(weights) == 3
    step = 2 if views % 2 == 0 else 1
    planes = 2 * width // QUAD
    out_shape = [pltpu.HBM((planes, views, rows, QUAD), BF16)]
    out_specs = [pl.BlockSpec((planes, step, rows, QUAD), lambda i, s: (0, i, 0, 0))]
    if with_query:
        out_shape = [pltpu.HBM((views, frames, padded, width), BF16)] + out_shape
        out_specs = [
            pl.BlockSpec((step, frames, padded, width), lambda i, s: (i, 0, 0, 0))
        ] + out_specs

    def token(begin):
        return pl.BlockSpec(
            (step, frames, padded, half), lambda i, s: (begin // step + i, 0, 0, 0)
        )

    weight = pl.BlockSpec((model, width), lambda i, s: (0, 0))
    return pl.pallas_call(
        functools.partial(project_kernel, with_query, joints),
        grid_spec=pltpu.PrefetchScalarGridSpec(
            num_scalar_prefetch=1,
            grid=(views // step,),
            in_specs=[token(begin) for begin in begins]
            + [pl.BlockSpec((1, model), lambda i, s: (0, 0))]
            + [weight] * len(weights),
            out_specs=out_specs,
        ),
        out_shape=out_shape,
        compiler_params=params(VMEM_MIB),
        cost_estimate=HINT,
        name="project",
    )(place, *tokens, gain, *weights)


def attend_kernel(frame, first, begin, joints, place_ref, slot_ref, q_ref, *rest):
    sources, out_ref = rest[:-1], rest[-1]
    views, padded, width = out_ref.shape
    blocks = slot_ref.shape[1]
    rows = sources[0].shape[2]
    queried = place_ref[frame]
    heads = QUAD // HD
    lane = lax.broadcasted_iota(jnp.int32, (1, QUAD), 1)
    column = lax.broadcasted_iota(jnp.int32, (1, blocks * rows), 1)
    real = lax.rem(column, padded) < joints
    scale = HD**-0.5 * LOG2E

    def key_set(plane, slots):
        return jnp.concatenate([sources[0][plane, slot] for slot in slots], axis=0)

    for view in range(views):
        slots = [slot_ref[first + view, block] for block in range(blocks)]
        for quad in range(width // QUAD):
            columns = slice(quad * QUAD, (quad + 1) * QUAD)
            query = q_ref[begin + view, queried, :, columns].astype(F32)
            stacked = jnp.concatenate(
                [jnp.where(lane // HD == head, query, 0.0) for head in range(heads)], axis=0
            ).astype(BF16)
            scores = lax.dot_general(
                stacked,
                key_set(2 * quad, slots),
                (((1,), (1,)), ((), ())),
                preferred_element_type=F32,
            )
            top = jnp.max(scores, axis=1, keepdims=True)
            powers = jnp.exp2((scores - top) * scale)
            weight = jnp.sum(jnp.where(real, powers, 0.0), axis=1, keepdims=True)
            found = jnp.dot(
                powers.astype(BF16), key_set(2 * quad + 1, slots), preferred_element_type=F32
            )
            found = found / weight
            total = found[:padded]
            for head in range(1, heads):
                part = found[head * padded : (head + 1) * padded]
                total = jnp.where(lane // HD == head, part, total)
            out_ref[view, :, columns] = total.astype(BF16)


def attend(place, frame, slots, first, query, begin, views, sources, joints):
    _, _, padded, width = query.shape
    scalars = pl.BlockSpec(memory_space=pltpu.SMEM)
    arrays = pl.BlockSpec(memory_space=pltpu.VMEM)
    return pl.pallas_call(
        functools.partial(attend_kernel, frame, first, begin, joints),
        in_specs=[scalars, scalars] + [arrays] * (1 + len(sources)),
        out_specs=arrays,
        out_shape=jax.ShapeDtypeStruct((views, padded, width), BF16),
        compiler_params=params(WINDOW_MIB),
        cost_estimate=HINT,
        name="attend",
    )(place, slots, query, *sources)


def graph_kernel(packed, place_ref, *refs):
    mine_ref, theirs_ref, own_ref, other_ref, w_mine_ref, w_got_ref, w_shared_ref = refs[:7]
    gain_ref, skeleton_ref, w_graph_ref, *outs = refs[7:]
    views, padded, width = mine_ref.shape
    joint, core = place_ref[0], place_ref[1]
    model = w_graph_ref.shape[0]
    gain = gain_ref[...]

    def rows_of(ref):
        pieces = [ref[view].astype(F32) for view in range(views)]
        return jnp.concatenate(pieces, axis=0).astype(BF16)

    mine, theirs = rows_of(mine_ref), rows_of(theirs_ref)
    w_low = jnp.where(core == 0, w_got_ref[...], w_shared_ref[...])
    w_high = jnp.where(core == 0, w_shared_ref[...], w_got_ref[...])
    projected = (
        jnp.dot(mine, w_mine_ref[...], preferred_element_type=F32)
        + jnp.dot(theirs[:, : width // 2], w_low, preferred_element_type=F32)
        + jnp.dot(theirs[:, width // 2 :], w_high, preferred_element_type=F32)
    )
    degree = jnp.sum(skeleton_ref[...].astype(F32), axis=1, keepdims=True)
    hiddens, mixed = [], []
    for view in range(views):
        own, other = own_ref[view, 0].astype(F32), other_ref[view, 0].astype(F32)
        part = projected[view * padded : (view + 1) * padded]
        hidden = (both_halves(joint, own, other) + part).astype(BF16).astype(F32)
        normed = layer_norm(hidden, gain).astype(BF16)
        summed = jnp.dot(skeleton_ref[...], normed, preferred_element_type=F32)
        hiddens.append(hidden)
        mixed.append(summed / degree)
    skeletal = jnp.concatenate(mixed, axis=0).astype(BF16)
    graph = jnp.dot(skeletal, w_graph_ref[...], preferred_element_type=F32)
    first = lax.broadcasted_iota(jnp.int32, (1, LANES), 1) < LANES // 2
    for view in range(views):
        term = graph[view * padded : (view + 1) * padded]
        if not packed:
            outs[0][view] = hiddens[view].astype(BF16)
            outs[1][view] = term.astype(BF16)
            continue
        for tile in range(model // LANES):
            columns = slice(tile * LANES, (tile + 1) * LANES)
            kept = hiddens[view][:, columns]
            turned = pltpu.roll(term[:, columns], LANES // 2, axis=1)
            outs[0][2 * tile, view] = jnp.where(first, kept, turned).astype(BF16)
            outs[0][2 * tile + 1, view] = jnp.where(first, turned, kept).astype(BF16)


def graph_part(packed, place, mine, theirs, own, other, begin, held):
    views, padded, width = mine.shape
    half = own.shape[3]
    model = held[-1].shape[0]
    heads = pl.BlockSpec((views, padded, width), lambda i, j: (0, 0, 0))
    token = pl.BlockSpec((views, 1, padded, half), lambda i, j: (begin // views, j[0], 0, 0))
    if packed:
        devices = 2 * model // LANES
        out_shape = [pltpu.HBM((devices, views, padded, LANES), BF16)]
        out_specs = [pl.BlockSpec((devices, views, padded, LANES), lambda i, j: (0, 0, 0, 0))]
    else:
        out_shape = [jax.ShapeDtypeStruct((views, padded, model), BF16)] * 2
        out_specs = [pl.BlockSpec((views, padded, model), lambda i, j: (0, 0, 0))] * 2
    return pl.pallas_call(
        functools.partial(graph_kernel, packed),
        grid_spec=pltpu.PrefetchScalarGridSpec(
            num_scalar_prefetch=1,
            grid=(1,),
            in_specs=[heads, heads, token, token]
            + [pl.BlockSpec(a.shape, lambda i, j: (0, 0)) for a in held],
            out_specs=out_specs,
        ),
        out_shape=out_shape,
        compiler_params=params(VMEM_MIB),
        cost_estimate=HINT,
        name="graph_part",
    )(place, mine, theirs, own, other, *held)


def mix_kernel(share, count, order_ref, *rest):
    parts, (counts_ref, kept_ref, *earlier, out_ref, wide) = rest[:count], rest[count:]
    rows, channels, _ = out_ref.shape
    views = 0
    for part in parts:
        block = part[...].astype(F32).reshape(part.shape[0] * rows, LANES)
        wide[views * rows : views * rows + block.shape[0]] = block
        views += part.shape[0]
    counts, keeper = counts_ref[...], kept_ref[...]
    flipped = order_ref[0] == 1
    for row in range(rows):
        lanes_first = wide[pl.ds(row, views, stride=rows), :].T
        low, high = lanes_first[:channels], lanes_first[channels:]
        term = jnp.where(flipped, low, high).astype(BF16)
        kept = jnp.where(flipped, high, low).astype(BF16)
        total = jnp.dot(kept, keeper, preferred_element_type=F32)
        total = total + jnp.dot(term, counts, preferred_element_type=F32) * share
        if earlier:
            total = total + earlier[0][row]
        out_ref[row] = total.astype(out_ref.dtype)


def mix(order, parts, counts, keeper, earlier, last, joints, share):
    parts = [part.reshape(-1, *part.shape[2:]) for part in parts]
    views, num_views = counts.shape
    padded = parts[0].shape[1]
    channels = LANES // 2
    rows = 16
    block = pl.BlockSpec((rows, channels, num_views), lambda i, s: (i, 0, 0))
    held = pl.BlockSpec(counts.shape, lambda i, s: (0, 0))
    return pl.pallas_call(
        functools.partial(mix_kernel, share, len(parts)),
        grid_spec=pltpu.PrefetchScalarGridSpec(
            num_scalar_prefetch=1,
            grid=(pl.cdiv(joints, rows),),
            in_specs=[
                pl.BlockSpec((part.shape[0], rows, LANES), lambda i, s: (0, i, 0))
                for part in parts
            ]
            + [held, held]
            + [block] * len(earlier),
            out_specs=block,
            scratch_shapes=[pltpu.VMEM((views * rows, LANES), F32)],
        ),
        out_shape=jax.ShapeDtypeStruct((joints, channels, num_views), BF16 if last else F32),
        compiler_params=params(VMEM_MIB),
        cost_estimate=HINT,
        name="mix",
    )(order, *parts, counts, keeper, *earlier)


def body(
    pose_tokens,
    gain_attn,
    gain_graph,
    w_query,
    w_key,
    w_value,
    w_out,
    w_graph,
    partners,
    parents,
    view_links,
):
    views_dev, frames, joints, half_width = pose_tokens.shape
    model = w_graph.shape[0]
    devices = lax.axis_size("view")
    place = lax.axis_index("view").astype(jnp.int32)
    joint_place = lax.axis_index("joint").astype(jnp.int32)
    num_views = devices * views_dev
    channels = model // devices
    padded = round_up(joints, 8)
    rows = frames * padded
    if views_dev == 8:
        chunks = ((0, 4), (4, 4))
        tail = ((0, 0, 4), (1, 0, 4))
    else:
        chunks = ((0, views_dev),)
        tail = ((0, 0, views_dev),)
    packed = 2 * channels == LANES and num_views == LANES
    swap = [(0, 1), (1, 0)]
    up = [(i, (i + 1) % devices) for i in range(devices)]
    down = [(j, i) for i, j in up]
    swap_even = [(2 * v + j, 2 * v + 1 - j) for v in range(0, devices, 2) for j in (0, 1)]
    to_odd = [(2 * v + j, 2 * v + 2 + j) for v in range(0, devices, 2) for j in (0, 1)]
    gain_attn = gain_attn.reshape(1, model)
    gain_graph = gain_graph.reshape(1, model)
    where = jnp.stack((joint_place, lax.rem(place, 2), 1 - joint_place))

    to_other_core = [(v, v ^ 1) for v in range(devices)]

    def tied(array, *others):
        return lax.optimization_barrier((array, *others))[0]

    own = []
    for begin, count in chunks:
        part = lax.slice_in_dim(pose_tokens, begin, begin + count)
        part = jnp.pad(part, ((0, 0), (0, 0), (0, padded - joints), (0, 0)))
        own.append(with_layout_constraint(part, Layout(major_to_minor=(0, 1, 2, 3))))

    near = [lax.ppermute(part, "view", up) for part in own]
    other, query, here, after = [], [], [], []
    for c in range(len(chunks)):
        other.append(lax.ppermute(own[c], "joint", swap))
        part = tied(other[c], *near)
        q, kv = project(
            where, (own[c], part), (0, 0), chunks[c][1], gain_attn, (w_query, w_key, w_value), joints
        )
        query.append(q)
        here.append(kv)
        after.append(lax.ppermute(kv, "view", down))
    before = []
    for c, (begin, count) in enumerate(chunks):
        far = lax.ppermute(
            tied(near[c], other[-1], here[0], *after[:c]), ("view", "joint"), swap_even
        )
        far_odd = lax.ppermute(tied(other[c], here[0]), ("view", "joint"), to_odd)
        (kv,) = project(
            where,
            (near[c], far, far_odd),
            (0, 0, 0),
            count,
            gain_attn,
            (w_key, w_value),
            joints,
        )
        before.append(kv)
    window = [jnp.concatenate(here + after + before, axis=1)]

    w_rows = w_out.shape[0] // 2
    w_part = lax.dynamic_slice_in_dim(w_out, lax.rem(place, 2) * w_rows, w_rows, 0)
    w_part = tied(w_part, far)
    w_got = lax.ppermute(w_part, "joint", swap)
    w_shared = lax.ppermute(w_got, "view", to_other_core)

    first_view = place * views_dev
    ahead = jnp.mod(partners - first_view, num_views)
    ahead = jnp.where(ahead >= num_views - views_dev, ahead - num_views + 3 * views_dev, ahead)
    own_slot = jnp.arange(views_dev, dtype=jnp.int32)[:, None]
    slots = jnp.concatenate((own_slot, ahead), axis=1)
    slots = jnp.clip(slots, 0, 3 * views_dev - 1)

    joint_ids = jnp.arange(padded, dtype=jnp.int32)
    line = jnp.concatenate((parents, jnp.full((padded - joints,), -1, jnp.int32)))
    skeleton = (
        (joint_ids[:, None] == joint_ids[None, :]).astype(F32)
        + (joint_ids[None, :] == line[:, None]).astype(F32)
        + (joint_ids[:, None] == line[None, :]).astype(F32)
    )
    skeleton = skeleton.astype(BF16)
    view_ids = jnp.arange(num_views, dtype=jnp.int32)
    counts = (view_ids[:, None] == view_ids[None, :]).astype(F32)
    counts = counts + jnp.sum(
        (view_links[:, :, None] == view_ids[None, None, :]).astype(F32), axis=1
    )
    share = 1.0 / (view_links.shape[1] + 1)
    at = [(chunks[c][0] + begin, count) for c, begin, count in tail]
    groups = (range(len(tail) - 1), range(len(tail) - 1, len(tail)))

    def rows_of(matrix, group):
        matrix = matrix.reshape(devices, views_dev, num_views)
        pieces = [
            matrix[:, at[k][0] : at[k][0] + at[k][1]].reshape(-1, num_views) for k in group
        ]
        return jnp.concatenate(pieces, axis=0).astype(BF16)

    groups = [group for group in groups if len(group)]
    mixers = [(rows_of(counts.T, group), rows_of(jnp.eye(num_views), group)) for group in groups]
    slots = tied(slots, skeleton, *(m for pair in mixers for m in pair))

    held = (w_out, w_got, w_shared, gain_graph, skeleton, w_graph)
    sent = []
    for c, begin, count in tail:
        first = chunks[c][0] + begin
        q = query[c]
        if sent:
            q = tied(q, sent[-1][0])
        theirs = attend(where, 2, slots, first, q, begin, count, window, joints)
        q = tied(q, theirs)
        moved = lax.ppermute(theirs, "joint", swap)
        mine = attend(where, 0, slots, first, q, begin, count, window, joints)
        sent.append(graph_part(packed, where, mine, moved, own[c], other[c], begin, held))

    if packed:
        order = lax.rem(place, 2).reshape(1)
        parts = [
            lax.all_to_all(part, "view", split_axis=0, concat_axis=0, tiled=True)
            for (part,) in sent
        ]
        total = ()
        for group, (counted, keeper) in zip(groups, mixers):
            total = (
                mix(
                    order,
                    [parts[k] for k in group],
                    counted,
                    keeper,
                    total,
                    group[-1] == len(tail) - 1,
                    joints,
                    share,
                ),
            )
        return jnp.transpose(total[0], (1, 0, 2))[None]

    hidden = jnp.concatenate([part[0] for part in sent], axis=0)[:, :joints]
    graph_term = jnp.concatenate([part[1] for part in sent], axis=0)[:, :joints]
    residual = jnp.transpose(hidden, (2, 1, 0))
    graph_term = jnp.transpose(graph_term, (2, 1, 0))
    residual = lax.all_to_all(residual, "view", split_axis=0, concat_axis=2, tiled=True)
    graph_term = lax.all_to_all(graph_term, "view", split_axis=0, concat_axis=2, tiled=True)
    mixed = jnp.einsum(
        "cjv,wv->cjw", graph_term, counts.astype(BF16), preferred_element_type=F32
    )
    return (residual.astype(F32) + mixed * share).astype(BF16)[None]


def solution(mesh):
    placed = (
        P("view", None, None, "joint"),
        P(),
        P(),
        P(None, "joint"),
        P(None, "joint"),
        P(None, "joint"),
        P("joint", None),
        P(),
        P("view", None),
        P(),
        P(),
    )
    return jax.shard_map(
        body, mesh=mesh, in_specs=placed, out_specs=P("joint", "view", None, None), check_vma=False
    )
```

```python
import functools

import jax
import jax.numpy as jnp
from jax import lax
from jax.experimental import pallas as pl
from jax.experimental.layout import Layout, with_layout_constraint
from jax.experimental.pallas import tpu as pltpu
from jax.sharding import PartitionSpec as P

HD = 64
LANES = 128
QUAD = 256
norm_eps = 1e-05
MIB = 1024 * 1024
VMEM_MIB = 16
WINDOW_MIB = 24
F32 = jnp.float32
BF16 = jnp.bfloat16
LOG2E = 1.4426950408889634


def round_up(value, unit):
    return (value + unit - 1) // unit * unit


def layer_norm(values, gain):
    average = jnp.mean(values, axis=-1, keepdims=True)
    centred = values - average
    spread = jnp.mean(centred * centred, axis=-1, keepdims=True)
    return centred * lax.rsqrt(spread + norm_eps) * gain


def both_halves(joint, own, other):
    low = jnp.where(joint == 0, own, other)
    high = jnp.where(joint == 0, other, own)
    return jnp.concatenate([low, high], axis=1)


def params(limit_mib):
    return pltpu.CompilerParams(vmem_limit_bytes=limit_mib * MIB)


HINT = pl.CostEstimate(flops=1_000_000, bytes_accessed=10_000, transcendentals=0)


def project_kernel(with_query, joints, place_ref, *refs):
    count = 3 if with_query else 2
    halves = 2 if with_query else 3
    tokens, rest = refs[:halves], refs[halves:]
    gain_ref, weights, outs = rest[0], rest[1 : 1 + count], rest[1 + count :]
    views, frames, padded, _ = tokens[0].shape
    joint = place_ref[0]
    gain = gain_ref[...]
    row = lax.broadcasted_iota(jnp.int32, (padded, 1), 0)
    real = row < joints
    pieces = []
    for view in range(views):
        for frame in range(frames):
            own = tokens[0][view, frame].astype(F32)
            other = tokens[1][view, frame].astype(F32)
            if not with_query:
                other = jnp.where(place_ref[1] == 0, other, tokens[2][view, frame].astype(F32))
            normed = layer_norm(both_halves(joint, own, other), gain)
            pieces.append(jnp.where(real, normed, normed[0:1]))
    flat = jnp.concatenate(pieces, axis=0).astype(BF16)
    real = jnp.concatenate([real] * (views * frames), axis=0)
    rows = frames * padded
    width = weights[-1].shape[1]
    keys = jnp.dot(flat, weights[-2][...], preferred_element_type=F32).astype(BF16)
    values = jnp.dot(flat, weights[-1][...], preferred_element_type=F32)
    values = jnp.where(real, values, 0.0).astype(BF16)
    for view in range(views):
        part = slice(view * rows, (view + 1) * rows)
        for quad in range(width // QUAD):
            columns = slice(quad * QUAD, (quad + 1) * QUAD)
            outs[-1][2 * quad, view] = keys[part, columns]
            outs[-1][2 * quad + 1, view] = values[part, columns]
    if with_query:
        query = jnp.dot(flat, weights[0][...], preferred_element_type=F32)
        for view in range(views):
            for frame in range(frames):
                at = (view * frames + frame) * padded
                outs[0][view, frame] = query[at : at + padded].astype(BF16)


def project(place, tokens, begins, views, gain, weights, joints):
    _, frames, padded, half = tokens[0].shape
    model, width = weights[0].shape
    rows = frames * padded
    with_query = len(weights) == 3
    step = 2 if views % 2 == 0 else 1
    planes = 2 * width // QUAD
    out_shape = [pltpu.HBM((planes, views, rows, QUAD), BF16)]
    out_specs = [pl.BlockSpec((planes, step, rows, QUAD), lambda i, s: (0, i, 0, 0))]
    if with_query:
        out_shape = [pltpu.HBM((views, frames, padded, width), BF16)] + out_shape
        out_specs = [
            pl.BlockSpec((step, frames, padded, width), lambda i, s: (i, 0, 0, 0))
        ] + out_specs

    def token(begin):
        return pl.BlockSpec(
            (step, frames, padded, half), lambda i, s: (begin // step + i, 0, 0, 0)
        )

    weight = pl.BlockSpec((model, width), lambda i, s: (0, 0))
    return pl.pallas_call(
        functools.partial(project_kernel, with_query, joints),
        grid_spec=pltpu.PrefetchScalarGridSpec(
            num_scalar_prefetch=1,
            grid=(views // step,),
            in_specs=[token(begin) for begin in begins]
            + [pl.BlockSpec((1, model), lambda i, s: (0, 0))]
            + [weight] * len(weights),
            out_specs=out_specs,
        ),
        out_shape=out_shape,
        compiler_params=params(VMEM_MIB),
        cost_estimate=HINT,
        name="project",
    )(place, *tokens, gain, *weights)


def attend_kernel(frame, first, begin, joints, place_ref, slot_ref, q_ref, *rest):
    sources, out_ref = rest[:-1], rest[-1]
    views, padded, width = out_ref.shape
    blocks = slot_ref.shape[1]
    rows = sources[0].shape[2]
    queried = place_ref[frame]
    heads = QUAD // HD
    lane = lax.broadcasted_iota(jnp.int32, (1, QUAD), 1)
    column = lax.broadcasted_iota(jnp.int32, (1, blocks * rows), 1)
    real = lax.rem(column, padded) < joints
    scale = HD**-0.5 * LOG2E

    def key_set(plane, slots):
        return jnp.concatenate([sources[0][plane, slot] for slot in slots], axis=0)

    for view in range(views):
        slots = [slot_ref[first + view, block] for block in range(blocks)]
        for quad in range(width // QUAD):
            columns = slice(quad * QUAD, (quad + 1) * QUAD)
            query = q_ref[begin + view, queried, :, columns].astype(F32)
            stacked = jnp.concatenate(
                [jnp.where(lane // HD == head, query, 0.0) for head in range(heads)], axis=0
            ).astype(BF16)
            scores = lax.dot_general(
                stacked,
                key_set(2 * quad, slots),
                (((1,), (1,)), ((), ())),
                preferred_element_type=F32,
            )
            top = jnp.max(scores, axis=1, keepdims=True)
            powers = jnp.exp2((scores - top) * scale)
            weight = jnp.sum(jnp.where(real, powers, 0.0), axis=1, keepdims=True)
            found = jnp.dot(
                powers.astype(BF16), key_set(2 * quad + 1, slots), preferred_element_type=F32
            )
            found = found / weight
            total = found[:padded]
            for head in range(1, heads):
                part = found[head * padded : (head + 1) * padded]
                total = jnp.where(lane // HD == head, part, total)
            out_ref[view, :, columns] = total.astype(BF16)


def attend(place, frame, slots, first, query, begin, views, sources, joints):
    _, _, padded, width = query.shape
    scalars = pl.BlockSpec(memory_space=pltpu.SMEM)
    arrays = pl.BlockSpec(memory_space=pltpu.VMEM)
    return pl.pallas_call(
        functools.partial(attend_kernel, frame, first, begin, joints),
        in_specs=[scalars, scalars] + [arrays] * (1 + len(sources)),
        out_specs=arrays,
        out_shape=jax.ShapeDtypeStruct((views, padded, width), BF16),
        compiler_params=params(WINDOW_MIB),
        cost_estimate=HINT,
        name="attend",
    )(place, slots, query, *sources)


def graph_kernel(packed, place_ref, *refs):
    mine_ref, theirs_ref, own_ref, other_ref, w_mine_ref, w_got_ref, w_shared_ref = refs[:7]
    gain_ref, skeleton_ref, w_graph_ref, *outs = refs[7:]
    views, padded, width = mine_ref.shape
    joint, core = place_ref[0], place_ref[1]
    model = w_graph_ref.shape[0]
    gain = gain_ref[...]

    def rows_of(ref):
        pieces = [ref[view].astype(F32) for view in range(views)]
        return jnp.concatenate(pieces, axis=0).astype(BF16)

    mine, theirs = rows_of(mine_ref), rows_of(theirs_ref)
    w_low = jnp.where(core == 0, w_got_ref[...], w_shared_ref[...])
    w_high = jnp.where(core == 0, w_shared_ref[...], w_got_ref[...])
    projected = (
        jnp.dot(mine, w_mine_ref[...], preferred_element_type=F32)
        + jnp.dot(theirs[:, : width // 2], w_low, preferred_element_type=F32)
        + jnp.dot(theirs[:, width // 2 :], w_high, preferred_element_type=F32)
    )
    degree = jnp.sum(skeleton_ref[...].astype(F32), axis=1, keepdims=True)
    hiddens, mixed = [], []
    for view in range(views):
        own, other = own_ref[view, 0].astype(F32), other_ref[view, 0].astype(F32)
        part = projected[view * padded : (view + 1) * padded]
        hidden = (both_halves(joint, own, other) + part).astype(BF16).astype(F32)
        normed = layer_norm(hidden, gain).astype(BF16)
        summed = jnp.dot(skeleton_ref[...], normed, preferred_element_type=F32)
        hiddens.append(hidden)
        mixed.append(summed / degree)
    skeletal = jnp.concatenate(mixed, axis=0).astype(BF16)
    graph = jnp.dot(skeletal, w_graph_ref[...], preferred_element_type=F32)
    first = lax.broadcasted_iota(jnp.int32, (1, LANES), 1) < LANES // 2
    for view in range(views):
        term = graph[view * padded : (view + 1) * padded]
        if not packed:
            outs[0][view] = hiddens[view].astype(BF16)
            outs[1][view] = term.astype(BF16)
            continue
        for tile in range(model // LANES):
            columns = slice(tile * LANES, (tile + 1) * LANES)
            kept = hiddens[view][:, columns]
            turned = pltpu.roll(term[:, columns], LANES // 2, axis=1)
            outs[0][2 * tile, view] = jnp.where(first, kept, turned).astype(BF16)
            outs[0][2 * tile + 1, view] = jnp.where(first, turned, kept).astype(BF16)


def graph_part(packed, place, mine, theirs, own, other, begin, held):
    views, padded, width = mine.shape
    half = own.shape[3]
    model = held[-1].shape[0]
    heads = pl.BlockSpec((views, padded, width), lambda i, j: (0, 0, 0))
    token = pl.BlockSpec((views, 1, padded, half), lambda i, j: (begin // views, j[0], 0, 0))
    if packed:
        devices = 2 * model // LANES
        out_shape = [pltpu.HBM((devices, views, padded, LANES), BF16)]
        out_specs = [pl.BlockSpec((devices, views, padded, LANES), lambda i, j: (0, 0, 0, 0))]
    else:
        out_shape = [jax.ShapeDtypeStruct((views, padded, model), BF16)] * 2
        out_specs = [pl.BlockSpec((views, padded, model), lambda i, j: (0, 0, 0))] * 2
    return pl.pallas_call(
        functools.partial(graph_kernel, packed),
        grid_spec=pltpu.PrefetchScalarGridSpec(
            num_scalar_prefetch=1,
            grid=(1,),
            in_specs=[heads, heads, token, token]
            + [pl.BlockSpec(a.shape, lambda i, j: (0, 0)) for a in held],
            out_specs=out_specs,
        ),
        out_shape=out_shape,
        compiler_params=params(VMEM_MIB),
        cost_estimate=HINT,
        name="graph_part",
    )(place, mine, theirs, own, other, *held)


def mix_kernel(share, count, order_ref, *rest):
    parts, (counts_ref, kept_ref, *earlier, out_ref, wide) = rest[:count], rest[count:]
    rows, channels, _ = out_ref.shape
    views = 0
    for part in parts:
        block = part[...].astype(F32).reshape(part.shape[0] * rows, LANES)
        wide[views * rows : views * rows + block.shape[0]] = block
        views += part.shape[0]
    counts, keeper = counts_ref[...], kept_ref[...]
    flipped = order_ref[0] == 1
    for row in range(rows):
        lanes_first = wide[pl.ds(row, views, stride=rows), :].T
        low, high = lanes_first[:channels], lanes_first[channels:]
        term = jnp.where(flipped, low, high).astype(BF16)
        kept = jnp.where(flipped, high, low).astype(BF16)
        total = jnp.dot(kept, keeper, preferred_element_type=F32)
        total = total + jnp.dot(term, counts, preferred_element_type=F32) * share
        if earlier:
            total = total + earlier[0][row]
        out_ref[row] = total.astype(out_ref.dtype)


def mix(order, parts, counts, keeper, earlier, last, joints, share):
    parts = [part.reshape(-1, *part.shape[2:]) for part in parts]
    views, num_views = counts.shape
    padded = parts[0].shape[1]
    channels = LANES // 2
    rows = 16
    block = pl.BlockSpec((rows, channels, num_views), lambda i, s: (i, 0, 0))
    held = pl.BlockSpec(counts.shape, lambda i, s: (0, 0))
    return pl.pallas_call(
        functools.partial(mix_kernel, share, len(parts)),
        grid_spec=pltpu.PrefetchScalarGridSpec(
            num_scalar_prefetch=1,
            grid=(pl.cdiv(joints, rows),),
            in_specs=[
                pl.BlockSpec((part.shape[0], rows, LANES), lambda i, s: (0, i, 0))
                for part in parts
            ]
            + [held, held]
            + [block] * len(earlier),
            out_specs=block,
            scratch_shapes=[pltpu.VMEM((views * rows, LANES), F32)],
        ),
        out_shape=jax.ShapeDtypeStruct((joints, channels, num_views), BF16 if last else F32),
        compiler_params=params(VMEM_MIB),
        cost_estimate=HINT,
        name="mix",
    )(order, *parts, counts, keeper, *earlier)


def body(
    pose_tokens,
    gain_attn,
    gain_graph,
    w_query,
    w_key,
    w_value,
    w_out,
    w_graph,
    partners,
    parents,
    view_links,
):
    views_dev, frames, joints, half_width = pose_tokens.shape
    model = w_graph.shape[0]
    devices = lax.axis_size("view")
    place = lax.axis_index("view").astype(jnp.int32)
    joint_place = lax.axis_index("joint").astype(jnp.int32)
    num_views = devices * views_dev
    channels = model // devices
    padded = round_up(joints, 8)
    rows = frames * padded
    if views_dev == 8:
        chunks = ((0, 4), (4, 4))
        tail = ((0, 0, 4), (1, 0, 4))
    else:
        chunks = ((0, views_dev),)
        tail = ((0, 0, views_dev),)
    packed = 2 * channels == LANES and num_views == LANES
    swap = [(0, 1), (1, 0)]
    up = [(i, (i + 1) % devices) for i in range(devices)]
    down = [(j, i) for i, j in up]
    swap_even = [(2 * v + j, 2 * v + 1 - j) for v in range(0, devices, 2) for j in (0, 1)]
    to_odd = [(2 * v + j, 2 * v + 2 + j) for v in range(0, devices, 2) for j in (0, 1)]
    gain_attn = gain_attn.reshape(1, model)
    gain_graph = gain_graph.reshape(1, model)
    where = jnp.stack((joint_place, lax.rem(place, 2), 1 - joint_place))

    to_other_core = [(v, v ^ 1) for v in range(devices)]

    def tied(array, *others):
        return lax.optimization_barrier((array, *others))[0]

    own = []
    for begin, count in chunks:
        part = lax.slice_in_dim(pose_tokens, begin, begin + count)
        part = jnp.pad(part, ((0, 0), (0, 0), (0, padded - joints), (0, 0)))
        own.append(with_layout_constraint(part, Layout(major_to_minor=(0, 1, 2, 3))))

    near = [lax.ppermute(part, "view", up) for part in own]
    other, query, here, after = [], [], [], []
    for c in range(len(chunks)):
        other.append(lax.ppermute(own[c], "joint", swap))
        part = tied(other[c], *near)
        q, kv = project(
            where, (own[c], part), (0, 0), chunks[c][1], gain_attn, (w_query, w_key, w_value), joints
        )
        query.append(q)
        here.append(kv)
        after.append(lax.ppermute(kv, "view", down))
    before = []
    for c, (begin, count) in enumerate(chunks):
        waits = (here[0], other[-1], *after[:c]) if c else here[:1]
        far = lax.ppermute(tied(near[c], *waits), ("view", "joint"), swap_even)
        far_odd = lax.ppermute(tied(other[c], here[0]), ("view", "joint"), to_odd)
        (kv,) = project(
            where,
            (near[c], far, far_odd),
            (0, 0, 0),
            count,
            gain_attn,
            (w_key, w_value),
            joints,
        )
        before.append(kv)
    window = [jnp.concatenate(here + after + before, axis=1)]

    w_rows = w_out.shape[0] // 2
    w_part = lax.dynamic_slice_in_dim(w_out, lax.rem(place, 2) * w_rows, w_rows, 0)
    w_part = tied(w_part, far)
    w_got = lax.ppermute(w_part, "joint", swap)
    w_shared = lax.ppermute(w_got, "view", to_other_core)

    first_view = place * views_dev
    ahead = jnp.mod(partners - first_view, num_views)
    ahead = jnp.where(ahead >= num_views - views_dev, ahead - num_views + 3 * views_dev, ahead)
    own_slot = jnp.arange(views_dev, dtype=jnp.int32)[:, None]
    slots = jnp.concatenate((own_slot, ahead), axis=1)
    slots = jnp.clip(slots, 0, 3 * views_dev - 1)

    joint_ids = jnp.arange(padded, dtype=jnp.int32)
    line = jnp.concatenate((parents, jnp.full((padded - joints,), -1, jnp.int32)))
    skeleton = (
        (joint_ids[:, None] == joint_ids[None, :]).astype(F32)
        + (joint_ids[None, :] == line[:, None]).astype(F32)
        + (joint_ids[:, None] == line[None, :]).astype(F32)
    )
    skeleton = skeleton.astype(BF16)
    view_ids = jnp.arange(num_views, dtype=jnp.int32)
    counts = (view_ids[:, None] == view_ids[None, :]).astype(F32)
    counts = counts + jnp.sum(
        (view_links[:, :, None] == view_ids[None, None, :]).astype(F32), axis=1
    )
    share = 1.0 / (view_links.shape[1] + 1)
    at = [(chunks[c][0] + begin, count) for c, begin, count in tail]
    groups = (range(len(tail) - 1), range(len(tail) - 1, len(tail)))

    def rows_of(matrix, group):
        matrix = matrix.reshape(devices, views_dev, num_views)
        pieces = [
            matrix[:, at[k][0] : at[k][0] + at[k][1]].reshape(-1, num_views) for k in group
        ]
        return jnp.concatenate(pieces, axis=0).astype(BF16)

    groups = [group for group in groups if len(group)]
    mixers = [(rows_of(counts.T, group), rows_of(jnp.eye(num_views), group)) for group in groups]
    slots = tied(slots, skeleton, *(m for pair in mixers for m in pair))

    held = (w_out, w_got, w_shared, gain_graph, skeleton, w_graph)
    sent = []
    for c, begin, count in tail:
        first = chunks[c][0] + begin
        q = query[c]
        if sent:
            q = tied(q, sent[-1][0])
        theirs = attend(where, 2, slots, first, q, begin, count, window, joints)
        q = tied(q, theirs)
        moved = lax.ppermute(theirs, "joint", swap)
        mine = attend(where, 0, slots, first, q, begin, count, window, joints)
        sent.append(graph_part(packed, where, mine, moved, own[c], other[c], begin, held))

    if packed:
        order = lax.rem(place, 2).reshape(1)
        parts = [
            lax.all_to_all(part, "view", split_axis=0, concat_axis=0, tiled=True)
            for (part,) in sent
        ]
        total = ()
        for group, (counted, keeper) in zip(groups, mixers):
            total = (
                mix(
                    order,
                    [parts[k] for k in group],
                    counted,
                    keeper,
                    total,
                    group[-1] == len(tail) - 1,
                    joints,
                    share,
                ),
            )
        return jnp.transpose(total[0], (1, 0, 2))[None]

    hidden = jnp.concatenate([part[0] for part in sent], axis=0)[:, :joints]
    graph_term = jnp.concatenate([part[1] for part in sent], axis=0)[:, :joints]
    residual = jnp.transpose(hidden, (2, 1, 0))
    graph_term = jnp.transpose(graph_term, (2, 1, 0))
    residual = lax.all_to_all(residual, "view", split_axis=0, concat_axis=2, tiled=True)
    graph_term = lax.all_to_all(graph_term, "view", split_axis=0, concat_axis=2, tiled=True)
    mixed = jnp.einsum(
        "cjv,wv->cjw", graph_term, counts.astype(BF16), preferred_element_type=F32
    )
    return (residual.astype(F32) + mixed * share).astype(BF16)[None]


def solution(mesh):
    placed = (
        P("view", None, None, "joint"),
        P(),
        P(),
        P(None, "joint"),
        P(None, "joint"),
        P(None, "joint"),
        P("joint", None),
        P(),
        P("view", None),
        P(),
        P(),
    )
    return jax.shard_map(
        body, mesh=mesh, in_specs=placed, out_specs=P("joint", "view", None, None), check_vma=False
    )
```

```python
import functools

import jax
import jax.numpy as jnp
from jax import lax
from jax.experimental import pallas as pl
from jax.experimental.layout import Layout, with_layout_constraint
from jax.experimental.pallas import tpu as pltpu
from jax.sharding import PartitionSpec as P

HD = 64
LANES = 128
QUAD = 256
norm_eps = 1e-05
MIB = 1024 * 1024
VMEM_MIB = 16
WINDOW_MIB = 24
F32 = jnp.float32
BF16 = jnp.bfloat16
LOG2E = 1.4426950408889634


def round_up(value, unit):
    return (value + unit - 1) // unit * unit


def layer_norm(values, gain):
    average = jnp.mean(values, axis=-1, keepdims=True)
    centred = values - average
    spread = jnp.mean(centred * centred, axis=-1, keepdims=True)
    return centred * lax.rsqrt(spread + norm_eps) * gain


def both_halves(joint, own, other):
    low = jnp.where(joint == 0, own, other)
    high = jnp.where(joint == 0, other, own)
    return jnp.concatenate([low, high], axis=1)


def params(limit_mib):
    return pltpu.CompilerParams(vmem_limit_bytes=limit_mib * MIB)


HINT = pl.CostEstimate(flops=1_000_000, bytes_accessed=10_000, transcendentals=0)


def project_kernel(with_query, joints, place_ref, *refs):
    count = 3 if with_query else 2
    halves = 2 if with_query else 3
    tokens, rest = refs[:halves], refs[halves:]
    gain_ref, weights, outs = rest[0], rest[1 : 1 + count], rest[1 + count :]
    views, frames, padded, _ = tokens[0].shape
    joint = place_ref[0]
    gain = gain_ref[...]
    row = lax.broadcasted_iota(jnp.int32, (padded, 1), 0)
    real = row < joints
    pieces = []
    for view in range(views):
        for frame in range(frames):
            own = tokens[0][view, frame].astype(F32)
            other = tokens[1][view, frame].astype(F32)
            if not with_query:
                other = jnp.where(place_ref[1] == 0, other, tokens[2][view, frame].astype(F32))
            normed = layer_norm(both_halves(joint, own, other), gain)
            pieces.append(jnp.where(real, normed, normed[0:1]))
    flat = jnp.concatenate(pieces, axis=0).astype(BF16)
    real = jnp.concatenate([real] * (views * frames), axis=0)
    rows = frames * padded
    width = weights[-1].shape[1]
    keys = jnp.dot(flat, weights[-2][...], preferred_element_type=F32).astype(BF16)
    values = jnp.dot(flat, weights[-1][...], preferred_element_type=F32)
    values = jnp.where(real, values, 0.0).astype(BF16)
    for view in range(views):
        part = slice(view * rows, (view + 1) * rows)
        for quad in range(width // QUAD):
            columns = slice(quad * QUAD, (quad + 1) * QUAD)
            outs[-1][2 * quad, view] = keys[part, columns]
            outs[-1][2 * quad + 1, view] = values[part, columns]
    if with_query:
        query = jnp.dot(flat, weights[0][...], preferred_element_type=F32)
        for view in range(views):
            for frame in range(frames):
                at = (view * frames + frame) * padded
                outs[0][view, frame] = query[at : at + padded].astype(BF16)


def project(place, tokens, begins, views, gain, weights, joints):
    _, frames, padded, half = tokens[0].shape
    model, width = weights[0].shape
    rows = frames * padded
    with_query = len(weights) == 3
    step = 2 if views % 2 == 0 else 1
    planes = 2 * width // QUAD
    out_shape = [pltpu.HBM((planes, views, rows, QUAD), BF16)]
    out_specs = [pl.BlockSpec((planes, step, rows, QUAD), lambda i, s: (0, i, 0, 0))]
    if with_query:
        out_shape = [pltpu.HBM((views, frames, padded, width), BF16)] + out_shape
        out_specs = [
            pl.BlockSpec((step, frames, padded, width), lambda i, s: (i, 0, 0, 0))
        ] + out_specs

    def token(begin):
        return pl.BlockSpec(
            (step, frames, padded, half), lambda i, s: (begin // step + i, 0, 0, 0)
        )

    weight = pl.BlockSpec((model, width), lambda i, s: (0, 0))
    return pl.pallas_call(
        functools.partial(project_kernel, with_query, joints),
        grid_spec=pltpu.PrefetchScalarGridSpec(
            num_scalar_prefetch=1,
            grid=(views // step,),
            in_specs=[token(begin) for begin in begins]
            + [pl.BlockSpec((1, model), lambda i, s: (0, 0))]
            + [weight] * len(weights),
            out_specs=out_specs,
        ),
        out_shape=out_shape,
        compiler_params=params(VMEM_MIB),
        cost_estimate=HINT,
        name="project",
    )(place, *tokens, gain, *weights)


def attend_kernel(frame, first, begin, joints, place_ref, slot_ref, q_ref, *rest):
    sources, out_ref = rest[:-1], rest[-1]
    views, padded, width = out_ref.shape
    blocks = slot_ref.shape[1]
    rows = sources[0].shape[2]
    queried = place_ref[frame]
    heads = QUAD // HD
    lane = lax.broadcasted_iota(jnp.int32, (1, QUAD), 1)
    column = lax.broadcasted_iota(jnp.int32, (1, blocks * rows), 1)
    real = lax.rem(column, padded) < joints
    scale = HD**-0.5 * LOG2E

    def key_set(plane, slots):
        return jnp.concatenate([sources[0][plane, slot] for slot in slots], axis=0)

    for view in range(views):
        slots = [slot_ref[first + view, block] for block in range(blocks)]
        for quad in range(width // QUAD):
            columns = slice(quad * QUAD, (quad + 1) * QUAD)
            query = q_ref[begin + view, queried, :, columns].astype(F32)
            stacked = jnp.concatenate(
                [jnp.where(lane // HD == head, query, 0.0) for head in range(heads)], axis=0
            ).astype(BF16)
            scores = lax.dot_general(
                stacked,
                key_set(2 * quad, slots),
                (((1,), (1,)), ((), ())),
                preferred_element_type=F32,
            )
            top = jnp.max(scores, axis=1, keepdims=True)
            powers = jnp.exp2((scores - top) * scale)
            weight = jnp.sum(jnp.where(real, powers, 0.0), axis=1, keepdims=True)
            found = jnp.dot(
                powers.astype(BF16), key_set(2 * quad + 1, slots), preferred_element_type=F32
            )
            found = found / weight
            total = found[:padded]
            for head in range(1, heads):
                part = found[head * padded : (head + 1) * padded]
                total = jnp.where(lane // HD == head, part, total)
            out_ref[view, :, columns] = total.astype(BF16)


def attend(place, frame, slots, first, query, begin, views, sources, joints):
    _, _, padded, width = query.shape
    scalars = pl.BlockSpec(memory_space=pltpu.SMEM)
    arrays = pl.BlockSpec(memory_space=pltpu.VMEM)
    return pl.pallas_call(
        functools.partial(attend_kernel, frame, first, begin, joints),
        in_specs=[scalars, scalars] + [arrays] * (1 + len(sources)),
        out_specs=arrays,
        out_shape=jax.ShapeDtypeStruct((views, padded, width), BF16),
        compiler_params=params(WINDOW_MIB),
        cost_estimate=HINT,
        name="attend",
    )(place, slots, query, *sources)


def graph_kernel(packed, place_ref, *refs):
    mine_ref, theirs_ref, own_ref, other_ref, w_mine_ref, w_got_ref, w_shared_ref = refs[:7]
    gain_ref, skeleton_ref, w_graph_ref, *outs = refs[7:]
    views, padded, width = mine_ref.shape
    joint, core = place_ref[0], place_ref[1]
    model = w_graph_ref.shape[0]
    gain = gain_ref[...]

    def rows_of(ref):
        pieces = [ref[view].astype(F32) for view in range(views)]
        return jnp.concatenate(pieces, axis=0).astype(BF16)

    mine, theirs = rows_of(mine_ref), rows_of(theirs_ref)
    w_low = jnp.where(core == 0, w_got_ref[...], w_shared_ref[...])
    w_high = jnp.where(core == 0, w_shared_ref[...], w_got_ref[...])
    projected = (
        jnp.dot(mine, w_mine_ref[...], preferred_element_type=F32)
        + jnp.dot(theirs[:, : width // 2], w_low, preferred_element_type=F32)
        + jnp.dot(theirs[:, width // 2 :], w_high, preferred_element_type=F32)
    )
    degree = jnp.sum(skeleton_ref[...].astype(F32), axis=1, keepdims=True)
    hiddens, mixed = [], []
    for view in range(views):
        own, other = own_ref[view, 0].astype(F32), other_ref[view, 0].astype(F32)
        part = projected[view * padded : (view + 1) * padded]
        hidden = (both_halves(joint, own, other) + part).astype(BF16).astype(F32)
        normed = layer_norm(hidden, gain).astype(BF16)
        summed = jnp.dot(skeleton_ref[...], normed, preferred_element_type=F32)
        hiddens.append(hidden)
        mixed.append(summed / degree)
    skeletal = jnp.concatenate(mixed, axis=0).astype(BF16)
    graph = jnp.dot(skeletal, w_graph_ref[...], preferred_element_type=F32)
    first = lax.broadcasted_iota(jnp.int32, (1, LANES), 1) < LANES // 2
    for view in range(views):
        term = graph[view * padded : (view + 1) * padded]
        if not packed:
            outs[0][view] = hiddens[view].astype(BF16)
            outs[1][view] = term.astype(BF16)
            continue
        for tile in range(model // LANES):
            columns = slice(tile * LANES, (tile + 1) * LANES)
            kept = hiddens[view][:, columns]
            turned = pltpu.roll(term[:, columns], LANES // 2, axis=1)
            outs[0][2 * tile, view] = jnp.where(first, kept, turned).astype(BF16)
            outs[0][2 * tile + 1, view] = jnp.where(first, turned, kept).astype(BF16)


def graph_part(packed, place, mine, theirs, own, other, begin, held):
    views, padded, width = mine.shape
    half = own.shape[3]
    model = held[-1].shape[0]
    heads = pl.BlockSpec((views, padded, width), lambda i, j: (0, 0, 0))
    token = pl.BlockSpec((views, 1, padded, half), lambda i, j: (begin // views, j[0], 0, 0))
    if packed:
        devices = 2 * model // LANES
        out_shape = [pltpu.HBM((devices, views, padded, LANES), BF16)]
        out_specs = [pl.BlockSpec((devices, views, padded, LANES), lambda i, j: (0, 0, 0, 0))]
    else:
        out_shape = [jax.ShapeDtypeStruct((views, padded, model), BF16)] * 2
        out_specs = [pl.BlockSpec((views, padded, model), lambda i, j: (0, 0, 0))] * 2
    return pl.pallas_call(
        functools.partial(graph_kernel, packed),
        grid_spec=pltpu.PrefetchScalarGridSpec(
            num_scalar_prefetch=1,
            grid=(1,),
            in_specs=[heads, heads, token, token]
            + [pl.BlockSpec(a.shape, lambda i, j: (0, 0)) for a in held],
            out_specs=out_specs,
        ),
        out_shape=out_shape,
        compiler_params=params(VMEM_MIB),
        cost_estimate=HINT,
        name="graph_part",
    )(place, mine, theirs, own, other, *held)


def mix_kernel(share, count, order_ref, *rest):
    parts, (counts_ref, kept_ref, *earlier, out_ref, wide) = rest[:count], rest[count:]
    rows, channels, _ = out_ref.shape
    views = 0
    for part in parts:
        block = part[...].astype(F32).reshape(part.shape[0] * rows, LANES)
        wide[views * rows : views * rows + block.shape[0]] = block
        views += part.shape[0]
    counts, keeper = counts_ref[...], kept_ref[...]
    flipped = order_ref[0] == 1
    for row in range(rows):
        lanes_first = wide[pl.ds(row, views, stride=rows), :].T
        low, high = lanes_first[:channels], lanes_first[channels:]
        term = jnp.where(flipped, low, high).astype(BF16)
        kept = jnp.where(flipped, high, low).astype(BF16)
        total = jnp.dot(kept, keeper, preferred_element_type=F32)
        total = total + jnp.dot(term, counts, preferred_element_type=F32) * share
        if earlier:
            total = total + earlier[0][row]
        out_ref[row] = total.astype(out_ref.dtype)


def mix(order, parts, counts, keeper, earlier, last, joints, share):
    parts = [part.reshape(-1, *part.shape[2:]) for part in parts]
    views, num_views = counts.shape
    padded = parts[0].shape[1]
    channels = LANES // 2
    rows = 16
    block = pl.BlockSpec((rows, channels, num_views), lambda i, s: (i, 0, 0))
    held = pl.BlockSpec(counts.shape, lambda i, s: (0, 0))
    return pl.pallas_call(
        functools.partial(mix_kernel, share, len(parts)),
        grid_spec=pltpu.PrefetchScalarGridSpec(
            num_scalar_prefetch=1,
            grid=(pl.cdiv(joints, rows),),
            in_specs=[
                pl.BlockSpec((part.shape[0], rows, LANES), lambda i, s: (0, i, 0))
                for part in parts
            ]
            + [held, held]
            + [block] * len(earlier),
            out_specs=block,
            scratch_shapes=[pltpu.VMEM((views * rows, LANES), F32)],
        ),
        out_shape=jax.ShapeDtypeStruct((joints, channels, num_views), BF16 if last else F32),
        compiler_params=params(VMEM_MIB),
        cost_estimate=HINT,
        name="mix",
    )(order, *parts, counts, keeper, *earlier)


def body(
    pose_tokens,
    gain_attn,
    gain_graph,
    w_query,
    w_key,
    w_value,
    w_out,
    w_graph,
    partners,
    parents,
    view_links,
):
    views_dev, frames, joints, half_width = pose_tokens.shape
    model = w_graph.shape[0]
    devices = lax.axis_size("view")
    place = lax.axis_index("view").astype(jnp.int32)
    joint_place = lax.axis_index("joint").astype(jnp.int32)
    num_views = devices * views_dev
    channels = model // devices
    padded = round_up(joints, 8)
    rows = frames * padded
    if views_dev == 8:
        chunks = ((0, 4), (4, 4))
        tail = ((0, 0, 4), (1, 0, 4))
    else:
        chunks = ((0, views_dev),)
        tail = ((0, 0, views_dev),)
    packed = 2 * channels == LANES and num_views == LANES
    swap = [(0, 1), (1, 0)]
    up = [(i, (i + 1) % devices) for i in range(devices)]
    down = [(j, i) for i, j in up]
    swap_even = [(2 * v + j, 2 * v + 1 - j) for v in range(0, devices, 2) for j in (0, 1)]
    to_odd = [(2 * v + j, 2 * v + 2 + j) for v in range(0, devices, 2) for j in (0, 1)]
    gain_attn = gain_attn.reshape(1, model)
    gain_graph = gain_graph.reshape(1, model)
    where = jnp.stack((joint_place, lax.rem(place, 2), 1 - joint_place))

    to_other_core = [(v, v ^ 1) for v in range(devices)]

    def tied(array, *others):
        return lax.optimization_barrier((array, *others))[0]

    own = []
    for begin, count in chunks:
        part = lax.slice_in_dim(pose_tokens, begin, begin + count)
        part = jnp.pad(part, ((0, 0), (0, 0), (0, padded - joints), (0, 0)))
        own.append(with_layout_constraint(part, Layout(major_to_minor=(0, 1, 2, 3))))

    near = [lax.ppermute(part, "view", up) for part in own]
    other, query, here, after, far = [], [], [], [], []
    for c in range(len(chunks)):
        other.append(lax.ppermute(own[c], "joint", swap))
        part = tied(other[c], *near, *far)
        q, kv = project(
            where, (own[c], part), (0, 0), chunks[c][1], gain_attn, (w_query, w_key, w_value), joints
        )
        query.append(q)
        here.append(kv)
        after.append(lax.ppermute(kv, "view", down))
        if c == 0:
            far.append(lax.ppermute(tied(near[0], kv), ("view", "joint"), swap_even))
    before = []
    for c, (begin, count) in enumerate(chunks):
        if c:
            part = tied(near[c], other[-1], *after[:c])
            far.append(lax.ppermute(part, ("view", "joint"), swap_even))
        far_odd = lax.ppermute(tied(other[c], here[0]), ("view", "joint"), to_odd)
        (kv,) = project(
            where,
            (near[c], far[c], far_odd),
            (0, 0, 0),
            count,
            gain_attn,
            (w_key, w_value),
            joints,
        )
        before.append(kv)
    window = [jnp.concatenate(here + before + after, axis=1)]

    w_rows = w_out.shape[0] // 2
    w_part = lax.dynamic_slice_in_dim(w_out, lax.rem(place, 2) * w_rows, w_rows, 0)
    w_part = tied(w_part, far[-1])
    w_got = lax.ppermute(w_part, "joint", swap)
    w_shared = lax.ppermute(w_got, "view", to_other_core)

    first_view = place * views_dev
    ahead = jnp.mod(partners - first_view, num_views)
    ahead = jnp.where(
        ahead >= num_views - views_dev,
        ahead - num_views + 2 * views_dev,
        ahead + jnp.where(ahead >= views_dev, views_dev, 0),
    )
    own_slot = jnp.arange(views_dev, dtype=jnp.int32)[:, None]
    slots = jnp.concatenate((own_slot, ahead), axis=1)
    slots = jnp.clip(slots, 0, 3 * views_dev - 1)

    joint_ids = jnp.arange(padded, dtype=jnp.int32)
    line = jnp.concatenate((parents, jnp.full((padded - joints,), -1, jnp.int32)))
    skeleton = (
        (joint_ids[:, None] == joint_ids[None, :]).astype(F32)
        + (joint_ids[None, :] == line[:, None]).astype(F32)
        + (joint_ids[:, None] == line[None, :]).astype(F32)
    )
    skeleton = skeleton.astype(BF16)
    view_ids = jnp.arange(num_views, dtype=jnp.int32)
    counts = (view_ids[:, None] == view_ids[None, :]).astype(F32)
    counts = counts + jnp.sum(
        (view_links[:, :, None] == view_ids[None, None, :]).astype(F32), axis=1
    )
    share = 1.0 / (view_links.shape[1] + 1)
    at = [(chunks[c][0] + begin, count) for c, begin, count in tail]
    groups = (range(len(tail) - 1), range(len(tail) - 1, len(tail)))

    def rows_of(matrix, group):
        matrix = matrix.reshape(devices, views_dev, num_views)
        pieces = [
            matrix[:, at[k][0] : at[k][0] + at[k][1]].reshape(-1, num_views) for k in group
        ]
        return jnp.concatenate(pieces, axis=0).astype(BF16)

    groups = [group for group in groups if len(group)]
    mixers = [(rows_of(counts.T, group), rows_of(jnp.eye(num_views), group)) for group in groups]
    slots = tied(slots, skeleton, *(m for pair in mixers for m in pair))

    held = (w_out, w_got, w_shared, gain_graph, skeleton, w_graph)
    sent = []
    for c, begin, count in tail:
        first = chunks[c][0] + begin
        q = query[c]
        if sent:
            q = tied(q, sent[-1][0])
        theirs = attend(where, 2, slots, first, q, begin, count, window, joints)
        q = tied(q, theirs)
        moved = lax.ppermute(theirs, "joint", swap)
        mine = attend(where, 0, slots, first, q, begin, count, window, joints)
        sent.append(graph_part(packed, where, mine, moved, own[c], other[c], begin, held))

    if packed:
        order = lax.rem(place, 2).reshape(1)
        parts = [
            lax.all_to_all(part, "view", split_axis=0, concat_axis=0, tiled=True)
            for (part,) in sent
        ]
        total = ()
        for group, (counted, keeper) in zip(groups, mixers):
            total = (
                mix(
                    order,
                    [parts[k] for k in group],
                    counted,
                    keeper,
                    total,
                    group[-1] == len(tail) - 1,
                    joints,
                    share,
                ),
            )
        return jnp.transpose(total[0], (1, 0, 2))[None]

    hidden = jnp.concatenate([part[0] for part in sent], axis=0)[:, :joints]
    graph_term = jnp.concatenate([part[1] for part in sent], axis=0)[:, :joints]
    residual = jnp.transpose(hidden, (2, 1, 0))
    graph_term = jnp.transpose(graph_term, (2, 1, 0))
    residual = lax.all_to_all(residual, "view", split_axis=0, concat_axis=2, tiled=True)
    graph_term = lax.all_to_all(graph_term, "view", split_axis=0, concat_axis=2, tiled=True)
    mixed = jnp.einsum(
        "cjv,wv->cjw", graph_term, counts.astype(BF16), preferred_element_type=F32
    )
    return (residual.astype(F32) + mixed * share).astype(BF16)[None]


def solution(mesh):
    placed = (
        P("view", None, None, "joint"),
        P(),
        P(),
        P(None, "joint"),
        P(None, "joint"),
        P(None, "joint"),
        P("joint", None),
        P(),
        P("view", None),
        P(),
        P(),
    )
    return jax.shard_map(
        body, mesh=mesh, in_specs=placed, out_specs=P("joint", "view", None, None), check_vma=False
    )
```

```python
import functools

import jax
import jax.numpy as jnp
from jax import lax
from jax.experimental import pallas as pl
from jax.experimental.layout import Layout, with_layout_constraint
from jax.experimental.pallas import tpu as pltpu
from jax.sharding import PartitionSpec as P

HD = 64
LANES = 128
QUAD = 256
norm_eps = 1e-05
MIB = 1024 * 1024
VMEM_MIB = 16
WINDOW_MIB = 38
F32 = jnp.float32
BF16 = jnp.bfloat16
LOG2E = 1.4426950408889634


def round_up(value, unit):
    return (value + unit - 1) // unit * unit


def layer_norm(values, gain):
    average = jnp.mean(values, axis=-1, keepdims=True)
    centred = values - average
    spread = jnp.mean(centred * centred, axis=-1, keepdims=True)
    return centred * lax.rsqrt(spread + norm_eps) * gain


def both_halves(joint, own, other):
    low = jnp.where(joint == 0, own, other)
    high = jnp.where(joint == 0, other, own)
    return jnp.concatenate([low, high], axis=1)


def params(limit_mib):
    return pltpu.CompilerParams(vmem_limit_bytes=limit_mib * MIB)


HINT = pl.CostEstimate(flops=1_000_000, bytes_accessed=10_000, transcendentals=0)


def project_kernel(with_query, joints, place_ref, *refs):
    count = 3 if with_query else 2
    halves = 2 if with_query else 3
    tokens, rest = refs[:halves], refs[halves:]
    gain_ref, weights, outs = rest[0], rest[1 : 1 + count], rest[1 + count :]
    views, frames, padded, _ = tokens[0].shape
    joint = place_ref[0]
    gain = gain_ref[...]
    row = lax.broadcasted_iota(jnp.int32, (padded, 1), 0)
    real = row < joints
    pieces = []
    for view in range(views):
        for frame in range(frames):
            own = tokens[0][view, frame].astype(F32)
            other = tokens[1][view, frame].astype(F32)
            if not with_query:
                other = jnp.where(place_ref[1] == 0, other, tokens[2][view, frame].astype(F32))
            normed = layer_norm(both_halves(joint, own, other), gain)
            pieces.append(jnp.where(real, normed, normed[0:1]))
    flat = jnp.concatenate(pieces, axis=0).astype(BF16)
    real = jnp.concatenate([real] * (views * frames), axis=0)
    rows = frames * padded
    width = weights[-1].shape[1]
    keys = jnp.dot(flat, weights[-2][...], preferred_element_type=F32).astype(BF16)
    values = jnp.dot(flat, weights[-1][...], preferred_element_type=F32)
    values = jnp.where(real, values, 0.0).astype(BF16)
    for view in range(views):
        part = slice(view * rows, (view + 1) * rows)
        for quad in range(width // QUAD):
            columns = slice(quad * QUAD, (quad + 1) * QUAD)
            outs[-1][2 * quad, view] = keys[part, columns]
            outs[-1][2 * quad + 1, view] = values[part, columns]
    if with_query:
        query = jnp.dot(flat, weights[0][...], preferred_element_type=F32)
        for view in range(views):
            for frame in range(frames):
                at = (view * frames + frame) * padded
                outs[0][view, frame] = query[at : at + padded].astype(BF16)


def project(place, tokens, begins, views, gain, weights, joints):
    _, frames, padded, half = tokens[0].shape
    model, width = weights[0].shape
    rows = frames * padded
    with_query = len(weights) == 3
    step = 2 if views % 2 == 0 else 1
    planes = 2 * width // QUAD
    out_shape = [pltpu.HBM((planes, views, rows, QUAD), BF16)]
    out_specs = [pl.BlockSpec((planes, step, rows, QUAD), lambda i, s: (0, i, 0, 0))]
    if with_query:
        out_shape = [pltpu.HBM((views, frames, padded, width), BF16)] + out_shape
        out_specs = [
            pl.BlockSpec((step, frames, padded, width), lambda i, s: (i, 0, 0, 0))
        ] + out_specs

    def token(begin):
        return pl.BlockSpec(
            (step, frames, padded, half), lambda i, s: (begin // step + i, 0, 0, 0)
        )

    weight = pl.BlockSpec((model, width), lambda i, s: (0, 0))
    return pl.pallas_call(
        functools.partial(project_kernel, with_query, joints),
        grid_spec=pltpu.PrefetchScalarGridSpec(
            num_scalar_prefetch=1,
            grid=(views // step,),
            in_specs=[token(begin) for begin in begins]
            + [pl.BlockSpec((1, model), lambda i, s: (0, 0))]
            + [weight] * len(weights),
            out_specs=out_specs,
        ),
        out_shape=out_shape,
        compiler_params=params(VMEM_MIB),
        cost_estimate=HINT,
        name="project",
    )(place, *tokens, gain, *weights)


def attend_kernel(frame, first, begin, joints, place_ref, slot_ref, q_ref, *rest):
    sources, out_ref, picked = rest[:-2], rest[-2], rest[-1]
    views, padded, width = out_ref.shape
    blocks = slot_ref.shape[1]
    rows = sources[0].shape[2]
    queried = place_ref[frame]
    heads = QUAD // HD
    lane = lax.broadcasted_iota(jnp.int32, (1, QUAD), 1)
    column = lax.broadcasted_iota(jnp.int32, (1, blocks * rows), 1)
    real = lax.rem(column, padded) < joints
    scale = HD**-0.5 * LOG2E

    for view in range(views):
        for block in range(1, blocks):
            slot = slot_ref[first + view, block]
            begin_at = 0
            for source in sources:
                low, begin_at = begin_at, begin_at + source.shape[1]

                @pl.when((slot >= low) & (slot < begin_at))
                def _():
                    span = slice((block - 1) * rows, block * rows)
                    picked[view, :, span, :] = source[:, slot - low]

    def key_set(plane, view):
        at = first + view
        for source in sources:
            if at < source.shape[1]:
                return jnp.concatenate([source[plane, at], picked[view, plane]], axis=0)
            at -= source.shape[1]

    for view in range(views):
        for quad in range(width // QUAD):
            columns = slice(quad * QUAD, (quad + 1) * QUAD)
            query = q_ref[begin + view, queried, :, columns].astype(F32)
            stacked = jnp.concatenate(
                [jnp.where(lane // HD == head, query, 0.0) for head in range(heads)], axis=0
            ).astype(BF16)
            scores = lax.dot_general(
                stacked,
                key_set(2 * quad, view),
                (((1,), (1,)), ((), ())),
                preferred_element_type=F32,
            )
            top = jnp.max(scores, axis=1, keepdims=True)
            powers = jnp.exp2((scores - top) * scale)
            weight = jnp.sum(jnp.where(real, powers, 0.0), axis=1, keepdims=True)
            found = jnp.dot(
                powers.astype(BF16), key_set(2 * quad + 1, view), preferred_element_type=F32
            )
            found = found / weight
            total = found[:padded]
            for head in range(1, heads):
                part = found[head * padded : (head + 1) * padded]
                total = jnp.where(lane // HD == head, part, total)
            out_ref[view, :, columns] = total.astype(BF16)


def attend(place, frame, slots, first, query, begin, views, sources, joints):
    _, _, padded, width = query.shape
    planes, _, rows, _ = sources[0].shape
    partners = slots.shape[1] - 1
    scalars = pl.BlockSpec(memory_space=pltpu.SMEM)
    arrays = pl.BlockSpec(memory_space=pltpu.VMEM)
    return pl.pallas_call(
        functools.partial(attend_kernel, frame, first, begin, joints),
        in_specs=[scalars, scalars] + [arrays] * (1 + len(sources)),
        out_specs=arrays,
        out_shape=jax.ShapeDtypeStruct((views, padded, width), BF16),
        scratch_shapes=[pltpu.VMEM((views, planes, partners * rows, QUAD), BF16)],
        compiler_params=params(WINDOW_MIB),
        cost_estimate=HINT,
        name="attend",
    )(place, slots, query, *sources)


def graph_kernel(packed, place_ref, *refs):
    mine_ref, theirs_ref, own_ref, other_ref, w_mine_ref, w_got_ref, w_shared_ref = refs[:7]
    gain_ref, skeleton_ref, w_graph_ref, *outs = refs[7:]
    views, padded, width = mine_ref.shape
    joint, core = place_ref[0], place_ref[1]
    model = w_graph_ref.shape[0]
    gain = gain_ref[...]

    def rows_of(ref):
        pieces = [ref[view].astype(F32) for view in range(views)]
        return jnp.concatenate(pieces, axis=0).astype(BF16)

    mine, theirs = rows_of(mine_ref), rows_of(theirs_ref)
    w_low = jnp.where(core == 0, w_got_ref[...], w_shared_ref[...])
    w_high = jnp.where(core == 0, w_shared_ref[...], w_got_ref[...])
    projected = (
        jnp.dot(mine, w_mine_ref[...], preferred_element_type=F32)
        + jnp.dot(theirs[:, : width // 2], w_low, preferred_element_type=F32)
        + jnp.dot(theirs[:, width // 2 :], w_high, preferred_element_type=F32)
    )
    degree = jnp.sum(skeleton_ref[...].astype(F32), axis=1, keepdims=True)
    hiddens, mixed = [], []
    for view in range(views):
        own, other = own_ref[view, 0].astype(F32), other_ref[view, 0].astype(F32)
        part = projected[view * padded : (view + 1) * padded]
        hidden = (both_halves(joint, own, other) + part).astype(BF16).astype(F32)
        normed = layer_norm(hidden, gain).astype(BF16)
        summed = jnp.dot(skeleton_ref[...], normed, preferred_element_type=F32)
        hiddens.append(hidden)
        mixed.append(summed / degree)
    skeletal = jnp.concatenate(mixed, axis=0).astype(BF16)
    graph = jnp.dot(skeletal, w_graph_ref[...], preferred_element_type=F32)
    first = lax.broadcasted_iota(jnp.int32, (1, LANES), 1) < LANES // 2
    for view in range(views):
        term = graph[view * padded : (view + 1) * padded]
        if not packed:
            outs[0][view] = hiddens[view].astype(BF16)
            outs[1][view] = term.astype(BF16)
            continue
        for tile in range(model // LANES):
            columns = slice(tile * LANES, (tile + 1) * LANES)
            kept = hiddens[view][:, columns]
            turned = pltpu.roll(term[:, columns], LANES // 2, axis=1)
            outs[0][2 * tile, view] = jnp.where(first, kept, turned).astype(BF16)
            outs[0][2 * tile + 1, view] = jnp.where(first, turned, kept).astype(BF16)


def graph_part(packed, place, mine, theirs, own, other, begin, held):
    views, padded, width = mine.shape
    half = own.shape[3]
    model = held[-1].shape[0]
    heads = pl.BlockSpec((views, padded, width), lambda i, j: (0, 0, 0))
    token = pl.BlockSpec((views, 1, padded, half), lambda i, j: (begin // views, j[0], 0, 0))
    if packed:
        devices = 2 * model // LANES
        out_shape = [pltpu.HBM((devices, views, padded, LANES), BF16)]
        out_specs = [pl.BlockSpec((devices, views, padded, LANES), lambda i, j: (0, 0, 0, 0))]
    else:
        out_shape = [jax.ShapeDtypeStruct((views, padded, model), BF16)] * 2
        out_specs = [pl.BlockSpec((views, padded, model), lambda i, j: (0, 0, 0))] * 2
    return pl.pallas_call(
        functools.partial(graph_kernel, packed),
        grid_spec=pltpu.PrefetchScalarGridSpec(
            num_scalar_prefetch=1,
            grid=(1,),
            in_specs=[heads, heads, token, token]
            + [pl.BlockSpec(a.shape, lambda i, j: (0, 0)) for a in held],
            out_specs=out_specs,
        ),
        out_shape=out_shape,
        compiler_params=params(VMEM_MIB),
        cost_estimate=HINT,
        name="graph_part",
    )(place, mine, theirs, own, other, *held)


def mix_kernel(share, count, order_ref, *rest):
    parts, (counts_ref, kept_ref, *earlier, out_ref, wide) = rest[:count], rest[count:]
    rows, channels, _ = out_ref.shape
    views = 0
    for part in parts:
        block = part[...].astype(F32).reshape(part.shape[0] * rows, LANES)
        wide[views * rows : views * rows + block.shape[0]] = block
        views += part.shape[0]
    counts, keeper = counts_ref[...], kept_ref[...]
    flipped = order_ref[0] == 1
    for row in range(rows):
        lanes_first = wide[pl.ds(row, views, stride=rows), :].T
        low, high = lanes_first[:channels], lanes_first[channels:]
        term = jnp.where(flipped, low, high).astype(BF16)
        kept = jnp.where(flipped, high, low).astype(BF16)
        total = jnp.dot(kept, keeper, preferred_element_type=F32)
        total = total + jnp.dot(term, counts, preferred_element_type=F32) * share
        if earlier:
            total = total + earlier[0][row]
        out_ref[row] = total.astype(out_ref.dtype)


def mix(order, parts, counts, keeper, earlier, last, joints, share):
    parts = [part.reshape(-1, *part.shape[2:]) for part in parts]
    views, num_views = counts.shape
    padded = parts[0].shape[1]
    channels = LANES // 2
    rows = 16
    block = pl.BlockSpec((rows, channels, num_views), lambda i, s: (i, 0, 0))
    held = pl.BlockSpec(counts.shape, lambda i, s: (0, 0))
    return pl.pallas_call(
        functools.partial(mix_kernel, share, len(parts)),
        grid_spec=pltpu.PrefetchScalarGridSpec(
            num_scalar_prefetch=1,
            grid=(pl.cdiv(joints, rows),),
            in_specs=[
                pl.BlockSpec((part.shape[0], rows, LANES), lambda i, s: (0, i, 0))
                for part in parts
            ]
            + [held, held]
            + [block] * len(earlier),
            out_specs=block,
            scratch_shapes=[pltpu.VMEM((views * rows, LANES), F32)],
        ),
        out_shape=jax.ShapeDtypeStruct((joints, channels, num_views), BF16 if last else F32),
        compiler_params=params(VMEM_MIB),
        cost_estimate=HINT,
        name="mix",
    )(order, *parts, counts, keeper, *earlier)


def body(
    pose_tokens,
    gain_attn,
    gain_graph,
    w_query,
    w_key,
    w_value,
    w_out,
    w_graph,
    partners,
    parents,
    view_links,
):
    views_dev, frames, joints, half_width = pose_tokens.shape
    model = w_graph.shape[0]
    devices = lax.axis_size("view")
    place = lax.axis_index("view").astype(jnp.int32)
    joint_place = lax.axis_index("joint").astype(jnp.int32)
    num_views = devices * views_dev
    channels = model // devices
    padded = round_up(joints, 8)
    rows = frames * padded
    if views_dev == 8:
        chunks = ((0, 4), (4, 4))
        tail = ((0, 0, 4), (1, 0, 4))
    else:
        chunks = ((0, views_dev),)
        tail = ((0, 0, views_dev),)
    packed = 2 * channels == LANES and num_views == LANES
    swap = [(0, 1), (1, 0)]
    up = [(i, (i + 1) % devices) for i in range(devices)]
    down = [(j, i) for i, j in up]
    swap_even = [(2 * v + j, 2 * v + 1 - j) for v in range(0, devices, 2) for j in (0, 1)]
    to_odd = [(2 * v + j, 2 * v + 2 + j) for v in range(0, devices, 2) for j in (0, 1)]
    gain_attn = gain_attn.reshape(1, model)
    gain_graph = gain_graph.reshape(1, model)
    where = jnp.stack((joint_place, lax.rem(place, 2), 1 - joint_place))

    to_other_core = [(v, v ^ 1) for v in range(devices)]

    def tied(array, *others):
        return lax.optimization_barrier((array, *others))[0]

    own = []
    for begin, count in chunks:
        part = lax.slice_in_dim(pose_tokens, begin, begin + count)
        part = jnp.pad(part, ((0, 0), (0, 0), (0, padded - joints), (0, 0)))
        own.append(with_layout_constraint(part, Layout(major_to_minor=(0, 1, 2, 3))))

    near = [lax.ppermute(part, "view", up) for part in own]
    other, query, here, after, far = [], [], [], [], []
    for c in range(len(chunks)):
        other.append(lax.ppermute(own[c], "joint", swap))
        part = tied(other[c], *near)
        q, kv = project(
            where, (own[c], part), (0, 0), chunks[c][1], gain_attn, (w_query, w_key, w_value), joints
        )
        query.append(q)
        here.append(kv)
        after.append(lax.ppermute(kv, "view", down))
    before = []
    for c, (begin, count) in enumerate(chunks):
        part = tied(near[c], other[-1], here[0])
        far.append(lax.ppermute(part, ("view", "joint"), swap_even))
        far_odd = lax.ppermute(tied(other[c], here[0]), ("view", "joint"), to_odd)
        (kv,) = project(
            where,
            (near[c], far[c], far_odd),
            (0, 0, 0),
            count,
            gain_attn,
            (w_key, w_value),
            joints,
        )
        before.append(kv)
    window = here + before + after

    w_rows = w_out.shape[0] // 2
    w_part = lax.dynamic_slice_in_dim(w_out, lax.rem(place, 2) * w_rows, w_rows, 0)
    w_part = tied(w_part, far[-1])
    w_got = lax.ppermute(w_part, "joint", swap)
    w_shared = lax.ppermute(w_got, "view", to_other_core)

    first_view = place * views_dev
    ahead = jnp.mod(partners - first_view, num_views)
    ahead = jnp.where(
        ahead >= num_views - views_dev,
        ahead - num_views + 2 * views_dev,
        ahead + jnp.where(ahead >= views_dev, views_dev, 0),
    )
    own_slot = jnp.arange(views_dev, dtype=jnp.int32)[:, None]
    slots = jnp.concatenate((own_slot, ahead), axis=1)
    slots = jnp.clip(slots, 0, 3 * views_dev - 1)

    joint_ids = jnp.arange(padded, dtype=jnp.int32)
    line = jnp.concatenate((parents, jnp.full((padded - joints,), -1, jnp.int32)))
    skeleton = (
        (joint_ids[:, None] == joint_ids[None, :]).astype(F32)
        + (joint_ids[None, :] == line[:, None]).astype(F32)
        + (joint_ids[:, None] == line[None, :]).astype(F32)
    )
    skeleton = skeleton.astype(BF16)
    view_ids = jnp.arange(num_views, dtype=jnp.int32)
    counts = (view_ids[:, None] == view_ids[None, :]).astype(F32)
    counts = counts + jnp.sum(
        (view_links[:, :, None] == view_ids[None, None, :]).astype(F32), axis=1
    )
    share = 1.0 / (view_links.shape[1] + 1)
    at = [(chunks[c][0] + begin, count) for c, begin, count in tail]
    groups = (range(len(tail) - 1), range(len(tail) - 1, len(tail)))

    def rows_of(matrix, group):
        matrix = matrix.reshape(devices, views_dev, num_views)
        pieces = [
            matrix[:, at[k][0] : at[k][0] + at[k][1]].reshape(-1, num_views) for k in group
        ]
        return jnp.concatenate(pieces, axis=0).astype(BF16)

    groups = [group for group in groups if len(group)]
    mixers = [(rows_of(counts.T, group), rows_of(jnp.eye(num_views), group)) for group in groups]
    slots = tied(slots, skeleton, *(m for pair in mixers for m in pair))

    held = (w_out, w_got, w_shared, gain_graph, skeleton, w_graph)
    sent = []
    for c, begin, count in tail:
        first = chunks[c][0] + begin
        q = query[c]
        if sent:
            q = tied(q, sent[-1][0])
        theirs = attend(where, 2, slots, first, q, begin, count, window, joints)
        q = tied(q, theirs)
        moved = lax.ppermute(theirs, "joint", swap)
        mine = attend(where, 0, slots, first, q, begin, count, window, joints)
        sent.append(graph_part(packed, where, mine, moved, own[c], other[c], begin, held))

    if packed:
        order = lax.rem(place, 2).reshape(1)
        parts = [
            lax.all_to_all(part, "view", split_axis=0, concat_axis=0, tiled=True)
            for (part,) in sent
        ]
        total = ()
        for group, (counted, keeper) in zip(groups, mixers):
            total = (
                mix(
                    order,
                    [parts[k] for k in group],
                    counted,
                    keeper,
                    total,
                    group[-1] == len(tail) - 1,
                    joints,
                    share,
                ),
            )
        return jnp.transpose(total[0], (1, 0, 2))[None]

    hidden = jnp.concatenate([part[0] for part in sent], axis=0)[:, :joints]
    graph_term = jnp.concatenate([part[1] for part in sent], axis=0)[:, :joints]
    residual = jnp.transpose(hidden, (2, 1, 0))
    graph_term = jnp.transpose(graph_term, (2, 1, 0))
    residual = lax.all_to_all(residual, "view", split_axis=0, concat_axis=2, tiled=True)
    graph_term = lax.all_to_all(graph_term, "view", split_axis=0, concat_axis=2, tiled=True)
    mixed = jnp.einsum(
        "cjv,wv->cjw", graph_term, counts.astype(BF16), preferred_element_type=F32
    )
    return (residual.astype(F32) + mixed * share).astype(BF16)[None]


def solution(mesh):
    placed = (
        P("view", None, None, "joint"),
        P(),
        P(),
        P(None, "joint"),
        P(None, "joint"),
        P(None, "joint"),
        P("joint", None),
        P(),
        P("view", None),
        P(),
        P(),
    )
    return jax.shard_map(
        body, mesh=mesh, in_specs=placed, out_specs=P("joint", "view", None, None), check_vma=False
    )
```
